32 devices in a mesh: gx: 4 (over z), gy: 4 (over y, core), gz: 2 (over x).
Axes of the slice: x: 2, y: 2, z: 4, core: 2. Of those that a mesh axis runs over, the one named last changes fastest.
Arguments:
- block: float32 [128, 64, 16, 128], P('gx', 'gy', 'gz'), may hold values from -30 to 30
- conductivity: float32 [128, 64, 16], P('gx', 'gy', 'gz'), may hold values from 0.3 to 3
Outputs:
- basis: float32 [128, 64, 16, 128], P('gx', 'gy', 'gz')
- projected: float32 [128, 128], replicated
The draws below stay inside these ranges and needn't reach their ends.
All inputs are finite; a program needn't handle non-finite values.
Results may differ from the reference program's by a relative error of at most 0.00028.
Values sent between devices are 32-bit elements; how exact they have to be, the bound alone decides.
No kernel may reach another device: no remote copies, remote signals or barrier semaphores. Data moves between devices by JAX's collectives and lax.ppermute only.
A program may use at most 64 MiB of HBM per device.

```python
import math
import jax
import jax.numpy as jnp
from jax import lax

K = 128
DEG = 4
NX = 128
NY = 64
NZ = 16


def draw_block(key, part):
    first = jax.random.fold_in(jax.random.fold_in(key, 17), 0)
    shape = (NX, NY, NZ, K)
    xpos = (jnp.arange(NX, dtype=jnp.float32) + 0.5) / NX
    noise = jnp.clip(jax.random.normal(first, shape, jnp.float32), -5.0, 5.0)
    profile = (1.0 + 2.0 * xpos)[:, None, None, None]
    mixed = noise + 0.5 * jnp.roll(noise, -1, axis=3) + 0.3 * jnp.roll(noise, -3, axis=3)
    return (mixed * profile).astype(jnp.float32)


def block_scale(rng, extent, shards, low, top_value):
    gain = 1.0
    for axis_at, parts in shards:
        draws = jax.random.uniform(jax.random.fold_in(jax.random.fold_in(rng, 6), axis_at), (parts,), jnp.float32, low / len(shards), top_value / len(shards))
        gain = gain * jnp.repeat(jnp.exp(draws), extent[axis_at] // parts).reshape((-1,) + (1,) * (len(extent) - 1 - axis_at))
    return gain


def setup_inputs(seed: int = 0) -> dict:
    arg_keys = jax.random.split(jax.random.key(seed), 3)
    return {
        "block": draw_block(jax.random.fold_in(arg_keys[2], 71), 0),
        "conductivity": jnp.clip(jnp.exp(math.log(3.0) - 2.3025851 * jax.random.uniform(arg_keys[1], (NX, NY, NZ), jnp.float32) ** block_scale(arg_keys[1], (NX, NY, NZ), ((0, 4), (1, 4), (2, 2)), -0.2, 0.2)), 0.3, 3.0),
    }


HIGH = lax.Precision.HIGHEST
center_value = 3.25
half_value = 2.75

def neighbours(padded):
    total = padded[2:, 1:-1, 1:-1] + padded[:-2, 1:-1, 1:-1]
    total = total + padded[1:-1, 2:, 1:-1] + padded[1:-1, :-2, 1:-1]
    total = total + padded[1:-1, 1:-1, 2:] + padded[1:-1, 1:-1, :-2]
    return total

def operator(vectors, sroot):
    scaled = sroot * vectors
    padded = jnp.pad(scaled, ((1, 1), (1, 1), (1, 1), (0, 0)))
    return sroot * (6.0 * scaled - neighbours(padded)) / 6.0

def chebyshev(start, sroot):
    previous = start
    current = (operator(start, sroot) - center_value * start) / half_value
    for step in range(DEG - 1):
        following = 2.0 * (operator(current, sroot) - center_value * current) / half_value - previous
        previous, current = (current, following)
    return current

def reference(block, conductivity):
    sroot = jnp.sqrt(conductivity)[..., None]
    width = min(16, K)
    pieces = []
    for index in range(K // width):
        pieces.append(chebyshev(block[..., index * width:(index + 1) * width], sroot))
    filtered = jnp.concatenate(pieces, axis=3)
    flat = filtered.reshape(-1, K)
    cells = float(NX * NY * NZ)
    gram = jnp.einsum('ck,cl->kl', flat, flat, precision=HIGH) / cells
    columns = []
    for index in range(K // width):
        image = operator(filtered[..., index * width:(index + 1) * width], sroot)
        columns.append(jnp.einsum('ck,cl->kl', flat, image.reshape(-1, width), precision=HIGH))
    raw = jnp.concatenate(columns, axis=1) / cells
    lower = jnp.linalg.cholesky(gram)
    inverse = lax.linalg.triangular_solve(lower, jnp.eye(K, dtype=gram.dtype), left_side=True, lower=True)
    basis = jnp.dot(flat, inverse.T, precision=HIGH).reshape(filtered.shape)
    projected = jnp.dot(jnp.dot(inverse, raw, precision=HIGH), inverse.T, precision=HIGH)
    return (basis, projected)
```

```python
import jax
import jax.numpy as jnp
from jax import lax
from jax.sharding import PartitionSpec as P

DEG = 4


HIGH = lax.Precision.HIGHEST
center_value = 3.25
half_value = 2.75


def extended(block, sides, width):
    for axis, dim in sides:
        count = lax.axis_size(axis)
        forward = [(i, i + 1) for i in range(count - 1)]
        backward = [(target, source) for source, target in forward]
        low = lax.ppermute(
            lax.slice_in_dim(block, block.shape[dim] - width, None, axis=dim), axis, forward
        )
        high = lax.ppermute(lax.slice_in_dim(block, 0, width, axis=dim), axis, backward)
        block = jnp.concatenate([low, block, high], axis=dim)
    return block


def neighbours(padded):
    total = padded[2:, 1:-1, 1:-1] + padded[:-2, 1:-1, 1:-1]
    total = total + padded[1:-1, 2:, 1:-1] + padded[1:-1, :-2, 1:-1]
    total = total + padded[1:-1, 1:-1, 2:] + padded[1:-1, 1:-1, :-2]
    return total


def inner(left, right):
    width = left.shape[-1]
    return jnp.einsum(
        "ck,cl->kl", left.reshape(-1, width), right.reshape(-1, width), precision=HIGH
    )


def operator(vectors, sroot):
    scaled = sroot * vectors
    padded = extended(scaled, (("gx", 0), ("gy", 1), ("gz", 2)), 1)
    return sroot * (6.0 * scaled - neighbours(padded)) / 6.0


def total(value, axes):
    for axis in axes:
        count = lax.axis_size(axis)
        bit = 1
        while bit < count:
            value = value + lax.ppermute(value, axis, [(i, i ^ bit) for i in range(count)])
            bit *= 2
    return value


def lower_inverse(gram):
    lower = jnp.linalg.cholesky(gram)
    return lax.linalg.triangular_solve(
        lower, jnp.eye(gram.shape[0], dtype=gram.dtype), left_side=True, lower=True
    )


def on_device(block, conductivity):
    sroot = jnp.sqrt(conductivity)[..., None]
    cells = float(
        block.shape[0]
        * block.shape[1]
        * block.shape[2]
        * lax.axis_size("gx")
        * lax.axis_size("gy")
        * lax.axis_size("gz")
    )
    previous = block
    current = (operator(block, sroot) - center_value * block) / half_value
    for step in range(DEG - 1):
        following = (
            2.0 * (operator(current, sroot) - center_value * current) / half_value - previous
        )
        previous, current = (current, following)
    width = current.shape[-1]
    flat = current.reshape(-1, width)
    image = operator(current, sroot)
    local = jnp.concatenate([inner(current, current), inner(current, image)], axis=0)
    summed = total(local, ("gy", "gz", "gx")) / cells
    gram, raw = summed[:width], summed[width:]
    inverse = lower_inverse(gram)
    basis = jnp.dot(flat, inverse.T, precision=HIGH).reshape(current.shape)
    projected = jnp.dot(jnp.dot(inverse, raw, precision=HIGH), inverse.T, precision=HIGH)
    return (basis, projected)


def solution(mesh):
    return jax.shard_map(
        on_device,
        mesh=mesh,
        in_specs=(P("gx", "gy", "gz", None), P("gx", "gy", "gz")),
        out_specs=(P("gx", "gy", "gz", None), P()),
        check_vma=False,
    )
```

```python
import functools
import jax
import jax.numpy as jnp
from jax import lax
from jax.experimental import pallas as pl
from jax.experimental.pallas import tpu as pltpu
from jax.sharding import PartitionSpec as P

DEG = 4

HIGH = lax.Precision.HIGHEST
center_value = 3.25
half_value = 2.75
VMEM = pl.BlockSpec(memory_space=pltpu.VMEM)
SMEM = pl.BlockSpec(memory_space=pltpu.SMEM)
BF = jnp.bfloat16


def call(body, outs, ins, flops, aliases=None):
    moved = sum(4 * a.size for a in list(outs) + list(ins))
    return pl.pallas_call(
        body,
        out_shape=outs,
        in_specs=[SMEM] + [VMEM] * (len(ins) - 1),
        out_specs=tuple(VMEM for _ in outs),
        input_output_aliases=aliases or {},
        compiler_params=pltpu.CompilerParams(vmem_limit_bytes=32 * 1024 * 1024),
        cost_estimate=pl.CostEstimate(flops=flops, bytes_accessed=moved, transcendentals=0),
    )(*ins)


def f32(rows, width):
    return jax.ShapeDtypeStruct((rows, width), jnp.float32)


class Shape:
    def __init__(self, shape):
        self.x, self.y, self.z, self.k = shape
        self.row = self.y * self.z
        self.cells = self.x * self.row


def faces_of(s, at, w_ref, out, x):
    for i in range(out["nz"]):
        out["z"][i][pl.ds(x * s.y, s.y), :] = w_ref[
            pl.ds(x * s.row + at[4 + i], s.y, stride=s.z), :
        ]
    for i in range(2):
        out["y"][i][pl.ds(x * s.z, s.z), :] = w_ref[pl.ds(x * s.row + at[2 + i] * s.z, s.z), :]


def x_faces(s, at, w_ref, out):
    for i in range(2):
        out["x"][i][...] = w_ref[pl.ds(at[i] * s.row, s.row), :]


def face_shapes(s, nz):
    return (
        [f32(s.row, s.k)] * 2 + [f32(s.x * s.z, s.k)] * 2 + [f32(s.x * s.y, s.k)] * nz
    )


def split_faces(refs, nz):
    return {"x": refs[0:2], "y": refs[2:4], "z": refs[4 : 4 + nz], "nz": nz}


def prepare(block, wide, at, s, nz):
    def body(at_ref, b_ref, k_ref, w_ref, *faces):
        out = split_faces(faces, nz)

        def step(x, _):
            here = pl.ds(pl.multiple_of(x * s.row, s.row), s.row)
            w_ref[here, :] = jnp.sqrt(k_ref[here, :]) * b_ref[here, :]
            faces_of(s, at_ref, w_ref, out, x)
            return 0

        lax.fori_loop(0, s.x, step, 0)
        x_faces(s, at_ref, w_ref, out)

    outs = [f32(s.cells, s.k)] + face_shapes(s, nz)
    return call(body, outs, [at, block, wide], 4 * s.cells * s.k)


def around(s, w_ref, x, low, high, emit):
    base = pl.multiple_of(x * s.row, s.row)
    place = lax.broadcasted_iota(jnp.int32, (s.z, s.k), 0)
    tiles = [w_ref[pl.ds(base + y * s.z, s.z), :] for y in range(s.y)]
    for y in range(s.y):
        c = tiles[y]
        up = jnp.where(place == s.z - 1, 0.0, pltpu.roll(c, s.z - 1, 0))
        down = jnp.where(place == 0, 0.0, pltpu.roll(c, 1, 0))
        near = up + down
        if y > 0:
            near = near + tiles[y - 1]
        if y < s.y - 1:
            near = near + tiles[y + 1]
        if low:
            near = near + w_ref[pl.ds(base - s.row + y * s.z, s.z), :]
        if high:
            near = near + w_ref[pl.ds(base + s.row + y * s.z, s.z), :]
        emit(pl.ds(base + y * s.z, s.z), c, near)


def sweep(s, w_ref, emit):
    around(s, w_ref, 0, False, True, emit)

    def step(x, _):
        around(s, w_ref, x, True, True, emit)
        return 0

    lax.fori_loop(1, s.x - 1, step, 0)
    around(s, w_ref, s.x - 1, True, False, emit)


def interior(w, before, wide, at, s):
    scale = (1.0 if before is None else 2.0) / half_value

    def body(at_ref, w_ref, k_ref, *rest):
        o_ref = rest[-1]

        def emit(here, c, near):
            new = k_ref[here, :] * ((c - near * (1.0 / 6.0)) * scale) - (scale * center_value) * c
            if before is not None:
                new = new - rest[0][here, :]
            o_ref[here, :] = new

        sweep(s, w_ref, emit)

    ins = [at, w, wide] + ([] if before is None else [before])
    return call(body, [f32(s.cells, s.k)], ins, 12 * s.cells * s.k)[0]


def finish(part, wide, ghosts, at, s, nz, scale):
    def body(at_ref, p_ref, k_ref, *refs):
        ghost = split_faces(refs[: 4 + nz], nz)
        w_ref = refs[4 + nz]
        out = split_faces(refs[5 + nz :], nz)
        factor = scale / 6.0
        for i in range(2):
            here = pl.ds(at_ref[i] * s.row, s.row)
            p_ref[here, :] = p_ref[here, :] - (k_ref[here, :] * factor) * ghost["x"][i][...]
        place = lax.broadcasted_iota(jnp.int32, (s.z, s.k), 0)

        def step(x, _):
            base = pl.multiple_of(x * s.row, s.row)
            for i in range(2):
                here = pl.ds(base + at_ref[2 + i] * s.z, s.z)
                g = ghost["y"][i][pl.ds(x * s.z, s.z), :]
                p_ref[here, :] = p_ref[here, :] - (k_ref[here, :] * factor) * g
            for y in range(s.y):
                here = pl.ds(base + y * s.z, s.z)
                add = 0.0
                for i in range(nz):
                    g = ghost["z"][i][pl.ds(x * s.y + y, 1), :]
                    add = jnp.where(place == at_ref[4 + i], jnp.broadcast_to(g, (s.z, s.k)), add)
                w_ref[here, :] = p_ref[here, :] - (k_ref[here, :] * factor) * add
            faces_of(s, at_ref, w_ref, out, x)
            return 0

        lax.fori_loop(0, s.x, step, 0)
        x_faces(s, at_ref, w_ref, out)

    outs = [f32(s.cells, s.k)] + face_shapes(s, nz)
    return call(body, outs, [at, part, wide] + list(ghosts), 4 * s.cells * s.k, {1: 0})


def exchange(faces, axes):
    got = []
    for face, (axis, first) in zip(faces, axes):
        count = lax.axis_size(axis)
        pairs = []
        for i in range(first, count - 1, 2):
            pairs += [(i, i + 1), (i + 1, i)]
        got.append(lax.ppermute(face, axis, pairs))
    return got


def transposed_dot(left, right):
    return lax.dot_general(
        left, right, (((0,), (0,)), ((), ())), preferred_element_type=jnp.float32
    )


def two(value):
    high = value.astype(BF)
    low = (value - high.astype(jnp.float32)).astype(BF)
    return jnp.concatenate([high, low], axis=1)


def both(left, right):
    k = left.shape[1] // 2
    full = transposed_dot(left, right)
    return full[:k, :k] + (full[:k, k:] + full[k:, :k]) + full[k:, k:]


def gather_terms(w, wide, at, s):
    rows = 4 * s.row

    def body(at_ref, w_ref, k_ref, f_ref, g_ref, m_ref, q_ref):
        def emit(here, c, near):
            q_ref[here, :] = c - near * (1.0 / 6.0)

        sweep(s, w_ref, emit)
        g_ref[...] = jnp.zeros_like(g_ref)
        m_ref[...] = jnp.zeros_like(m_ref)

        def step(i, _):
            here = pl.ds(pl.multiple_of(i * rows, rows), rows)
            w = w_ref[here, :]
            f = w * lax.rsqrt(k_ref[here, :])
            f_ref[here, :] = f
            pair = two(f)
            g_ref[...] += both(pair, pair)
            m_ref[...] += both(two(w), two(q_ref[here, :]))
            return 0

        lax.fori_loop(0, s.cells // rows, step, 0)

    outs = [f32(s.cells, s.k), f32(s.k, s.k), f32(s.k, s.k)]
    moved = 4 * 4 * s.cells * s.k
    return pl.pallas_call(
        body,
        out_shape=outs,
        in_specs=[SMEM, VMEM, VMEM],
        out_specs=(VMEM, VMEM, VMEM),
        scratch_shapes=[pltpu.VMEM((s.cells, s.k), jnp.float32)],
        compiler_params=pltpu.CompilerParams(vmem_limit_bytes=32 * 1024 * 1024),
        cost_estimate=pl.CostEstimate(
            flops=16 * s.cells * s.k * s.k, bytes_accessed=moved, transcendentals=0
        ),
    )(at, w, wide)


def pack_terms(gram, own, faces, ghosts, at, s, cells):
    k = s.k

    def body(at_ref, g_ref, m_ref, *refs):
        n = len(faces)
        m = jnp.zeros((k, k), jnp.float32)
        for left, right in zip(refs[:n], refs[n : 2 * n]):
            m += both(two(left[...]), two(right[...]))
        m = m_ref[...] - m * (1.0 / 6.0)
        raw = (m + m.T) * (0.5 / cells)
        below = lax.broadcasted_iota(jnp.int32, (k, k), 0)
        along = lax.broadcasted_iota(jnp.int32, (k, k), 1)
        refs[-1][:k, :] = jnp.where(below >= along, g_ref[...] * (1.0 / cells), raw)
        diagonal = jnp.sum(jnp.where(below == along, raw, 0.0), axis=0, keepdims=True)
        refs[-1][k:, :] = jnp.broadcast_to(diagonal, (8, k))

    ins = [at, gram, own] + list(faces) + list(ghosts)
    return call(body, [f32(k + 8, k)], ins, 6 * s.cells * k)[0]


def total(value, axes):
    for axis in axes:
        count = lax.axis_size(axis)
        bit = 1
        while bit < count:
            value = value + lax.ppermute(value, axis, [(i, i ^ bit) for i in range(count)])
            bit *= 2
    return value


def lower_inverse(gram):
    lower = jnp.linalg.cholesky(gram)
    return lax.linalg.triangular_solve(
        lower, jnp.eye(gram.shape[0], dtype=gram.dtype), left_side=True, lower=True
    )


def on_device(block, conductivity):
    s = Shape(block.shape)
    sizes = [lax.axis_size(a) for a in ("gx", "gy", "gz")]
    nz = 1 if sizes[2] == 2 else 2
    cells = float(s.cells * sizes[0] * sizes[1] * sizes[2])
    odd = [lax.rem(lax.axis_index(a), 2) for a in ("gx", "gy", "gz")]
    tops = (s.x - 1, s.y - 1, s.z - 1)
    at = jnp.stack(
        [jnp.where(odd[d] == first, tops[d], 0) for d in range(3) for first in range(2)]
    ).astype(jnp.int32)
    axes = [("gx", 0), ("gx", 1), ("gy", 0), ("gy", 1), ("gz", 0), ("gz", 1)][: 4 + nz]

    flat = block.reshape(s.cells, s.k)
    wide = jnp.broadcast_to(conductivity[..., None], block.shape).reshape(s.cells, s.k)
    w, *faces = prepare(flat, wide, at, s, nz)
    before = None
    for step in range(DEG):
        ghosts = exchange(faces, axes)
        part = interior(w, before, wide, at, s)
        scale = (1.0 if before is None else 2.0) / half_value
        before = w
        w, *faces = finish(part, wide, ghosts, at, s, nz, scale)
    ghosts = exchange(faces, axes)
    filtered, gram, own = gather_terms(w, wide, at, s)
    packed = total(pack_terms(gram, own, faces, ghosts, at, s, cells), ("gy", "gz", "gx"))
    upper, diagonal = packed[: s.k], packed[s.k]
    keep = jnp.tril(jnp.ones((s.k, s.k), bool))
    strict = jnp.tril(jnp.ones((s.k, s.k), bool), -1)
    gram = jnp.where(keep, upper, upper.T)
    raw = jnp.where(strict, upper.T, upper)
    raw = jnp.where(jnp.eye(s.k, dtype=bool), diagonal[None, :], raw)
    inverse = lower_inverse(gram)
    basis = jnp.dot(filtered, inverse.T, precision=HIGH).reshape(block.shape)
    projected = jnp.dot(jnp.dot(inverse, raw, precision=HIGH), inverse.T, precision=HIGH)
    return (basis, projected)


def solution(mesh):
    return jax.shard_map(
        on_device,
        mesh=mesh,
        in_specs=(P("gx", "gy", "gz", None), P("gx", "gy", "gz")),
        out_specs=(P("gx", "gy", "gz", None), P()),
        check_vma=False,
    )
```

```python
import functools
import jax
import jax.numpy as jnp
from jax import lax
from jax.experimental import pallas as pl
from jax.experimental.pallas import tpu as pltpu
from jax.sharding import PartitionSpec as P

DEG = 4

HIGH = lax.Precision.HIGHEST
center_value = 3.25
half_value = 2.75
VMEM = pl.BlockSpec(memory_space=pltpu.VMEM)
SMEM = pl.BlockSpec(memory_space=pltpu.SMEM)
BF = jnp.bfloat16


def call(body, outs, ins, flops, aliases=None):
    moved = sum(4 * a.size for a in list(outs) + list(ins))
    return pl.pallas_call(
        body,
        out_shape=outs,
        in_specs=[SMEM] + [VMEM] * (len(ins) - 1),
        out_specs=tuple(VMEM for _ in outs),
        input_output_aliases=aliases or {},
        compiler_params=pltpu.CompilerParams(vmem_limit_bytes=32 * 1024 * 1024),
        cost_estimate=pl.CostEstimate(flops=flops, bytes_accessed=moved, transcendentals=0),
    )(*ins)


def f32(rows, width):
    return jax.ShapeDtypeStruct((rows, width), jnp.float32)


class Shape:
    def __init__(self, shape):
        self.x, self.y, self.z, self.k = shape
        self.row = self.y * self.z
        self.cells = self.x * self.row


def faces_of(s, at, w_ref, out, x):
    for i in range(out["nz"]):
        out["z"][i][pl.ds(x * s.y, s.y), :] = w_ref[
            pl.ds(x * s.row + at[4 + i], s.y, stride=s.z), :
        ]
    for i in range(2):
        out["y"][i][pl.ds(x * s.z, s.z), :] = w_ref[pl.ds(x * s.row + at[2 + i] * s.z, s.z), :]


def x_faces(s, at, w_ref, out):
    for i in range(2):
        out["x"][i][...] = w_ref[pl.ds(at[i] * s.row, s.row), :]


def face_shapes(s, nz):
    return (
        [f32(s.row, s.k)] * 2 + [f32(s.x * s.z, s.k)] * 2 + [f32(s.x * s.y, s.k)] * nz
    )


def split_faces(refs, nz):
    return {"x": refs[0:2], "y": refs[2:4], "z": refs[4 : 4 + nz], "nz": nz}


def prepare(block, wide, at, s, nz):
    def body(at_ref, b_ref, k_ref, w_ref, *faces):
        out = split_faces(faces, nz)

        def step(x, _):
            here = pl.ds(pl.multiple_of(x * s.row, s.row), s.row)
            w_ref[here, :] = jnp.sqrt(k_ref[here, :]) * b_ref[here, :]
            faces_of(s, at_ref, w_ref, out, x)
            return 0

        lax.fori_loop(0, s.x, step, 0)
        x_faces(s, at_ref, w_ref, out)

    outs = [f32(s.cells, s.k)] + face_shapes(s, nz)
    return call(body, outs, [at, block, wide], 4 * s.cells * s.k)


def around(s, w_ref, x, low, high, emit):
    base = pl.multiple_of(x * s.row, s.row)
    place = lax.broadcasted_iota(jnp.int32, (s.z, s.k), 0)
    tiles = [w_ref[pl.ds(base + y * s.z, s.z), :] for y in range(s.y)]
    for y in range(s.y):
        c = tiles[y]
        up = jnp.where(place == s.z - 1, 0.0, pltpu.roll(c, s.z - 1, 0))
        down = jnp.where(place == 0, 0.0, pltpu.roll(c, 1, 0))
        near = up + down
        if y > 0:
            near = near + tiles[y - 1]
        if y < s.y - 1:
            near = near + tiles[y + 1]
        if low:
            near = near + w_ref[pl.ds(base - s.row + y * s.z, s.z), :]
        if high:
            near = near + w_ref[pl.ds(base + s.row + y * s.z, s.z), :]
        emit(pl.ds(base + y * s.z, s.z), c, near)


def sweep(s, w_ref, emit):
    around(s, w_ref, 0, False, True, emit)

    def step(x, _):
        around(s, w_ref, x, True, True, emit)
        return 0

    lax.fori_loop(1, s.x - 1, step, 0)
    around(s, w_ref, s.x - 1, True, False, emit)


def interior(w, before, wide, at, s):
    scale = (1.0 if before is None else 2.0) / half_value

    def body(at_ref, w_ref, k_ref, *rest):
        o_ref = rest[-1]

        def emit(here, c, near):
            new = k_ref[here, :] * ((c - near * (1.0 / 6.0)) * scale) - (scale * center_value) * c
            if before is not None:
                new = new - rest[0][here, :]
            o_ref[here, :] = new

        sweep(s, w_ref, emit)

    ins = [at, w, wide] + ([] if before is None else [before])
    return call(body, [f32(s.cells, s.k)], ins, 12 * s.cells * s.k)[0]


def finish(part, wide, ghosts, at, s, nz, scale):
    def body(at_ref, p_ref, k_ref, *refs):
        ghost = split_faces(refs[: 4 + nz], nz)
        w_ref = refs[4 + nz]
        out = split_faces(refs[5 + nz :], nz)
        factor = scale / 6.0
        for i in range(2):
            here = pl.ds(at_ref[i] * s.row, s.row)
            p_ref[here, :] = p_ref[here, :] - (k_ref[here, :] * factor) * ghost["x"][i][...]
        place = lax.broadcasted_iota(jnp.int32, (s.z, s.k), 0)

        def step(x, _):
            base = pl.multiple_of(x * s.row, s.row)
            for i in range(2):
                here = pl.ds(base + at_ref[2 + i] * s.z, s.z)
                g = ghost["y"][i][pl.ds(x * s.z, s.z), :]
                p_ref[here, :] = p_ref[here, :] - (k_ref[here, :] * factor) * g
            for y in range(s.y):
                here = pl.ds(base + y * s.z, s.z)
                add = 0.0
                for i in range(nz):
                    g = ghost["z"][i][pl.ds(x * s.y + y, 1), :]
                    add = jnp.where(place == at_ref[4 + i], jnp.broadcast_to(g, (s.z, s.k)), add)
                w_ref[here, :] = p_ref[here, :] - (k_ref[here, :] * factor) * add
            faces_of(s, at_ref, w_ref, out, x)
            return 0

        lax.fori_loop(0, s.x, step, 0)
        x_faces(s, at_ref, w_ref, out)

    outs = [f32(s.cells, s.k)] + face_shapes(s, nz)
    return call(body, outs, [at, part, wide] + list(ghosts), 4 * s.cells * s.k, {1: 0})


def exchange(faces, axes):
    got = []
    for face, (axis, first) in zip(faces, axes):
        count = lax.axis_size(axis)
        pairs = []
        for i in range(first, count - 1, 2):
            pairs += [(i, i + 1), (i + 1, i)]
        got.append(lax.ppermute(face, axis, pairs))
    return got


def transposed_dot(left, right):
    return lax.dot_general(
        left, right, (((0,), (0,)), ((), ())), preferred_element_type=jnp.float32
    )


def two(value):
    high = value.astype(BF)
    low = (value - high.astype(jnp.float32)).astype(BF)
    return jnp.concatenate([high, low], axis=1)


def both(left, right):
    k = left.shape[1] // 2
    full = transposed_dot(left, right)
    return full[:k, :k] + (full[:k, k:] + full[k:, :k]) + full[k:, k:]


def gather_terms(w, wide, at, s):
    rows = 4 * s.row

    def body(at_ref, w_ref, k_ref, f_ref, g_ref, m_ref, q_ref):
        def emit(here, c, near):
            q_ref[here, :] = c - near * (1.0 / 6.0)

        sweep(s, w_ref, emit)
        g_ref[...] = jnp.zeros_like(g_ref)
        m_ref[...] = jnp.zeros_like(m_ref)

        def step(i, _):
            here = pl.ds(pl.multiple_of(i * rows, rows), rows)
            w = w_ref[here, :]
            f = w * lax.rsqrt(k_ref[here, :])
            f_ref[here, :] = f
            pair = two(f)
            g_ref[...] += both(pair, pair)
            m_ref[...] += both(two(w), two(q_ref[here, :]))
            return 0

        lax.fori_loop(0, s.cells // rows, step, 0)

    outs = [f32(s.cells, s.k), f32(s.k, s.k), f32(s.k, s.k)]
    moved = 4 * 4 * s.cells * s.k
    return pl.pallas_call(
        body,
        out_shape=outs,
        in_specs=[SMEM, VMEM, VMEM],
        out_specs=(VMEM, VMEM, VMEM),
        scratch_shapes=[pltpu.VMEM((s.cells, s.k), jnp.float32)],
        compiler_params=pltpu.CompilerParams(vmem_limit_bytes=32 * 1024 * 1024),
        cost_estimate=pl.CostEstimate(
            flops=16 * s.cells * s.k * s.k, bytes_accessed=moved, transcendentals=0
        ),
    )(at, w, wide)


def pack_terms(gram, own, faces, ghosts, at, s, cells):
    k = s.k

    def body(at_ref, g_ref, m_ref, *refs):
        n = len(faces)
        m = jnp.zeros((k, k), jnp.float32)
        for left, right in zip(refs[:n], refs[n : 2 * n]):
            m += both(two(left[...]), two(right[...]))
        m = m_ref[...] - m * (1.0 / 6.0)
        raw = (m + m.T) * (0.5 / cells)
        below = lax.broadcasted_iota(jnp.int32, (k, k), 0)
        along = lax.broadcasted_iota(jnp.int32, (k, k), 1)
        refs[-1][:k, :] = jnp.where(below >= along, g_ref[...] * (1.0 / cells), raw)
        diagonal = jnp.sum(jnp.where(below == along, raw, 0.0), axis=0, keepdims=True)
        refs[-1][k:, :] = jnp.broadcast_to(diagonal, (8, k))

    ins = [at, gram, own] + list(faces) + list(ghosts)
    return call(body, [f32(k + 8, k)], ins, 6 * s.cells * k)[0]


def total(value, axes):
    for axis in axes:
        count = lax.axis_size(axis)
        bit = 1
        while bit < count:
            value = value + lax.ppermute(value, axis, [(i, i ^ bit) for i in range(count)])
            bit *= 2
    return value


PANEL = 32
GROUP = 8


def eliminate(m_ref, n):
    place = lax.broadcasted_iota(jnp.int32, (PANEL, n), 0)
    for top in range(0, n, PANEL):
        left, right = m_ref[top : top + PANEL, :n], m_ref[top : top + PANEL, n:]
        for first in range(0, PANEL, GROUP):
            columns = [
                jnp.broadcast_to(left[:, top + k : top + k + 1], (PANEL, n))
                for k in range(first, first + GROUP)
            ]
            for i in range(GROUP):
                k = first + i
                pivot = columns[i][k : k + 1, :]
                inverse = 1.0 / pivot
                root = lax.rsqrt(pivot)
                below = jnp.where(place > k, columns[i], 0.0)
                for t in range(i + 1, GROUP):
                    columns[t] = columns[t] - below * (columns[t][k : k + 1, :] * inverse)
                here = place == k
                one, two_ = left[k : k + 1, :], right[k : k + 1, :]
                left = jnp.where(here, one * root, left - below * (one * inverse))
                right = jnp.where(here, two_ * root, right - below * (two_ * inverse))
        m_ref[top : top + PANEL, :n] = left
        m_ref[top : top + PANEL, n:] = right
        if top + PANEL < n:
            both_sides = jnp.concatenate([left, right], axis=1)
            update = lax.dot_general(
                left, both_sides, (((0,), (0,)), ((), ())),
                precision=HIGH, preferred_element_type=jnp.float32,
            )
            m_ref[top + PANEL :, :] = m_ref[top + PANEL :, :] - update[top + PANEL :, :]


def orthonormal(packed, filtered, s):
    k = s.k
    rows = s.cells // 8

    def body(p_ref, f_ref, b_ref, o_ref, m_ref, t_ref):
        @pl.when(pl.program_id(0) == 0)
        def _():
            upper = p_ref[:k, :]
            turned = upper.T
            below = lax.broadcasted_iota(jnp.int32, (k, k), 0)
            along = lax.broadcasted_iota(jnp.int32, (k, k), 1)
            m_ref[:, :k] = jnp.where(below >= along, upper, turned)
            m_ref[:, k:] = jnp.where(below == along, 1.0, 0.0)
            raw = jnp.where(below < along, upper, turned)
            raw = jnp.where(below == along, p_ref[k : k + 1, :], raw)
            eliminate(m_ref, k)
            inverse = m_ref[:, k:]
            half = jnp.dot(inverse, raw, precision=HIGH, preferred_element_type=jnp.float32)
            o_ref[...] = lax.dot_general(
                half, inverse, (((1,), (1,)), ((), ())),
                precision=HIGH, preferred_element_type=jnp.float32,
            )
            pair = two(inverse.T)
            t_ref[:k, :] = pair
            t_ref[k:, :] = pair

        f = f_ref[pl.ds(pl.multiple_of(pl.program_id(0) * rows, rows), rows), :]
        out = jnp.dot(two(f), t_ref[...], preferred_element_type=jnp.float32)
        b_ref[...] = out[:, :k] + out[:, k:]

    return pl.pallas_call(
        body,
        grid=(8,),
        out_shape=[f32(s.cells, k), f32(k, k)],
        in_specs=[VMEM, VMEM],
        out_specs=(
            pl.BlockSpec((rows, k), lambda i: (i, 0)),
            pl.BlockSpec((k, k), lambda i: (0, 0)),
        ),
        scratch_shapes=[pltpu.VMEM((k, 2 * k), jnp.float32), pltpu.VMEM((2 * k, 2 * k), BF)],
        compiler_params=pltpu.CompilerParams(vmem_limit_bytes=32 * 1024 * 1024),
        cost_estimate=pl.CostEstimate(
            flops=8 * s.cells * k * k, bytes_accessed=8 * s.cells * k, transcendentals=0
        ),
    )(packed, filtered)


def on_device(block, conductivity):
    s = Shape(block.shape)
    sizes = [lax.axis_size(a) for a in ("gx", "gy", "gz")]
    nz = 1 if sizes[2] == 2 else 2
    cells = float(s.cells * sizes[0] * sizes[1] * sizes[2])
    odd = [lax.rem(lax.axis_index(a), 2) for a in ("gx", "gy", "gz")]
    tops = (s.x - 1, s.y - 1, s.z - 1)
    at = jnp.stack(
        [jnp.where(odd[d] == first, tops[d], 0) for d in range(3) for first in range(2)]
    ).astype(jnp.int32)
    axes = [("gx", 0), ("gx", 1), ("gy", 0), ("gy", 1), ("gz", 0), ("gz", 1)][: 4 + nz]

    flat = block.reshape(s.cells, s.k)
    wide = jnp.broadcast_to(conductivity[..., None], block.shape).reshape(s.cells, s.k)
    w, *faces = prepare(flat, wide, at, s, nz)
    before = None
    for step in range(DEG):
        ghosts = exchange(faces, axes)
        part = interior(w, before, wide, at, s)
        scale = (1.0 if before is None else 2.0) / half_value
        before = w
        w, *faces = finish(part, wide, ghosts, at, s, nz, scale)
    ghosts = exchange(faces, axes)
    filtered, gram, own = gather_terms(w, wide, at, s)
    packed = total(pack_terms(gram, own, faces, ghosts, at, s, cells), ("gy", "gz", "gx"))
    basis, projected = orthonormal(packed, filtered, s)
    return (basis.reshape(block.shape), projected)


def solution(mesh):
    return jax.shard_map(
        on_device,
        mesh=mesh,
        in_specs=(P("gx", "gy", "gz", None), P("gx", "gy", "gz")),
        out_specs=(P("gx", "gy", "gz", None), P()),
        check_vma=False,
    )
```

```python
import functools
import jax
import jax.numpy as jnp
from jax import lax
from jax.experimental import pallas as pl
from jax.experimental.pallas import tpu as pltpu
from jax.sharding import PartitionSpec as P

DEG = 4

HIGH = lax.Precision.HIGHEST
center_value = 3.25
half_value = 2.75
VMEM = pl.BlockSpec(memory_space=pltpu.VMEM)
SMEM = pl.BlockSpec(memory_space=pltpu.SMEM)
BF = jnp.bfloat16


def call(body, outs, ins, flops, aliases=None):
    moved = sum(4 * a.size for a in list(outs) + list(ins))
    return pl.pallas_call(
        body,
        out_shape=outs,
        in_specs=[SMEM] + [VMEM] * (len(ins) - 1),
        out_specs=tuple(VMEM for _ in outs),
        input_output_aliases=aliases or {},
        compiler_params=pltpu.CompilerParams(vmem_limit_bytes=32 * 1024 * 1024),
        cost_estimate=pl.CostEstimate(flops=flops, bytes_accessed=moved, transcendentals=0),
    )(*ins)


def f32(rows, width):
    return jax.ShapeDtypeStruct((rows, width), jnp.float32)


class Shape:
    def __init__(self, shape):
        self.x, self.y, self.z, self.k = shape
        self.row = self.y * self.z
        self.cells = self.x * self.row


def faces_of(s, at, w_ref, out, with_z=True):
    if with_z:
        for i in range(out["nz"]):
            out["z"][i][...] = w_ref[pl.ds(at[4 + i], s.x * s.y, stride=s.z), :]
    for i in range(2):
        out["x"][i][...] = w_ref[pl.ds(at[i] * s.row, s.row), :]
        for x in range(s.x):
            out["y"][i][pl.ds(x * s.z, s.z), :] = w_ref[
                pl.ds(x * s.row + at[2 + i] * s.z, s.z), :
            ]


def face_shapes(s, nz):
    return (
        [f32(s.row, s.k)] * 2 + [f32(s.x * s.z, s.k)] * 2 + [f32(s.x * s.y, s.k)] * nz
    )


def split_faces(refs, nz):
    return {"x": refs[0:2], "y": refs[2:4], "z": refs[4 : 4 + nz], "nz": nz}


def prepare(block, turned, at, s, nz):
    parts = 4
    rows = s.cells // parts

    def body(at_ref, b_hbm, k_ref, w_ref, wide_ref, *refs):
        out = split_faces(refs[: 4 + nz], nz)
        edge = refs[4 + nz : 4 + 2 * nz]
        b_ref, sems = refs[-2:]
        copies = []
        for i in range(parts):
            here = pl.ds(i * rows, rows)
            copies.append(pltpu.make_async_copy(b_hbm.at[here], b_ref.at[here], sems.at[i]))
            copies[-1].start()
        tiles = [k_ref[y] for y in range(s.y)]
        for x in range(s.x):
            for y in range(s.y):
                wide_ref[pl.ds(x * s.row + y * s.z, s.z), :] = jnp.broadcast_to(
                    tiles[y][:, x : x + 1], (s.z, s.k)
                )
        for i in range(parts):
            copies[i].wait()

            def step(x, _):
                here = pl.ds(pl.multiple_of(x * s.row, s.row), s.row)
                w_ref[here, :] = jnp.sqrt(wide_ref[here, :]) * b_ref[here, :]
                return 0

            lax.fori_loop(i * s.x // parts, (i + 1) * s.x // parts, step, 0, unroll=2)
        for i in range(nz):
            edge[i][...] = wide_ref[pl.ds(at_ref[4 + i], s.x * s.y, stride=s.z), :]
        faces_of(s, at_ref, w_ref, out)

    outs = [f32(s.cells, s.k)] * 2 + face_shapes(s, nz) + [f32(s.x * s.y, s.k)] * nz
    return pl.pallas_call(
        body,
        out_shape=outs,
        in_specs=[SMEM, pl.BlockSpec(memory_space=pl.ANY), VMEM],
        out_specs=tuple(VMEM for _ in outs),
        scratch_shapes=[
            pltpu.VMEM((s.cells, s.k), jnp.float32),
            pltpu.SemaphoreType.DMA((parts,)),
        ],
        compiler_params=pltpu.CompilerParams(vmem_limit_bytes=32 * 1024 * 1024),
        cost_estimate=pl.CostEstimate(
            flops=4 * s.cells * s.k, bytes_accessed=16 * s.cells * s.k, transcendentals=0
        ),
    )(at, block, turned)


def around(s, w_ref, x, low, high, emit):
    base = pl.multiple_of(x * s.row, s.row)
    place = lax.broadcasted_iota(jnp.int32, (s.z, s.k), 0)
    tiles = [w_ref[pl.ds(base + y * s.z, s.z), :] for y in range(s.y)]
    for y in range(s.y):
        c = tiles[y]
        up = jnp.where(place == s.z - 1, 0.0, pltpu.roll(c, s.z - 1, 0))
        down = jnp.where(place == 0, 0.0, pltpu.roll(c, 1, 0))
        near = up + down
        if y > 0:
            near = near + tiles[y - 1]
        if y < s.y - 1:
            near = near + tiles[y + 1]
        if low:
            near = near + w_ref[pl.ds(base - s.row + y * s.z, s.z), :]
        if high:
            near = near + w_ref[pl.ds(base + s.row + y * s.z, s.z), :]
        emit(pl.ds(base + y * s.z, s.z), c, near)


def sweep(s, w_ref, emit):
    around(s, w_ref, 0, False, True, emit)

    def step(x, _):
        around(s, w_ref, x, True, True, emit)
        return 0

    lax.fori_loop(1, s.x - 1, step, 0)
    around(s, w_ref, s.x - 1, True, False, emit)


def interior(w, before, wide, at, s):
    scale = (1.0 if before is None else 2.0) / half_value

    def body(at_ref, w_ref, k_ref, *rest):
        o_ref = rest[-1]

        def emit(here, c, near):
            new = k_ref[here, :] * ((c - near * (1.0 / 6.0)) * scale) - (scale * center_value) * c
            if before is not None:
                new = new - rest[0][here, :]
            o_ref[here, :] = new

        sweep(s, w_ref, emit)

    ins = [at, w, wide] + ([] if before is None else [before])
    return call(body, [f32(s.cells, s.k)], ins, 12 * s.cells * s.k)[0]


def finish(part, wide, edge, ghosts, at, s, nz, scale):
    def body(at_ref, p_ref, k_ref, *refs):
        del p_ref
        edges = refs[:nz]
        ghost = split_faces(refs[nz : 4 + 2 * nz], nz)
        w_ref = refs[4 + 2 * nz]
        out = split_faces(refs[5 + 2 * nz :], nz)
        factor = scale / 6.0
        for i in range(2):
            here = pl.ds(at_ref[i] * s.row, s.row)
            w_ref[here, :] = w_ref[here, :] - (k_ref[here, :] * factor) * ghost["x"][i][...]
            for x in range(s.x):
                here = pl.ds(x * s.row + at_ref[2 + i] * s.z, s.z)
                g = ghost["y"][i][pl.ds(x * s.z, s.z), :]
                w_ref[here, :] = w_ref[here, :] - (k_ref[here, :] * factor) * g
        for i in range(nz):
            for x in range(s.x):
                here = pl.ds(x * s.row + at_ref[4 + i], s.y, stride=s.z)
                flat = pl.ds(x * s.y, s.y)
                new = w_ref[here, :] - (edges[i][flat, :] * factor) * ghost["z"][i][flat, :]
                w_ref[here, :] = new
                out["z"][i][flat, :] = new
        faces_of(s, at_ref, w_ref, out, with_z=False)

    outs = [f32(s.cells, s.k)] + face_shapes(s, nz)
    ins = [at, part, wide] + list(edge) + list(ghosts)
    return call(body, outs, ins, 4 * s.x * s.y * s.k, {1: 0})


def exchange(faces, axes):
    got = []
    for face, (axis, first) in zip(faces, axes):
        count = lax.axis_size(axis)
        pairs = []
        for i in range(first, count - 1, 2):
            pairs += [(i, i + 1), (i + 1, i)]
        got.append(lax.ppermute(face, axis, pairs))
    return got


def transposed_dot(left, right):
    return lax.dot_general(
        left, right, (((0,), (0,)), ((), ())), preferred_element_type=jnp.float32
    )


def two(value):
    high = value.astype(BF)
    low = (value - high.astype(jnp.float32)).astype(BF)
    return jnp.concatenate([high, low], axis=1)


def both(full):
    k = full.shape[0] // 2
    return full[:k, :k] + (full[:k, k:] + full[k:, :k]) + full[k:, k:]


def gather_terms(w, wide, at, s):
    rows = s.cells // 4

    def body(at_ref, w_ref, k_ref, f_ref, g_ref, m_ref, q_ref):
        def emit(here, c, near):
            q_ref[here, :] = c - near * (1.0 / 6.0)

        sweep(s, w_ref, emit)
        sums = jnp.zeros((2 * s.k, 4 * s.k), jnp.float32)
        for i in range(s.cells // rows):
            here = pl.ds(i * rows, rows)
            k = k_ref[here, :]
            inverse = lax.rsqrt(k)
            f = w_ref[here, :] * inverse
            f_ref[here, :] = f
            pair = two(f)
            image = two((k * inverse) * q_ref[here, :])
            sums += transposed_dot(pair, jnp.concatenate([pair, image], axis=1))
        g_ref[...] = both(sums[:, : 2 * s.k])
        m_ref[...] = both(sums[:, 2 * s.k :])

    outs = [f32(s.cells, s.k), f32(s.k, s.k), f32(s.k, s.k)]
    moved = 4 * 4 * s.cells * s.k
    return pl.pallas_call(
        body,
        out_shape=outs,
        in_specs=[SMEM, VMEM, VMEM],
        out_specs=(VMEM, VMEM, VMEM),
        scratch_shapes=[pltpu.VMEM((s.cells, s.k), jnp.float32)],
        compiler_params=pltpu.CompilerParams(vmem_limit_bytes=32 * 1024 * 1024),
        cost_estimate=pl.CostEstimate(
            flops=16 * s.cells * s.k * s.k, bytes_accessed=moved, transcendentals=0
        ),
    )(at, w, wide)


def pack_terms(gram, own, faces, ghosts, at, s, cells):
    k = s.k

    def body(at_ref, g_ref, m_ref, *refs):
        n = len(faces)
        m = jnp.zeros((k, k), jnp.float32)
        for left, right in zip(refs[:n], refs[n : 2 * n]):
            m += both(transposed_dot(two(left[...]), two(right[...])))
        m = m_ref[...] - m * (1.0 / 6.0)
        raw = (m + m.T) * (0.5 / cells)
        below = lax.broadcasted_iota(jnp.int32, (k, k), 0)
        along = lax.broadcasted_iota(jnp.int32, (k, k), 1)
        refs[-1][:k, :] = jnp.where(below >= along, g_ref[...] * (1.0 / cells), raw)
        diagonal = jnp.sum(jnp.where(below == along, raw, 0.0), axis=0, keepdims=True)
        refs[-1][k:, :] = jnp.broadcast_to(diagonal, (8, k))

    ins = [at, gram, own] + list(faces) + list(ghosts)
    return call(body, [f32(k + 8, k)], ins, 6 * s.cells * k)[0]


def total(value, axes):
    for axis in axes:
        count = lax.axis_size(axis)
        bit = 1
        while bit < count:
            value = value + lax.ppermute(value, axis, [(i, i ^ bit) for i in range(count)])
            bit *= 2
    return value


PANEL = 32
GROUP = 8


def eliminate(m_ref, n):
    place = lax.broadcasted_iota(jnp.int32, (PANEL, n), 0)
    for top in range(0, n, PANEL):
        left, right = m_ref[top : top + PANEL, :n], m_ref[top : top + PANEL, n:]
        for first in range(0, PANEL, GROUP):
            columns = [
                jnp.broadcast_to(left[:, top + k : top + k + 1], (PANEL, n))
                for k in range(first, first + GROUP)
            ]
            for i in range(GROUP):
                k = first + i
                pivot = columns[i][k : k + 1, :]
                inverse = 1.0 / pivot
                root = lax.rsqrt(pivot)
                below = jnp.where(place > k, columns[i], 0.0)
                for t in range(i + 1, GROUP):
                    columns[t] = columns[t] - below * (columns[t][k : k + 1, :] * inverse)
                here = place == k
                one, two_ = left[k : k + 1, :], right[k : k + 1, :]
                left = jnp.where(here, one * root, left - below * (one * inverse))
                right = jnp.where(here, two_ * root, right - below * (two_ * inverse))
        m_ref[top : top + PANEL, :n] = left
        m_ref[top : top + PANEL, n:] = right
        if top + PANEL < n:
            both_sides = jnp.concatenate([left, right], axis=1)
            update = lax.dot_general(
                left, both_sides, (((0,), (0,)), ((), ())),
                precision=HIGH, preferred_element_type=jnp.float32,
            )
            m_ref[top + PANEL :, :] = m_ref[top + PANEL :, :] - update[top + PANEL :, :]


def orthonormal(packed, filtered, s):
    k = s.k
    rows = s.cells // 8

    def body(p_ref, f_ref, b_ref, o_ref, m_ref, t_ref):
        @pl.when(pl.program_id(0) == 0)
        def _():
            upper = p_ref[:k, :]
            turned = upper.T
            below = lax.broadcasted_iota(jnp.int32, (k, k), 0)
            along = lax.broadcasted_iota(jnp.int32, (k, k), 1)
            m_ref[:, :k] = jnp.where(below >= along, upper, turned)
            m_ref[:, k:] = jnp.where(below == along, 1.0, 0.0)
            raw = jnp.where(below < along, upper, turned)
            raw = jnp.where(below == along, p_ref[k : k + 1, :], raw)
            eliminate(m_ref, k)
            inverse = m_ref[:, k:]
            half = jnp.dot(inverse, raw, precision=HIGH, preferred_element_type=jnp.float32)
            o_ref[...] = lax.dot_general(
                half, inverse, (((1,), (1,)), ((), ())),
                precision=HIGH, preferred_element_type=jnp.float32,
            )
            pair = two(inverse.T)
            t_ref[:k, :] = pair
            t_ref[k:, :] = pair

        f = f_ref[pl.ds(pl.multiple_of(pl.program_id(0) * rows, rows), rows), :]
        out = jnp.dot(two(f), t_ref[...], preferred_element_type=jnp.float32)
        b_ref[...] = out[:, :k] + out[:, k:]

    return pl.pallas_call(
        body,
        grid=(8,),
        out_shape=[f32(s.cells, k), f32(k, k)],
        in_specs=[VMEM, VMEM],
        out_specs=(
            pl.BlockSpec((rows, k), lambda i: (i, 0)),
            pl.BlockSpec((k, k), lambda i: (0, 0)),
        ),
        scratch_shapes=[pltpu.VMEM((k, 2 * k), jnp.float32), pltpu.VMEM((2 * k, 2 * k), BF)],
        compiler_params=pltpu.CompilerParams(vmem_limit_bytes=32 * 1024 * 1024),
        cost_estimate=pl.CostEstimate(
            flops=8 * s.cells * k * k, bytes_accessed=8 * s.cells * k, transcendentals=0
        ),
    )(packed, filtered)


def on_device(block, conductivity):
    s = Shape(block.shape)
    sizes = [lax.axis_size(a) for a in ("gx", "gy", "gz")]
    nz = 1 if sizes[2] == 2 else 2
    cells = float(s.cells * sizes[0] * sizes[1] * sizes[2])
    odd = [lax.rem(lax.axis_index(a), 2) for a in ("gx", "gy", "gz")]
    tops = (s.x - 1, s.y - 1, s.z - 1)
    at = jnp.stack(
        [jnp.where(odd[d] == first, tops[d], 0) for d in range(3) for first in range(2)]
    ).astype(jnp.int32)
    axes = [("gx", 0), ("gx", 1), ("gy", 0), ("gy", 1), ("gz", 0), ("gz", 1)][: 4 + nz]

    flat = block.reshape(s.cells, s.k)
    turned = jnp.transpose(conductivity, (1, 2, 0))
    w, wide, *rest = prepare(flat, turned, at, s, nz)
    faces, edge = rest[: 4 + nz], rest[4 + nz :]
    before = None
    for step in range(DEG):
        ghosts = exchange(faces, axes)
        part = interior(w, before, wide, at, s)
        scale = (1.0 if before is None else 2.0) / half_value
        before = w
        w, *faces = finish(part, wide, edge, ghosts, at, s, nz, scale)
    ghosts = exchange(faces, axes)
    filtered, gram, own = gather_terms(w, wide, at, s)
    packed = total(pack_terms(gram, own, faces, ghosts, at, s, cells), ("gy", "gz", "gx"))
    basis, projected = orthonormal(packed, filtered, s)
    return (basis.reshape(block.shape), projected)


def solution(mesh):
    return jax.shard_map(
        on_device,
        mesh=mesh,
        in_specs=(P("gx", "gy", "gz", None), P("gx", "gy", "gz")),
        out_specs=(P("gx", "gy", "gz", None), P()),
        check_vma=False,
    )
```

```python
import functools
import jax
import jax.numpy as jnp
from jax import lax
from jax.experimental import pallas as pl
from jax.experimental.pallas import tpu as pltpu
from jax.sharding import PartitionSpec as P

DEG = 4

HIGH = lax.Precision.HIGHEST
center_value = 3.25
half_value = 2.75
VMEM = pl.BlockSpec(memory_space=pltpu.VMEM)
SMEM = pl.BlockSpec(memory_space=pltpu.SMEM)
BF = jnp.bfloat16


def call(body, outs, ins, flops, aliases=None):
    moved = sum(4 * a.size for a in list(outs) + list(ins))
    return pl.pallas_call(
        body,
        out_shape=outs,
        in_specs=[SMEM] + [VMEM] * (len(ins) - 1),
        out_specs=tuple(VMEM for _ in outs),
        input_output_aliases=aliases or {},
        compiler_params=pltpu.CompilerParams(vmem_limit_bytes=32 * 1024 * 1024),
        cost_estimate=pl.CostEstimate(flops=flops, bytes_accessed=moved, transcendentals=0),
    )(*ins)


def f32(rows, width):
    return jax.ShapeDtypeStruct((rows, width), jnp.float32)


class Shape:
    def __init__(self, shape):
        self.x, self.y, self.z, self.k = shape
        self.row = self.y * self.z
        self.cells = self.x * self.row
        self.room = self.cells + self.z


def faces_of(s, at, w_ref, out, with_z=True):
    if with_z:
        for i in range(out["nz"]):
            out["z"][i][...] = w_ref[pl.ds(at[4 + i], s.x * s.y, stride=s.z), :]
    for i in range(2):
        out["x"][i][...] = w_ref[pl.ds(at[i] * s.row, s.row), :]
        for x in range(s.x):
            out["y"][i][pl.ds(x * s.z, s.z), :] = w_ref[
                pl.ds(x * s.row + at[2 + i] * s.z, s.z), :
            ]


def face_shapes(s, nz):
    return (
        [f32(s.row, s.k)] * 2 + [f32(s.x * s.z, s.k)] * 2 + [f32(s.x * s.y, s.k)] * nz
    )


def split_faces(refs, nz):
    return {"x": refs[0:2], "y": refs[2:4], "z": refs[4 : 4 + nz], "nz": nz}


def prepare(block, turned, at, s, nz):
    parts = 4
    rows = s.cells // parts

    def body(at_ref, b_hbm, k_ref, w_ref, wide_ref, *refs):
        out = split_faces(refs[: 4 + nz], nz)
        edge = refs[4 + nz : 4 + 2 * nz]
        b_ref, c_ref, sems = refs[-3:]
        first = pltpu.make_async_copy(k_ref, c_ref, sems.at[parts])
        first.start()
        copies = []
        for i in range(parts):
            here = pl.ds(i * rows, rows)
            copies.append(pltpu.make_async_copy(b_hbm.at[here], b_ref.at[here], sems.at[i]))
            copies[-1].start()
        first.wait()
        tiles = [c_ref[y] for y in range(s.y)]
        for x in range(s.x):
            for y in range(s.y):
                wide_ref[pl.ds(x * s.row + y * s.z, s.z), :] = jnp.broadcast_to(
                    tiles[y][:, x : x + 1], (s.z, s.k)
                )
        for i in range(parts):
            copies[i].wait()

            def step(x, _):
                here = pl.ds(pl.multiple_of(x * s.row, s.row), s.row)
                w_ref[here, :] = jnp.sqrt(wide_ref[here, :]) * b_ref[here, :]
                return 0

            lax.fori_loop(i * s.x // parts, (i + 1) * s.x // parts, step, 0, unroll=2)
        for i in range(nz):
            edge[i][...] = wide_ref[pl.ds(at_ref[4 + i], s.x * s.y, stride=s.z), :]
        faces_of(s, at_ref, w_ref, out)

    outs = [f32(s.room, s.k)] * 2 + face_shapes(s, nz) + [f32(s.x * s.y, s.k)] * nz
    return pl.pallas_call(
        body,
        out_shape=outs,
        in_specs=[SMEM] + [pl.BlockSpec(memory_space=pltpu.HBM)] * 2,
        out_specs=tuple(VMEM for _ in outs),
        scratch_shapes=[
            pltpu.VMEM((s.cells, s.k), jnp.float32),
            pltpu.VMEM(turned.shape, jnp.float32),
            pltpu.SemaphoreType.DMA((parts + 1,)),
        ],
        compiler_params=pltpu.CompilerParams(vmem_limit_bytes=32 * 1024 * 1024),
        cost_estimate=pl.CostEstimate(
            flops=4 * s.cells * s.k, bytes_accessed=16 * s.cells * s.k, transcendentals=0
        ),
    )(at, block, turned)


def around(s, w_ref, x, low, high, emit):
    base = pl.multiple_of(x * s.row, s.row)
    place = lax.broadcasted_iota(jnp.int32, (s.z, s.k), 0)
    tiles = [w_ref[pl.ds(base + y * s.z, s.z), :] for y in range(s.y)]
    for y in range(s.y):
        c = tiles[y]
        up = jnp.where(place == s.z - 1, 0.0, pltpu.roll(c, s.z - 1, 0))
        down = jnp.where(place == 0, 0.0, pltpu.roll(c, 1, 0))
        near = up + down
        if y > 0:
            near = near + tiles[y - 1]
        if y < s.y - 1:
            near = near + tiles[y + 1]
        if low:
            near = near + w_ref[pl.ds(base - s.row + y * s.z, s.z), :]
        if high:
            near = near + w_ref[pl.ds(base + s.row + y * s.z, s.z), :]
        emit(pl.ds(base + y * s.z, s.z), c, near)


def sweep(s, w_ref, emit):
    around(s, w_ref, 0, False, True, emit)

    def step(x, _):
        around(s, w_ref, x, True, True, emit)
        return 0

    lax.fori_loop(1, s.x - 1, step, 0)
    around(s, w_ref, s.x - 1, True, False, emit)


def interior(w, before, wide, at, s):
    scale = (1.0 if before is None else 2.0) / half_value

    def body(at_ref, w_ref, k_ref, *rest):
        o_ref = rest[-1]

        def emit(here, c, near):
            new = k_ref[here, :] * ((c - near * (1.0 / 6.0)) * scale) - (scale * center_value) * c
            if before is not None:
                new = new - rest[0][here, :]
            o_ref[here, :] = new

        sweep(s, w_ref, emit)

    ins = [at, w, wide] + ([] if before is None else [before])
    return call(body, [f32(s.room, s.k)], ins, 12 * s.cells * s.k)[0]


def finish(part, wide, edge, ghosts, at, s, nz, scale, last):
    def body(at_ref, p_ref, k_ref, *refs):
        del p_ref
        edges = refs[:nz]
        ghost = split_faces(refs[nz : 4 + 2 * nz], nz)
        w_ref = refs[4 + 2 * nz]
        if last:
            out = refs[5 + 2 * nz :]
        else:
            out = split_faces(refs[5 + 2 * nz :], nz)
        factor = scale / 6.0
        for i in range(2):
            here = pl.ds(at_ref[i] * s.row, s.row)
            w_ref[here, :] = w_ref[here, :] - (k_ref[here, :] * factor) * ghost["x"][i][...]
            for x in range(s.x):
                here = pl.ds(x * s.row + at_ref[2 + i] * s.z, s.z)
                g = ghost["y"][i][pl.ds(x * s.z, s.z), :]
                w_ref[here, :] = w_ref[here, :] - (k_ref[here, :] * factor) * g
        for i in range(nz):
            for x in range(s.x):
                here = pl.ds(x * s.row + at_ref[4 + i], s.y, stride=s.z)
                flat = pl.ds(x * s.y, s.y)
                new = w_ref[here, :] - (edges[i][flat, :] * factor) * ghost["z"][i][flat, :]
                w_ref[here, :] = new
                if not last:
                    out["z"][i][flat, :] = new
        if last:
            out[0][...] = w_ref[: s.row, :]
            for x in range(s.x):
                out[1][x * s.z : (x + 1) * s.z, :] = w_ref[x * s.row : x * s.row + s.z, :]
            if halved(s, nz):
                start = (1 - at_ref[6]) * (s.cells // 2) + at_ref[4]
                out[2][...] = w_ref[pl.ds(start, s.x * s.y // 2, stride=s.z), :]
            else:
                out[2][...] = w_ref[pl.ds(0, s.x * s.y, stride=s.z), :]
        else:
            faces_of(s, at_ref, w_ref, out, with_z=False)

    if last:
        outs = [f32(s.room, s.k), f32(s.row, s.k), f32(s.x * s.z, s.k), f32(s.x * s.y // (2 if halved(s, nz) else 1), s.k)]
    else:
        outs = [f32(s.room, s.k)] + face_shapes(s, nz)
    ins = [at, part, wide] + list(edge) + list(ghosts)
    return call(body, outs, ins, 4 * s.x * s.y * s.k, {1: 0})


def halved(s, nz):
    return nz == 1 and s.x % 2 == 0


def one_way(faces, s, nz):
    got = []
    for face, axis in zip(faces, ("gx", "gy", "gz")):
        pairs = [(i, i - 1) for i in range(1, lax.axis_size(axis))]
        if axis == "gz" and halved(s, nz):
            pairs = [(0, 1), (1, 0)]
        got.append(lax.ppermute(face, axis, pairs))
    return got


def exchange(faces, axes):
    got = []
    for face, (axis, first) in zip(faces, axes):
        count = lax.axis_size(axis)
        pairs = []
        for i in range(first, count - 1, 2):
            pairs += [(i, i + 1), (i + 1, i)]
        got.append(lax.ppermute(face, axis, pairs))
    return got


def transposed_dot(left, right):
    return lax.dot_general(
        left, right, (((0,), (0,)), ((), ())), preferred_element_type=jnp.float32
    )


def two(value):
    high = value.astype(BF)
    low = (value - high.astype(jnp.float32)).astype(BF)
    return jnp.concatenate([high, low], axis=1)


def both(full):
    k = full.shape[0] // 2
    return full[:k, :k] + (full[:k, k:] + full[k:, :k]) + full[k:, k:]


def gather_terms(w, wide, at, s):
    rows = s.cells // 4

    def body(at_ref, w_ref, k_ref, f_ref, g_ref, m_ref, q_ref):
        def emit(here, c, near):
            q_ref[here, :] = c - near * (1.0 / 6.0)

        sweep(s, w_ref, emit)
        sums = jnp.zeros((2 * s.k, 4 * s.k), jnp.float32)
        for i in range(s.cells // rows):
            here = pl.ds(i * rows, rows)
            k = k_ref[here, :]
            inverse = lax.rsqrt(k)
            f = w_ref[here, :] * inverse
            f_ref[here, :] = f
            pair = two(f)
            image = two((k * inverse) * q_ref[here, :])
            sums += transposed_dot(pair, jnp.concatenate([pair, image], axis=1))
        g_ref[...] = both(sums[:, : 2 * s.k])
        m_ref[...] = both(sums[:, 2 * s.k :])

    outs = [f32(s.cells, s.k), f32(s.k, s.k), f32(s.k, s.k)]
    moved = 4 * 4 * s.cells * s.k
    return pl.pallas_call(
        body,
        out_shape=outs,
        in_specs=[SMEM, VMEM, VMEM],
        out_specs=(VMEM, VMEM, VMEM),
        scratch_shapes=[pltpu.VMEM((s.cells, s.k), jnp.float32)],
        compiler_params=pltpu.CompilerParams(vmem_limit_bytes=32 * 1024 * 1024),
        cost_estimate=pl.CostEstimate(
            flops=16 * s.cells * s.k * s.k, bytes_accessed=moved, transcendentals=0
        ),
    )(at, w, wide)


def pack_terms(gram, own, w, ghosts, at, s, nz, cells):
    k = s.k

    def body(at_ref, g_ref, m_ref, w_ref, x_ref, y_ref, z_ref, p_ref):
        lefts = [w_ref[s.cells - s.row : s.cells, :]]
        tops = [w_ref[(x + 1) * s.row - s.z : (x + 1) * s.row, :] for x in range(s.x)]
        lefts.append(jnp.concatenate(tops, axis=0))
        if halved(s, nz):
            start = at_ref[6] * (s.cells // 2) + at_ref[4]
            lefts.append(w_ref[pl.ds(start, s.x * s.y // 2, stride=s.z), :])
        else:
            lefts.append(w_ref[pl.ds(s.z - 1, s.x * s.y, stride=s.z), :])
        left = jnp.concatenate(lefts, axis=0)
        right = jnp.concatenate([x_ref[...], y_ref[...], z_ref[...]], axis=0)
        m = m_ref[...] - both(transposed_dot(two(left), two(right))) * (2.0 / 6.0)
        raw = (m + m.T) * (0.5 / cells)
        below = lax.broadcasted_iota(jnp.int32, (k, k), 0)
        along = lax.broadcasted_iota(jnp.int32, (k, k), 1)
        p_ref[:k, :] = jnp.where(below >= along, g_ref[...] * (1.0 / cells), raw)
        diagonal = jnp.sum(jnp.where(below == along, raw, 0.0), axis=0, keepdims=True)
        p_ref[k:, :] = jnp.broadcast_to(diagonal, (8, k))

    ins = [at, gram, own, w] + list(ghosts)
    return call(body, [f32(k + 8, k)], ins, 6 * s.cells * k)[0]


def total(value, axes):
    for axis in axes:
        count = lax.axis_size(axis)
        bit = 1
        while bit < count:
            value = value + lax.ppermute(value, axis, [(i, i ^ bit) for i in range(count)])
            bit *= 2
    return value


PANEL = 32
GROUP = 8


def eliminate(m_ref, n):
    place = lax.broadcasted_iota(jnp.int32, (PANEL, n), 0)
    for top in range(0, n, PANEL):
        left, right = m_ref[top : top + PANEL, :n], m_ref[top : top + PANEL, n:]
        for first in range(0, PANEL, GROUP):
            columns = [
                jnp.broadcast_to(left[:, top + k : top + k + 1], (PANEL, n))
                for k in range(first, first + GROUP)
            ]
            for i in range(GROUP):
                k = first + i
                pivot = columns[i][k : k + 1, :]
                inverse = 1.0 / pivot
                root = lax.rsqrt(pivot)
                below = jnp.where(place > k, columns[i], 0.0)
                for t in range(i + 1, GROUP):
                    columns[t] = columns[t] - below * (columns[t][k : k + 1, :] * inverse)
                here = place == k
                one, two_ = left[k : k + 1, :], right[k : k + 1, :]
                left = jnp.where(here, one * root, left - below * (one * inverse))
                right = jnp.where(here, two_ * root, right - below * (two_ * inverse))
        m_ref[top : top + PANEL, :n] = left
        m_ref[top : top + PANEL, n:] = right
        if top + PANEL < n:
            both_sides = jnp.concatenate([left, right], axis=1)
            update = lax.dot_general(
                left, both_sides, (((0,), (0,)), ((), ())),
                precision=HIGH, preferred_element_type=jnp.float32,
            )
            m_ref[top + PANEL :, :] = m_ref[top + PANEL :, :] - update[top + PANEL :, :]


def orthonormal(packed, filtered, s):
    k = s.k
    rows = s.cells // 8

    def body(p_ref, f_ref, b_ref, o_ref, m_ref, t_ref):
        @pl.when(pl.program_id(0) == 0)
        def _():
            upper = p_ref[:k, :]
            turned = upper.T
            below = lax.broadcasted_iota(jnp.int32, (k, k), 0)
            along = lax.broadcasted_iota(jnp.int32, (k, k), 1)
            m_ref[:, :k] = jnp.where(below >= along, upper, turned)
            m_ref[:, k:] = jnp.where(below == along, 1.0, 0.0)
            raw = jnp.where(below < along, upper, turned)
            raw = jnp.where(below == along, p_ref[k : k + 1, :], raw)
            eliminate(m_ref, k)
            inverse = m_ref[:, k:]
            half = jnp.dot(inverse, raw, precision=HIGH, preferred_element_type=jnp.float32)
            o_ref[...] = lax.dot_general(
                half, inverse, (((1,), (1,)), ((), ())),
                precision=HIGH, preferred_element_type=jnp.float32,
            )
            pair = two(inverse.T)
            t_ref[:k, :] = pair
            t_ref[k:, :] = pair

        f = f_ref[pl.ds(pl.multiple_of(pl.program_id(0) * rows, rows), rows), :]
        out = jnp.dot(two(f), t_ref[...], preferred_element_type=jnp.float32)
        b_ref[...] = out[:, :k] + out[:, k:]

    return pl.pallas_call(
        body,
        grid=(8,),
        out_shape=[f32(s.cells, k), f32(k, k)],
        in_specs=[VMEM, VMEM],
        out_specs=(
            pl.BlockSpec((rows, k), lambda i: (i, 0)),
            pl.BlockSpec((k, k), lambda i: (0, 0)),
        ),
        scratch_shapes=[pltpu.VMEM((k, 2 * k), jnp.float32), pltpu.VMEM((2 * k, 2 * k), BF)],
        compiler_params=pltpu.CompilerParams(vmem_limit_bytes=32 * 1024 * 1024),
        cost_estimate=pl.CostEstimate(
            flops=8 * s.cells * k * k, bytes_accessed=8 * s.cells * k, transcendentals=0
        ),
    )(packed, filtered)


def on_device(block, conductivity):
    s = Shape(block.shape)
    sizes = [lax.axis_size(a) for a in ("gx", "gy", "gz")]
    nz = 1 if sizes[2] == 2 else 2
    cells = float(s.cells * sizes[0] * sizes[1] * sizes[2])
    odd = [lax.rem(lax.axis_index(a), 2) for a in ("gx", "gy", "gz")]
    tops = (s.x - 1, s.y - 1, s.z - 1)
    at = jnp.stack(
        [jnp.where(odd[d] == first, tops[d], 0) for d in range(3) for first in range(2)]
        + [odd[2], odd[1]]
    ).astype(jnp.int32)
    axes = [("gx", 0), ("gx", 1), ("gy", 0), ("gy", 1), ("gz", 0), ("gz", 1)][: 4 + nz]

    flat = block.reshape(s.cells, s.k)
    turned = jnp.transpose(conductivity, (1, 2, 0))
    w, wide, *rest = prepare(flat, turned, at, s, nz)
    faces, edge = rest[: 4 + nz], rest[4 + nz :]
    before = None
    for step in range(DEG):
        ghosts = exchange(faces, axes)
        part = interior(w, before, wide, at, s)
        scale = (1.0 if before is None else 2.0) / half_value
        before = w
        w, *faces = finish(part, wide, edge, ghosts, at, s, nz, scale, step == DEG - 1)
    ghosts = one_way(faces, s, nz)
    filtered, gram, own = gather_terms(w, wide, at, s)
    packed = total(pack_terms(gram, own, w, ghosts, at, s, nz, cells), ("gy", "gz", "gx"))
    basis, projected = orthonormal(packed, filtered, s)
    return (basis.reshape(block.shape), projected)


def solution(mesh):
    return jax.shard_map(
        on_device,
        mesh=mesh,
        in_specs=(P("gx", "gy", "gz", None), P("gx", "gy", "gz")),
        out_specs=(P("gx", "gy", "gz", None), P()),
        check_vma=False,
    )
```

```python
import functools
import jax
import jax.numpy as jnp
from jax import lax
from jax.experimental import pallas as pl
from jax.experimental.pallas import tpu as pltpu
from jax.sharding import PartitionSpec as P

DEG = 4

HIGH = lax.Precision.HIGHEST
center_value = 3.25
half_value = 2.75
VMEM = pl.BlockSpec(memory_space=pltpu.VMEM)
SMEM = pl.BlockSpec(memory_space=pltpu.SMEM)
BF = jnp.bfloat16


def call(body, outs, ins, flops, aliases=None):
    moved = sum(4 * a.size for a in list(outs) + list(ins))
    return pl.pallas_call(
        body,
        out_shape=outs,
        in_specs=[SMEM] + [VMEM] * (len(ins) - 1),
        out_specs=tuple(VMEM for _ in outs),
        input_output_aliases=aliases or {},
        compiler_params=pltpu.CompilerParams(vmem_limit_bytes=32 * 1024 * 1024),
        cost_estimate=pl.CostEstimate(flops=flops, bytes_accessed=moved, transcendentals=0),
    )(*ins)


def f32(rows, width):
    return jax.ShapeDtypeStruct((rows, width), jnp.float32)


class Shape:
    def __init__(self, shape):
        self.x, self.y, self.z, self.k = shape
        self.row = self.y * self.z
        self.cells = self.x * self.row
        self.room = self.cells + self.z


def faces_of(s, at, w_ref, out, with_z=True):
    if with_z:
        for i in range(out["nz"]):
            out["z"][i][...] = w_ref[pl.ds(at[4 + i], s.x * s.y, stride=s.z), :]
    for i in range(2):
        out["x"][i][...] = w_ref[pl.ds(at[i] * s.row, s.row), :]
        for x in range(s.x):
            out["y"][i][pl.ds(x * s.z, s.z), :] = w_ref[
                pl.ds(x * s.row + at[2 + i] * s.z, s.z), :
            ]


def face_shapes(s, nz):
    return (
        [f32(s.row, s.k)] * 2 + [f32(s.x * s.z, s.k)] * 2 + [f32(s.x * s.y, s.k)] * nz
    )


def split_faces(refs, nz):
    return {"x": refs[0:2], "y": refs[2:4], "z": refs[4 : 4 + nz], "nz": nz}


def spread(turned, at, s, nz):
    def body(at_ref, k_ref, wide_ref, *edge):
        for y in range(s.y):
            tile = k_ref[y]
            for x in range(s.x):
                wide_ref[pl.ds(x * s.row + y * s.z, s.z), :] = jnp.broadcast_to(
                    tile[:, x : x + 1], (s.z, s.k)
                )
        for i in range(nz):
            edge[i][...] = wide_ref[pl.ds(at_ref[4 + i], s.x * s.y, stride=s.z), :]

    outs = [f32(s.room, s.k)] + [f32(s.x * s.y, s.k)] * nz
    return call(body, outs, [at, turned], s.cells * s.k)


def prepare(block, wide, at, s, nz):
    def body(at_ref, b_ref, k_ref, w_ref, *faces):
        def step(x, _):
            here = pl.ds(pl.multiple_of(x * s.row, s.row), s.row)
            w_ref[here, :] = jnp.sqrt(k_ref[here, :]) * b_ref[here, :]
            return 0

        lax.fori_loop(0, s.x, step, 0, unroll=2)
        faces_of(s, at_ref, w_ref, split_faces(faces, nz))

    return call(body, [f32(s.room, s.k)] + face_shapes(s, nz), [at, block, wide], 4 * s.cells * s.k)


def around(s, w_ref, x, low, high, emit):
    base = pl.multiple_of(x * s.row, s.row)
    place = lax.broadcasted_iota(jnp.int32, (s.z, s.k), 0)
    tiles = [w_ref[pl.ds(base + y * s.z, s.z), :] for y in range(s.y)]
    for y in range(s.y):
        c = tiles[y]
        up = jnp.where(place == s.z - 1, 0.0, pltpu.roll(c, s.z - 1, 0))
        down = jnp.where(place == 0, 0.0, pltpu.roll(c, 1, 0))
        near = up + down
        if y > 0:
            near = near + tiles[y - 1]
        if y < s.y - 1:
            near = near + tiles[y + 1]
        if low:
            near = near + w_ref[pl.ds(base - s.row + y * s.z, s.z), :]
        if high:
            near = near + w_ref[pl.ds(base + s.row + y * s.z, s.z), :]
        emit(pl.ds(base + y * s.z, s.z), c, near)


def sweep(s, w_ref, emit):
    around(s, w_ref, 0, False, True, emit)

    def step(x, _):
        around(s, w_ref, x, True, True, emit)
        return 0

    lax.fori_loop(1, s.x - 1, step, 0)
    around(s, w_ref, s.x - 1, True, False, emit)


def interior(w, before, wide, at, s):
    scale = (1.0 if before is None else 2.0) / half_value

    def body(at_ref, w_ref, k_ref, *rest):
        o_ref = rest[-1]

        def emit(here, c, near):
            new = k_ref[here, :] * ((c - near * (1.0 / 6.0)) * scale) - (scale * center_value) * c
            if before is not None:
                new = new - rest[0][here, :]
            o_ref[here, :] = new

        sweep(s, w_ref, emit)

    ins = [at, w, wide] + ([] if before is None else [before])
    return call(body, [f32(s.room, s.k)], ins, 12 * s.cells * s.k)[0]


def finish(part, wide, edge, ghosts, at, s, nz, scale, last):
    def body(at_ref, p_ref, k_ref, *refs):
        del p_ref
        edges = refs[:nz]
        ghost = split_faces(refs[nz : 4 + 2 * nz], nz)
        w_ref = refs[4 + 2 * nz]
        if last:
            out = refs[5 + 2 * nz :]
        else:
            out = split_faces(refs[5 + 2 * nz :], nz)
        factor = scale / 6.0
        for i in range(2):
            here = pl.ds(at_ref[i] * s.row, s.row)
            w_ref[here, :] = w_ref[here, :] - (k_ref[here, :] * factor) * ghost["x"][i][...]
            for x in range(s.x):
                here = pl.ds(x * s.row + at_ref[2 + i] * s.z, s.z)
                g = ghost["y"][i][pl.ds(x * s.z, s.z), :]
                w_ref[here, :] = w_ref[here, :] - (k_ref[here, :] * factor) * g
        for i in range(nz):
            for x in range(s.x):
                here = pl.ds(x * s.row + at_ref[4 + i], s.y, stride=s.z)
                flat = pl.ds(x * s.y, s.y)
                new = w_ref[here, :] - (edges[i][flat, :] * factor) * ghost["z"][i][flat, :]
                w_ref[here, :] = new
                if not last:
                    out["z"][i][flat, :] = new
        if last:
            out[0][...] = w_ref[: s.row, :]
            for x in range(s.x):
                out[1][x * s.z : (x + 1) * s.z, :] = w_ref[x * s.row : x * s.row + s.z, :]
            if halved(s, nz):
                start = (1 - at_ref[6]) * (s.cells // 2) + at_ref[4]
                out[2][...] = w_ref[pl.ds(start, s.x * s.y // 2, stride=s.z), :]
            else:
                out[2][...] = w_ref[pl.ds(0, s.x * s.y, stride=s.z), :]
        else:
            faces_of(s, at_ref, w_ref, out, with_z=False)

    if last:
        outs = [f32(s.room, s.k), f32(s.row, s.k), f32(s.x * s.z, s.k), f32(s.x * s.y // (2 if halved(s, nz) else 1), s.k)]
    else:
        outs = [f32(s.room, s.k)] + face_shapes(s, nz)
    ins = [at, part, wide] + list(edge) + list(ghosts)
    return call(body, outs, ins, 4 * s.x * s.y * s.k, {1: 0})


def halved(s, nz):
    return nz == 1 and s.x % 2 == 0


def one_way(faces, s, nz):
    got = []
    for face, axis in zip(faces, ("gx", "gy", "gz")):
        pairs = [(i, i - 1) for i in range(1, lax.axis_size(axis))]
        if axis == "gz" and halved(s, nz):
            pairs = [(0, 1), (1, 0)]
        got.append(lax.ppermute(face, axis, pairs))
    return got


def exchange(faces, axes):
    got = []
    for face, (axis, first) in zip(faces, axes):
        count = lax.axis_size(axis)
        pairs = []
        for i in range(first, count - 1, 2):
            pairs += [(i, i + 1), (i + 1, i)]
        got.append(lax.ppermute(face, axis, pairs))
    return got


def transposed_dot(left, right):
    return lax.dot_general(
        left, right, (((0,), (0,)), ((), ())), preferred_element_type=jnp.float32
    )


def two(value):
    high = value.astype(BF)
    low = (value - high.astype(jnp.float32)).astype(BF)
    return jnp.concatenate([high, low], axis=1)


def both(full):
    k = full.shape[0] // 2
    return full[:k, :k] + (full[:k, k:] + full[k:, :k]) + full[k:, k:]


def gather_terms(w, wide, at, s):
    rows = s.cells // 4

    def body(at_ref, w_ref, k_ref, f_ref, g_ref, m_ref, q_ref):
        def emit(here, c, near):
            q_ref[here, :] = c - near * (1.0 / 6.0)

        sweep(s, w_ref, emit)
        sums = jnp.zeros((2 * s.k, 4 * s.k), jnp.float32)
        for i in range(s.cells // rows):
            here = pl.ds(i * rows, rows)
            k = k_ref[here, :]
            inverse = lax.rsqrt(k)
            f = w_ref[here, :] * inverse
            f_ref[here, :] = f
            pair = two(f)
            image = two((k * inverse) * q_ref[here, :])
            sums += transposed_dot(pair, jnp.concatenate([pair, image], axis=1))
        g_ref[...] = both(sums[:, : 2 * s.k])
        m_ref[...] = both(sums[:, 2 * s.k :])

    outs = [f32(s.cells, s.k), f32(s.k, s.k), f32(s.k, s.k)]
    moved = 4 * 4 * s.cells * s.k
    return pl.pallas_call(
        body,
        out_shape=outs,
        in_specs=[SMEM, VMEM, VMEM],
        out_specs=(VMEM, VMEM, VMEM),
        scratch_shapes=[pltpu.VMEM((s.cells, s.k), jnp.float32)],
        compiler_params=pltpu.CompilerParams(vmem_limit_bytes=32 * 1024 * 1024),
        cost_estimate=pl.CostEstimate(
            flops=16 * s.cells * s.k * s.k, bytes_accessed=moved, transcendentals=0
        ),
    )(at, w, wide)


def pack_terms(gram, own, w, ghosts, at, s, nz, cells):
    k = s.k

    def body(at_ref, g_ref, m_ref, w_ref, x_ref, y_ref, z_ref, mine_ref, other_ref):
        lefts = [w_ref[s.cells - s.row : s.cells, :]]
        tops = [w_ref[(x + 1) * s.row - s.z : (x + 1) * s.row, :] for x in range(s.x)]
        lefts.append(jnp.concatenate(tops, axis=0))
        if halved(s, nz):
            start = at_ref[6] * (s.cells // 2) + at_ref[4]
            lefts.append(w_ref[pl.ds(start, s.x * s.y // 2, stride=s.z), :])
        else:
            lefts.append(w_ref[pl.ds(s.z - 1, s.x * s.y, stride=s.z), :])
        left = jnp.concatenate(lefts, axis=0)
        right = jnp.concatenate([x_ref[...], y_ref[...], z_ref[...]], axis=0)
        m = m_ref[...] - both(transposed_dot(two(left), two(right))) * (2.0 / 6.0)
        raw = (m + m.T) * (0.5 / cells)
        below = lax.broadcasted_iota(jnp.int32, (k, k), 0)
        along = lax.broadcasted_iota(jnp.int32, (k, k), 1)
        full = jnp.where(below >= along, g_ref[...] * (1.0 / cells), raw)
        diagonal = jnp.sum(jnp.where(below == along, raw, 0.0), axis=0, keepdims=True)
        even = at_ref[7] == 0
        for ref, first in ((mine_ref, even), (other_ref, jnp.logical_not(even))):
            ref[: k // 2, :] = jnp.where(first, full[: k // 2, :], full[k // 2 :, :])
            ref[k // 2 :, :] = jnp.broadcast_to(diagonal, (8, k))

    ins = [at, gram, own, w] + list(ghosts)
    return call(body, [f32(k // 2 + 8, k)] * 2, ins, 6 * s.cells * k)


def total(mine, other):
    axes = ("gx", "gy", "gz")
    sizes = [lax.axis_size(a) for a in axes]

    def swap(value, flip):
        pairs = []
        for i in range(sizes[0] * sizes[1] * sizes[2]):
            x, y, z = i // (sizes[1] * sizes[2]), i // sizes[2] % sizes[1], i % sizes[2]
            x, y, z = x ^ flip[0], y ^ flip[1], z ^ flip[2]
            pairs.append((i, (x * sizes[1] + y) * sizes[2] + z))
        return lax.ppermute(value, axes, pairs)

    hops = []
    for d, first in ((1, 2), (2, 1), (0, 1)):
        bit = first
        while bit < sizes[d]:
            hops.append(tuple(bit if e == d else 0 for e in range(3)))
            bit *= 2
    pair = (0, 1, 0)
    value = mine + swap(other, pair)
    while hops:
        a, *hops = hops
        if hops:
            b, *hops = hops
            c = tuple(i ^ j for i, j in zip(a, b))
            value = (value + swap(value, a)) + (swap(value, b) + swap(value, c))
        else:
            value = value + swap(value, a)
    return value, swap(value, pair)


PANEL = 32
GROUP = 8


def eliminate(m_ref, n):
    place = lax.broadcasted_iota(jnp.int32, (PANEL, n), 0)
    for top in range(0, n, PANEL):
        left, right = m_ref[top : top + PANEL, :n], m_ref[top : top + PANEL, n:]
        for first in range(0, PANEL, GROUP):
            columns = [
                jnp.broadcast_to(left[:, top + k : top + k + 1], (PANEL, n))
                for k in range(first, first + GROUP)
            ]
            for i in range(GROUP):
                k = first + i
                pivot = columns[i][k : k + 1, :]
                inverse = 1.0 / pivot
                root = lax.rsqrt(pivot)
                below = jnp.where(place > k, columns[i], 0.0)
                for t in range(i + 1, GROUP):
                    columns[t] = columns[t] - below * (columns[t][k : k + 1, :] * inverse)
                here = place == k
                one, two_ = left[k : k + 1, :], right[k : k + 1, :]
                left = jnp.where(here, one * root, left - below * (one * inverse))
                right = jnp.where(here, two_ * root, right - below * (two_ * inverse))
        m_ref[top : top + PANEL, :n] = left
        m_ref[top : top + PANEL, n:] = right
        if top + PANEL < n:
            both_sides = jnp.concatenate([left, right], axis=1)
            update = lax.dot_general(
                left, both_sides, (((0,), (0,)), ((), ())),
                precision=HIGH, preferred_element_type=jnp.float32,
            )
            m_ref[top + PANEL :, :] = m_ref[top + PANEL :, :] - update[top + PANEL :, :]


def orthonormal(own, got, filtered, at, s):
    k = s.k
    parts = 4
    rows = s.cells // parts

    def body(at_ref, own_ref, got_ref, f_ref, b_ref, o_ref, m_ref, t_ref):
        @pl.when(pl.program_id(0) == 0)
        def _():
            even = at_ref[7] == 0
            one, other = own_ref[: k // 2, :], got_ref[: k // 2, :]
            upper = jnp.concatenate(
                [jnp.where(even, one, other), jnp.where(even, other, one)], axis=0
            )
            diagonal = jnp.where(even, own_ref[k // 2 : k // 2 + 1, :], got_ref[k // 2 : k // 2 + 1, :])
            turned = upper.T
            below = lax.broadcasted_iota(jnp.int32, (k, k), 0)
            along = lax.broadcasted_iota(jnp.int32, (k, k), 1)
            m_ref[:, :k] = jnp.where(below >= along, upper, turned)
            m_ref[:, k:] = jnp.where(below == along, 1.0, 0.0)
            raw = jnp.where(below < along, upper, turned)
            raw = jnp.where(below == along, diagonal, raw)
            eliminate(m_ref, k)
            inverse = m_ref[:, k:]
            half = jnp.dot(inverse, raw, precision=HIGH, preferred_element_type=jnp.float32)
            o_ref[...] = lax.dot_general(
                half, inverse, (((1,), (1,)), ((), ())),
                precision=HIGH, preferred_element_type=jnp.float32,
            )
            pair = two(inverse.T)
            t_ref[:k, :] = pair
            t_ref[k:, :] = pair

        f = f_ref[pl.ds(pl.multiple_of(pl.program_id(0) * rows, rows), rows), :]
        out = jnp.dot(two(f), t_ref[...], preferred_element_type=jnp.float32)
        b_ref[...] = out[:, :k] + out[:, k:]

    return pl.pallas_call(
        body,
        grid=(parts,),
        out_shape=[f32(s.cells, k), f32(k, k)],
        in_specs=[SMEM, VMEM, VMEM, VMEM],
        out_specs=(
            pl.BlockSpec((rows, k), lambda i: (i, 0)),
            pl.BlockSpec((k, k), lambda i: (0, 0)),
        ),
        scratch_shapes=[pltpu.VMEM((k, 2 * k), jnp.float32), pltpu.VMEM((2 * k, 2 * k), BF)],
        compiler_params=pltpu.CompilerParams(vmem_limit_bytes=32 * 1024 * 1024),
        cost_estimate=pl.CostEstimate(
            flops=8 * s.cells * k * k, bytes_accessed=8 * s.cells * k, transcendentals=0
        ),
    )(at, own, got, filtered)


def on_device(block, conductivity):
    s = Shape(block.shape)
    sizes = [lax.axis_size(a) for a in ("gx", "gy", "gz")]
    nz = 1 if sizes[2] == 2 else 2
    cells = float(s.cells * sizes[0] * sizes[1] * sizes[2])
    odd = [lax.rem(lax.axis_index(a), 2) for a in ("gx", "gy", "gz")]
    tops = (s.x - 1, s.y - 1, s.z - 1)
    at = jnp.stack(
        [jnp.where(odd[d] == first, tops[d], 0) for d in range(3) for first in range(2)]
        + [odd[2], odd[1]]
    ).astype(jnp.int32)
    axes = [("gx", 0), ("gx", 1), ("gy", 0), ("gy", 1), ("gz", 0), ("gz", 1)][: 4 + nz]

    flat = block.reshape(s.cells, s.k)
    turned = jnp.transpose(conductivity, (1, 2, 0))
    wide, *edge = spread(turned, at, s, nz)
    w, *faces = prepare(flat, wide, at, s, nz)
    before = None
    for step in range(DEG):
        ghosts = exchange(faces, axes)
        part = interior(w, before, wide, at, s)
        scale = (1.0 if before is None else 2.0) / half_value
        before = w
        w, *faces = finish(part, wide, edge, ghosts, at, s, nz, scale, step == DEG - 1)
    ghosts = one_way(faces, s, nz)
    filtered, gram, own = gather_terms(w, wide, at, s)
    halves = total(*pack_terms(gram, own, w, ghosts, at, s, nz, cells))
    basis, projected = orthonormal(*halves, filtered, at, s)
    return (basis.reshape(block.shape), projected)


def solution(mesh):
    return jax.shard_map(
        on_device,
        mesh=mesh,
        in_specs=(P("gx", "gy", "gz", None), P("gx", "gy", "gz")),
        out_specs=(P("gx", "gy", "gz", None), P()),
        check_vma=False,
    )
```

```python
import functools
import jax
import jax.numpy as jnp
from jax import lax
from jax.experimental import pallas as pl
from jax.experimental.pallas import tpu as pltpu
from jax.sharding import PartitionSpec as P

DEG = 4

HIGH = lax.Precision.HIGHEST
center_value = 3.25
half_value = 2.75
VMEM = pl.BlockSpec(memory_space=pltpu.VMEM)
SMEM = pl.BlockSpec(memory_space=pltpu.SMEM)
BF = jnp.bfloat16


def call(body, outs, ins, flops, aliases=None):
    moved = sum(4 * a.size for a in list(outs) + list(ins))
    return pl.pallas_call(
        body,
        out_shape=outs,
        in_specs=[SMEM] + [VMEM] * (len(ins) - 1),
        out_specs=tuple(VMEM for _ in outs),
        input_output_aliases=aliases or {},
        compiler_params=pltpu.CompilerParams(vmem_limit_bytes=32 * 1024 * 1024),
        cost_estimate=pl.CostEstimate(flops=flops, bytes_accessed=moved, transcendentals=0),
    )(*ins)


def f32(rows, width):
    return jax.ShapeDtypeStruct((rows, width), jnp.float32)


class Shape:
    def __init__(self, shape):
        self.x, self.y, self.z, self.k = shape
        self.row = self.y * self.z
        self.cells = self.x * self.row
        self.room = self.cells + self.z


def faces_of(s, at, w_ref, out, with_z=True):
    if with_z:
        for i in range(out["nz"]):
            out["z"][i][...] = w_ref[pl.ds(at[4 + i], s.x * s.y, stride=s.z), :]
    for i in range(2):
        out["x"][i][...] = w_ref[pl.ds(at[i] * s.row, s.row), :]
        for x in range(s.x):
            out["y"][i][pl.ds(x * s.z, s.z), :] = w_ref[
                pl.ds(x * s.row + at[2 + i] * s.z, s.z), :
            ]


def face_shapes(s, nz):
    return (
        [f32(s.row, s.k)] * 2 + [f32(s.x * s.z, s.k)] * 2 + [f32(s.x * s.y, s.k)] * nz
    )


def split_faces(refs, nz):
    return {"x": refs[0:2], "y": refs[2:4], "z": refs[4 : 4 + nz], "nz": nz}


def prepare(block, turned, at, s, nz):
    def body(at_ref, b_ref, k_ref, w_ref, wide_ref, *refs):
        for y in range(s.y):
            tile = k_ref[y]
            for x in range(s.x):
                here = pl.ds(x * s.row + y * s.z, s.z)
                k = jnp.broadcast_to(tile[:, x : x + 1], (s.z, s.k))
                wide_ref[here, :] = k
                w_ref[here, :] = jnp.sqrt(k) * b_ref[here, :]
        for i in range(nz):
            refs[4 + nz + i][...] = wide_ref[pl.ds(at_ref[4 + i], s.x * s.y, stride=s.z), :]
        faces_of(s, at_ref, w_ref, split_faces(refs, nz))

    outs = [f32(s.room, s.k)] * 2 + face_shapes(s, nz) + [f32(s.x * s.y, s.k)] * nz
    return call(body, outs, [at, block, turned], 4 * s.cells * s.k)


def around(s, w_ref, o_ref, x, low, high, emit):
    base = pl.multiple_of(x * s.row, s.row)
    place = lax.broadcasted_iota(jnp.int32, (s.z, s.k), 0)
    tiles = [w_ref[pl.ds(base + y * s.z, s.z), :] for y in range(s.y)]
    done = []
    for y in range(s.y):
        c = tiles[y]
        up = jnp.where(place == s.z - 1, 0.0, pltpu.roll(c, s.z - 1, 0))
        down = jnp.where(place == 0, 0.0, pltpu.roll(c, 1, 0))
        near = up + down
        if y > 0:
            near = near + tiles[y - 1]
        if y < s.y - 1:
            near = near + tiles[y + 1]
        if low:
            near = near + w_ref[pl.ds(base - s.row + y * s.z, s.z), :]
        if high:
            near = near + w_ref[pl.ds(base + s.row + y * s.z, s.z), :]
        here = pl.ds(base + y * s.z, s.z)
        done.append((here, emit(here, c, near)))
    for here, new in done:
        o_ref[here, :] = new


def sweep(s, w_ref, o_ref, emit):
    around(s, w_ref, o_ref, 0, False, True, emit)

    def step(x, _):
        around(s, w_ref, o_ref, x, True, True, emit)
        return 0

    lax.fori_loop(1, s.x - 1, step, 0, unroll=2)
    around(s, w_ref, o_ref, s.x - 1, True, False, emit)


def interior(w, before, wide, at, s):
    scale = (1.0 if before is None else 2.0) / half_value

    def body(at_ref, w_ref, k_ref, *rest):
        o_ref = rest[-1]

        def emit(here, c, near):
            new = k_ref[here, :] * ((c - near * (1.0 / 6.0)) * scale) - (scale * center_value) * c
            if before is not None:
                new = new - rest[0][here, :]
            return new

        sweep(s, w_ref, o_ref, emit)

    ins = [at, w, wide] + ([] if before is None else [before])
    return call(body, [f32(s.room, s.k)], ins, 12 * s.cells * s.k)[0]


def finish(part, wide, edge, ghosts, at, s, nz, scale, last):
    def body(at_ref, p_ref, k_ref, *refs):
        del p_ref
        edges = refs[:nz]
        ghost = split_faces(refs[nz : 4 + 2 * nz], nz)
        w_ref = refs[4 + 2 * nz]
        if last:
            out = refs[5 + 2 * nz :]
        else:
            out = split_faces(refs[5 + 2 * nz :], nz)
        factor = scale / 6.0
        for i in range(2):
            here = pl.ds(at_ref[i] * s.row, s.row)
            w_ref[here, :] = w_ref[here, :] - (k_ref[here, :] * factor) * ghost["x"][i][...]
            done = []
            for x in range(s.x):
                here = pl.ds(x * s.row + at_ref[2 + i] * s.z, s.z)
                g = ghost["y"][i][pl.ds(x * s.z, s.z), :]
                done.append((here, w_ref[here, :] - (k_ref[here, :] * factor) * g))
            for here, new in done:
                w_ref[here, :] = new
        for i in range(nz):
            for first in range(0, s.x, 8):
                done = []
                for x in range(first, min(first + 8, s.x)):
                    here = pl.ds(x * s.row + at_ref[4 + i], s.y, stride=s.z)
                    flat = pl.ds(x * s.y, s.y)
                    new = w_ref[here, :] - (edges[i][flat, :] * factor) * ghost["z"][i][flat, :]
                    done.append((here, flat, new))
                for here, flat, new in done:
                    w_ref[here, :] = new
                    if not last:
                        out["z"][i][flat, :] = new
        if last:
            out[0][...] = w_ref[: s.row, :]
            for x in range(s.x):
                out[1][x * s.z : (x + 1) * s.z, :] = w_ref[x * s.row : x * s.row + s.z, :]
            if halved(s, nz):
                start = (1 - at_ref[6]) * (s.cells // 2) + at_ref[4]
                out[2][...] = w_ref[pl.ds(start, s.x * s.y // 2, stride=s.z), :]
            else:
                out[2][...] = w_ref[pl.ds(0, s.x * s.y, stride=s.z), :]
        else:
            faces_of(s, at_ref, w_ref, out, with_z=False)

    if last:
        outs = [f32(s.room, s.k), f32(s.row, s.k), f32(s.x * s.z, s.k), f32(s.x * s.y // (2 if halved(s, nz) else 1), s.k)]
    else:
        outs = [f32(s.room, s.k)] + face_shapes(s, nz)
    ins = [at, part, wide] + list(edge) + list(ghosts)
    return call(body, outs, ins, 4 * s.x * s.y * s.k, {1: 0})


def halved(s, nz):
    return nz == 1 and s.x % 2 == 0


def one_way(faces, s, nz):
    got = []
    for face, axis in zip(faces, ("gx", "gy", "gz")):
        pairs = [(i, i - 1) for i in range(1, lax.axis_size(axis))]
        if axis == "gz" and halved(s, nz):
            pairs = [(0, 1), (1, 0)]
        got.append(lax.ppermute(face, axis, pairs))
    return got


def exchange(faces, axes):
    got = []
    for face, (axis, first) in zip(faces, axes):
        count = lax.axis_size(axis)
        pairs = []
        for i in range(first, count - 1, 2):
            pairs += [(i, i + 1), (i + 1, i)]
        got.append(lax.ppermute(face, axis, pairs))
    return got


def transposed_dot(left, right):
    return lax.dot_general(
        left, right, (((0,), (0,)), ((), ())), preferred_element_type=jnp.float32
    )


def two(value):
    high = value.astype(BF)
    low = (value - high.astype(jnp.float32)).astype(BF)
    return jnp.concatenate([high, low], axis=1)


def both(full):
    k = full.shape[0] // 2
    return full[:k, :k] + (full[:k, k:] + full[k:, :k]) + full[k:, k:]


def gather_terms(w, wide, at, s):
    rows = s.cells // 4

    def body(at_ref, w_ref, k_ref, f_ref, g_ref, m_ref, q_ref):
        def emit(here, c, near):
            return c - near * (1.0 / 6.0)

        sweep(s, w_ref, q_ref, emit)
        sums = jnp.zeros((2 * s.k, 4 * s.k), jnp.float32)
        for i in range(s.cells // rows):
            here = pl.ds(i * rows, rows)
            k = k_ref[here, :]
            inverse = lax.rsqrt(k)
            pair = two(w_ref[here, :] * inverse)
            f_ref[here, :] = pair
            image = two((k * inverse) * q_ref[here, :])
            sums += transposed_dot(pair, jnp.concatenate([pair, image], axis=1))
        g_ref[...] = both(sums[:, : 2 * s.k])
        m_ref[...] = both(sums[:, 2 * s.k :])

    outs = [jax.ShapeDtypeStruct((s.cells, 2 * s.k), BF), f32(s.k, s.k), f32(s.k, s.k)]
    moved = 4 * 4 * s.cells * s.k
    return pl.pallas_call(
        body,
        out_shape=outs,
        in_specs=[SMEM, VMEM, VMEM],
        out_specs=(VMEM, VMEM, VMEM),
        scratch_shapes=[pltpu.VMEM((s.cells, s.k), jnp.float32)],
        compiler_params=pltpu.CompilerParams(vmem_limit_bytes=32 * 1024 * 1024),
        cost_estimate=pl.CostEstimate(
            flops=16 * s.cells * s.k * s.k, bytes_accessed=moved, transcendentals=0
        ),
    )(at, w, wide)


def pack_terms(gram, own, w, ghosts, at, s, nz, cells):
    k = s.k

    def body(at_ref, g_ref, m_ref, w_ref, x_ref, y_ref, z_ref, mine_ref, other_ref):
        lefts = [w_ref[s.cells - s.row : s.cells, :]]
        tops = [w_ref[(x + 1) * s.row - s.z : (x + 1) * s.row, :] for x in range(s.x)]
        lefts.append(jnp.concatenate(tops, axis=0))
        if halved(s, nz):
            start = at_ref[6] * (s.cells // 2) + at_ref[4]
            lefts.append(w_ref[pl.ds(start, s.x * s.y // 2, stride=s.z), :])
        else:
            lefts.append(w_ref[pl.ds(s.z - 1, s.x * s.y, stride=s.z), :])
        left = jnp.concatenate(lefts, axis=0)
        right = jnp.concatenate([x_ref[...], y_ref[...], z_ref[...]], axis=0)
        m = m_ref[...] - both(transposed_dot(two(left), two(right))) * (2.0 / 6.0)
        raw = (m + m.T) * (0.5 / cells)
        below = lax.broadcasted_iota(jnp.int32, (k, k), 0)
        along = lax.broadcasted_iota(jnp.int32, (k, k), 1)
        full = jnp.where(below >= along, g_ref[...] * (1.0 / cells), raw)
        diagonal = jnp.sum(jnp.where(below == along, raw, 0.0), axis=0, keepdims=True)
        even = at_ref[7] == 0
        for ref, first in ((mine_ref, even), (other_ref, jnp.logical_not(even))):
            ref[: k // 2, :] = jnp.where(first, full[: k // 2, :], full[k // 2 :, :])
            ref[k // 2 :, :] = jnp.broadcast_to(diagonal, (8, k))

    ins = [at, gram, own, w] + list(ghosts)
    return call(body, [f32(k // 2 + 8, k)] * 2, ins, 6 * s.cells * k)


def total(mine, other):
    axes = ("gx", "gy", "gz")
    sizes = [lax.axis_size(a) for a in axes]

    def swap(value, flip):
        pairs = []
        for i in range(sizes[0] * sizes[1] * sizes[2]):
            x, y, z = i // (sizes[1] * sizes[2]), i // sizes[2] % sizes[1], i % sizes[2]
            x, y, z = x ^ flip[0], y ^ flip[1], z ^ flip[2]
            pairs.append((i, (x * sizes[1] + y) * sizes[2] + z))
        return lax.ppermute(value, axes, pairs)

    hops = []
    for d, first in ((1, 2), (2, 1), (0, 1)):
        bit = first
        while bit < sizes[d]:
            hops.append(tuple(bit if e == d else 0 for e in range(3)))
            bit *= 2
    pair = (0, 1, 0)
    value = mine + swap(other, pair)
    while hops:
        a, *hops = hops
        if hops:
            b, *hops = hops
            c = tuple(i ^ j for i, j in zip(a, b))
            value = (value + swap(value, a)) + (swap(value, b) + swap(value, c))
        else:
            value = value + swap(value, a)
    return value, swap(value, pair)


PANEL = 32
GROUP = 16


def eliminate(m_ref, n):
    place = lax.broadcasted_iota(jnp.int32, (PANEL, n), 0)
    for top in range(0, n, PANEL):
        left, right = m_ref[top : top + PANEL, :n], m_ref[top : top + PANEL, n:]
        for first in range(0, PANEL, GROUP):
            columns = [
                jnp.broadcast_to(left[:, top + k : top + k + 1], (PANEL, n))
                for k in range(first, first + GROUP)
            ]
            for i in range(GROUP):
                k = first + i
                pivot = columns[i][k : k + 1, :]
                inverse = 1.0 / pivot
                root = lax.rsqrt(pivot)
                below = jnp.where(place > k, columns[i], 0.0)
                for t in range(i + 1, GROUP):
                    columns[t] = columns[t] - below * (columns[t][k : k + 1, :] * inverse)
                here = place == k
                one, two_ = left[k : k + 1, :], right[k : k + 1, :]
                left = jnp.where(here, one * root, left - below * (one * inverse))
                right = jnp.where(here, two_ * root, right - below * (two_ * inverse))
        m_ref[top : top + PANEL, :n] = left
        m_ref[top : top + PANEL, n:] = right
        if top + PANEL < n:
            both_sides = jnp.concatenate([left, right], axis=1)
            update = lax.dot_general(
                left, both_sides, (((0,), (0,)), ((), ())),
                precision=HIGH, preferred_element_type=jnp.float32,
            )
            m_ref[top + PANEL :, :] = m_ref[top + PANEL :, :] - update[top + PANEL :, :]


def orthonormal(own, got, filtered, at, s):
    k = s.k
    parts = 4
    rows = s.cells // parts

    def body(at_ref, own_ref, got_ref, f_ref, b_hbm, o_ref, m_ref, b_ref, sems):
        even = at_ref[7] == 0
        one, other = own_ref[: k // 2, :], got_ref[: k // 2, :]
        upper = jnp.concatenate(
            [jnp.where(even, one, other), jnp.where(even, other, one)], axis=0
        )
        low, high = own_ref[k // 2 : k // 2 + 1, :], got_ref[k // 2 : k // 2 + 1, :]
        turned = upper.T
        below = lax.broadcasted_iota(jnp.int32, (k, k), 0)
        along = lax.broadcasted_iota(jnp.int32, (k, k), 1)
        m_ref[:, :k] = jnp.where(below >= along, upper, turned)
        m_ref[:, k:] = jnp.where(below == along, 1.0, 0.0)
        eliminate(m_ref, k)
        inverse = m_ref[:, k:]
        pair = two(inverse.T)
        pair = jnp.concatenate([pair, pair], axis=0)
        copies = []
        for i in range(parts):
            here = pl.ds(i * rows, rows)
            out = jnp.dot(f_ref[here, :], pair, preferred_element_type=jnp.float32)
            b_ref[here, :] = out[:, :k] + out[:, k:]
            copies.append(pltpu.make_async_copy(b_ref.at[here], b_hbm.at[here], sems.at[i]))
            copies[-1].start()
        raw = jnp.where(below < along, upper, turned)
        raw = jnp.where(below == along, jnp.where(even, low, high), raw)
        half = jnp.dot(inverse, raw, precision=HIGH, preferred_element_type=jnp.float32)
        o_ref[...] = lax.dot_general(
            half, inverse, (((1,), (1,)), ((), ())),
            precision=HIGH, preferred_element_type=jnp.float32,
        )
        for copy in copies:
            copy.wait()

    return pl.pallas_call(
        body,
        out_shape=[f32(s.cells, k), f32(k, k)],
        in_specs=[SMEM, VMEM, VMEM, VMEM],
        out_specs=(pl.BlockSpec(memory_space=pl.ANY), VMEM),
        scratch_shapes=[
            pltpu.VMEM((k, 2 * k), jnp.float32),
            pltpu.VMEM((s.cells, k), jnp.float32),
            pltpu.SemaphoreType.DMA((parts,)),
        ],
        compiler_params=pltpu.CompilerParams(vmem_limit_bytes=32 * 1024 * 1024),
        cost_estimate=pl.CostEstimate(
            flops=8 * s.cells * k * k, bytes_accessed=8 * s.cells * k, transcendentals=0
        ),
    )(at, own, got, filtered)


def on_device(block, conductivity):
    s = Shape(block.shape)
    sizes = [lax.axis_size(a) for a in ("gx", "gy", "gz")]
    nz = 1 if sizes[2] == 2 else 2
    cells = float(s.cells * sizes[0] * sizes[1] * sizes[2])
    odd = [lax.rem(lax.axis_index(a), 2) for a in ("gx", "gy", "gz")]
    tops = (s.x - 1, s.y - 1, s.z - 1)
    at = jnp.stack(
        [jnp.where(odd[d] == first, tops[d], 0) for d in range(3) for first in range(2)]
        + [odd[2], odd[1]]
    ).astype(jnp.int32)
    axes = [("gx", 0), ("gx", 1), ("gy", 0), ("gy", 1), ("gz", 0), ("gz", 1)][: 4 + nz]

    flat = block.reshape(s.cells, s.k)
    turned = jnp.transpose(conductivity, (1, 2, 0))
    w, wide, *rest = prepare(flat, turned, at, s, nz)
    faces, edge = rest[: 4 + nz], rest[4 + nz :]
    before = None
    for step in range(DEG):
        ghosts = exchange(faces, axes)
        part = interior(w, before, wide, at, s)
        scale = (1.0 if before is None else 2.0) / half_value
        before = w
        w, *faces = finish(part, wide, edge, ghosts, at, s, nz, scale, step == DEG - 1)
    ghosts = one_way(faces, s, nz)
    filtered, gram, own = gather_terms(w, wide, at, s)
    halves = total(*pack_terms(gram, own, w, ghosts, at, s, nz, cells))
    basis, projected = orthonormal(*halves, filtered, at, s)
    return (basis.reshape(block.shape), projected)


def solution(mesh):
    return jax.shard_map(
        on_device,
        mesh=mesh,
        in_specs=(P("gx", "gy", "gz", None), P("gx", "gy", "gz")),
        out_specs=(P("gx", "gy", "gz", None), P()),
        check_vma=False,
    )
```

```python
import functools
import jax
import jax.numpy as jnp
from jax import lax
from jax.experimental import pallas as pl
from jax.experimental.pallas import tpu as pltpu
from jax.sharding import PartitionSpec as P

DEG = 4

HIGH = lax.Precision.HIGHEST
center_value = 3.25
half_value = 2.75
VMEM = pl.BlockSpec(memory_space=pltpu.VMEM)
BF = jnp.bfloat16


def call(body, outs, ins, flops, aliases=None):
    moved = sum(4 * a.size for a in list(outs) + list(ins))
    return pl.pallas_call(
        body,
        out_shape=outs,
        in_specs=[VMEM] * len(ins),
        out_specs=tuple(VMEM for _ in outs),
        input_output_aliases=aliases or {},
        compiler_params=pltpu.CompilerParams(vmem_limit_bytes=32 * 1024 * 1024),
        cost_estimate=pl.CostEstimate(flops=flops, bytes_accessed=moved, transcendentals=0),
    )(*ins)


def f32(rows, width):
    return jax.ShapeDtypeStruct((rows, width), jnp.float32)


class Shape:
    def __init__(self, shape):
        self.x, self.y, self.z, self.k = shape
        self.row = self.y * self.z
        self.cells = self.x * self.row
        self.room = self.cells + self.z


def places(s):
    odd = [lax.rem(lax.axis_index(a), 2) for a in ("gx", "gy", "gz")]
    tops = (s.x - 1, s.y - 1, s.z - 1)
    at = [jnp.where(odd[d] == first, tops[d], 0) for d in range(3) for first in range(2)]
    return at + [odd[2], odd[1]]


def faces_of(s, at, w_ref, out, with_z=True):
    if with_z:
        for i in range(out["nz"]):
            out["z"][i][...] = w_ref[pl.ds(at[4 + i], s.x * s.y, stride=s.z), :]
    for i in range(2):
        out["x"][i][...] = w_ref[pl.ds(at[i] * s.row, s.row), :]
        for x in range(s.x):
            out["y"][i][pl.ds(x * s.z, s.z), :] = w_ref[
                pl.ds(x * s.row + at[2 + i] * s.z, s.z), :
            ]


def face_shapes(s, nz):
    return (
        [f32(s.row, s.k)] * 2 + [f32(s.x * s.z, s.k)] * 2 + [f32(s.x * s.y, s.k)] * nz
    )


def split_faces(refs, nz):
    return {"x": refs[0:2], "y": refs[2:4], "z": refs[4 : 4 + nz], "nz": nz}


def prepare(block, turned, s, nz):
    def body(b_ref, k_ref, w_ref, wide_ref, *refs):
        at_ref = places(s)
        for y in range(s.y):
            tile = k_ref[y]
            for x in range(s.x):
                here = pl.ds(x * s.row + y * s.z, s.z)
                k = jnp.broadcast_to(tile[:, x : x + 1], (s.z, s.k))
                wide_ref[here, :] = k
                w_ref[here, :] = jnp.sqrt(k) * b_ref[here, :]
        for i in range(nz):
            refs[4 + nz + i][...] = wide_ref[pl.ds(at_ref[4 + i], s.x * s.y, stride=s.z), :]
        faces_of(s, at_ref, w_ref, split_faces(refs, nz))

    outs = [f32(s.room, s.k)] * 2 + face_shapes(s, nz) + [f32(s.x * s.y, s.k)] * nz
    return call(body, outs, [block, turned], 4 * s.cells * s.k)


def around(s, w_ref, o_ref, x, low, high, emit):
    base = pl.multiple_of(x * s.row, s.row)
    place = lax.broadcasted_iota(jnp.int32, (s.z, s.k), 0)
    tiles = [w_ref[pl.ds(base + y * s.z, s.z), :] for y in range(s.y)]
    done = []
    for y in range(s.y):
        c = tiles[y]
        up = jnp.where(place == s.z - 1, 0.0, pltpu.roll(c, s.z - 1, 0))
        down = jnp.where(place == 0, 0.0, pltpu.roll(c, 1, 0))
        near = up + down
        if y > 0:
            near = near + tiles[y - 1]
        if y < s.y - 1:
            near = near + tiles[y + 1]
        if low:
            near = near + w_ref[pl.ds(base - s.row + y * s.z, s.z), :]
        if high:
            near = near + w_ref[pl.ds(base + s.row + y * s.z, s.z), :]
        here = pl.ds(base + y * s.z, s.z)
        done.append((here, emit(here, c, near)))
    for here, new in done:
        o_ref[here, :] = new


def sweep(s, w_ref, o_ref, emit):
    around(s, w_ref, o_ref, 0, False, True, emit)

    def step(x, _):
        around(s, w_ref, o_ref, x, True, True, emit)
        return 0

    lax.fori_loop(1, s.x - 1, step, 0, unroll=2)
    around(s, w_ref, o_ref, s.x - 1, True, False, emit)


def interior(w, before, wide, s):
    scale = (1.0 if before is None else 2.0) / half_value

    def body(w_ref, k_ref, *rest):
        o_ref = rest[-1]

        def emit(here, c, near):
            new = k_ref[here, :] * ((c - near * (1.0 / 6.0)) * scale) - (scale * center_value) * c
            if before is not None:
                new = new - rest[0][here, :]
            return new

        sweep(s, w_ref, o_ref, emit)

    ins = [w, wide] + ([] if before is None else [before])
    return call(body, [f32(s.room, s.k)], ins, 12 * s.cells * s.k)[0]


def finish(part, wide, edge, ghosts, s, nz, scale, last):
    def body(p_ref, k_ref, *refs):
        del p_ref
        at_ref = places(s)
        edges = refs[:nz]
        ghost = split_faces(refs[nz : 4 + 2 * nz], nz)
        w_ref = refs[4 + 2 * nz]
        if last:
            out = refs[5 + 2 * nz :]
        else:
            out = split_faces(refs[5 + 2 * nz :], nz)
        factor = scale / 6.0
        for i in range(2):
            here = pl.ds(at_ref[i] * s.row, s.row)
            w_ref[here, :] = w_ref[here, :] - (k_ref[here, :] * factor) * ghost["x"][i][...]
            done = []
            for x in range(s.x):
                here = pl.ds(x * s.row + at_ref[2 + i] * s.z, s.z)
                g = ghost["y"][i][pl.ds(x * s.z, s.z), :]
                done.append((here, w_ref[here, :] - (k_ref[here, :] * factor) * g))
            for here, new in done:
                w_ref[here, :] = new
        for i in range(nz):
            for first in range(0, s.x, 8):
                done = []
                for x in range(first, min(first + 8, s.x)):
                    here = pl.ds(x * s.row + at_ref[4 + i], s.y, stride=s.z)
                    flat = pl.ds(x * s.y, s.y)
                    new = w_ref[here, :] - (edges[i][flat, :] * factor) * ghost["z"][i][flat, :]
                    done.append((here, flat, new))
                for here, flat, new in done:
                    w_ref[here, :] = new
                    if not last:
                        out["z"][i][flat, :] = new
        if last:
            out[0][...] = w_ref[: s.row, :]
            for x in range(s.x):
                out[1][x * s.z : (x + 1) * s.z, :] = w_ref[x * s.row : x * s.row + s.z, :]
            if halved(s, nz):
                start = (1 - at_ref[6]) * (s.cells // 2) + at_ref[4]
                out[2][...] = w_ref[pl.ds(start, s.x * s.y // 2, stride=s.z), :]
            else:
                out[2][...] = w_ref[pl.ds(0, s.x * s.y, stride=s.z), :]
        else:
            faces_of(s, at_ref, w_ref, out, with_z=False)

    if last:
        outs = [f32(s.room, s.k), f32(s.row, s.k), f32(s.x * s.z, s.k), f32(s.x * s.y // (2 if halved(s, nz) else 1), s.k)]
    else:
        outs = [f32(s.room, s.k)] + face_shapes(s, nz)
    ins = [part, wide] + list(edge) + list(ghosts)
    return call(body, outs, ins, 4 * s.x * s.y * s.k, {0: 0})


def halved(s, nz):
    return nz == 1 and s.x % 2 == 0


def one_way(faces, s, nz):
    got = []
    for face, axis in zip(faces, ("gx", "gy", "gz")):
        pairs = [(i, i - 1) for i in range(1, lax.axis_size(axis))]
        if axis == "gz" and halved(s, nz):
            pairs = [(0, 1), (1, 0)]
        got.append(lax.ppermute(face, axis, pairs))
    return got


def exchange(faces, axes):
    got = []
    for face, (axis, first) in zip(faces, axes):
        count = lax.axis_size(axis)
        pairs = []
        for i in range(first, count - 1, 2):
            pairs += [(i, i + 1), (i + 1, i)]
        got.append(lax.ppermute(face, axis, pairs))
    return got


def transposed_dot(left, right):
    return lax.dot_general(
        left, right, (((0,), (0,)), ((), ())), preferred_element_type=jnp.float32
    )


def two(value):
    high = value.astype(BF)
    low = (value - high.astype(jnp.float32)).astype(BF)
    return jnp.concatenate([high, low], axis=1)


def both(full):
    k = full.shape[0] // 2
    return full[:k, :k] + (full[:k, k:] + full[k:, :k]) + full[k:, k:]


def gather_terms(w, wide, s):
    rows = s.cells // 4

    def body(w_ref, k_ref, f_ref, g_ref, m_ref, q_ref):
        def emit(here, c, near):
            return c - near * (1.0 / 6.0)

        sweep(s, w_ref, q_ref, emit)
        sums = jnp.zeros((2 * s.k, 4 * s.k), jnp.float32)
        for i in range(s.cells // rows):
            here = pl.ds(i * rows, rows)
            k = k_ref[here, :]
            inverse = lax.rsqrt(k)
            pair = two(w_ref[here, :] * inverse)
            f_ref[here, :] = pair
            image = two((k * inverse) * q_ref[here, :])
            sums += transposed_dot(pair, jnp.concatenate([pair, image], axis=1))
        g_ref[...] = both(sums[:, : 2 * s.k])
        m_ref[...] = both(sums[:, 2 * s.k :])

    outs = [jax.ShapeDtypeStruct((s.cells, 2 * s.k), BF), f32(s.k, s.k), f32(s.k, s.k)]
    moved = 4 * 4 * s.cells * s.k
    return pl.pallas_call(
        body,
        out_shape=outs,
        in_specs=[VMEM, VMEM],
        out_specs=(VMEM, VMEM, VMEM),
        scratch_shapes=[pltpu.VMEM((s.cells, s.k), jnp.float32)],
        compiler_params=pltpu.CompilerParams(vmem_limit_bytes=32 * 1024 * 1024),
        cost_estimate=pl.CostEstimate(
            flops=16 * s.cells * s.k * s.k, bytes_accessed=moved, transcendentals=0
        ),
    )(w, wide)


def pack_terms(gram, own, w, ghosts, s, nz, cells):
    k = s.k

    def body(g_ref, m_ref, w_ref, x_ref, y_ref, z_ref, mine_ref, other_ref):
        at_ref = places(s)
        lefts = [w_ref[s.cells - s.row : s.cells, :]]
        tops = [w_ref[(x + 1) * s.row - s.z : (x + 1) * s.row, :] for x in range(s.x)]
        lefts.append(jnp.concatenate(tops, axis=0))
        if halved(s, nz):
            start = at_ref[6] * (s.cells // 2) + at_ref[4]
            lefts.append(w_ref[pl.ds(start, s.x * s.y // 2, stride=s.z), :])
        else:
            lefts.append(w_ref[pl.ds(s.z - 1, s.x * s.y, stride=s.z), :])
        left = jnp.concatenate(lefts, axis=0)
        right = jnp.concatenate([x_ref[...], y_ref[...], z_ref[...]], axis=0)
        m = m_ref[...] - both(transposed_dot(two(left), two(right))) * (2.0 / 6.0)
        raw = (m + m.T) * (0.5 / cells)
        below = lax.broadcasted_iota(jnp.int32, (k, k), 0)
        along = lax.broadcasted_iota(jnp.int32, (k, k), 1)
        full = jnp.where(below >= along, g_ref[...] * (1.0 / cells), raw)
        diagonal = jnp.sum(jnp.where(below == along, raw, 0.0), axis=0, keepdims=True)
        even = at_ref[7] == 0
        for ref, first in ((mine_ref, even), (other_ref, jnp.logical_not(even))):
            ref[: k // 2, :] = jnp.where(first, full[: k // 2, :], full[k // 2 :, :])
            ref[k // 2 :, :] = jnp.broadcast_to(diagonal, (8, k))

    ins = [gram, own, w] + list(ghosts)
    return call(body, [f32(k // 2 + 8, k)] * 2, ins, 6 * s.cells * k)


def total(mine, other):
    axes = ("gx", "gy", "gz")
    sizes = [lax.axis_size(a) for a in axes]

    def swap(value, flip):
        pairs = []
        for i in range(sizes[0] * sizes[1] * sizes[2]):
            x, y, z = i // (sizes[1] * sizes[2]), i // sizes[2] % sizes[1], i % sizes[2]
            x, y, z = x ^ flip[0], y ^ flip[1], z ^ flip[2]
            pairs.append((i, (x * sizes[1] + y) * sizes[2] + z))
        return lax.ppermute(value, axes, pairs)

    hops = []
    for d, first in ((1, 2), (2, 1), (0, 1)):
        bit = first
        while bit < sizes[d]:
            hops.append(tuple(bit if e == d else 0 for e in range(3)))
            bit *= 2
    pair = (0, 1, 0)
    value = mine + swap(other, pair)
    while hops:
        a, *hops = hops
        if hops:
            b, *hops = hops
            c = tuple(i ^ j for i, j in zip(a, b))
            value = (value + swap(value, a)) + (swap(value, b) + swap(value, c))
        else:
            value = value + swap(value, a)
    return value, swap(value, pair)


PANEL = 32
GROUP = 16


def eliminate(m_ref, n):
    place = lax.broadcasted_iota(jnp.int32, (PANEL, n), 0)
    for top in range(0, n, PANEL):
        left, right = m_ref[top : top + PANEL, :n], m_ref[top : top + PANEL, n:]
        for first in range(0, PANEL, GROUP):
            columns = [
                jnp.broadcast_to(left[:, top + k : top + k + 1], (PANEL, n))
                for k in range(first, first + GROUP)
            ]
            for i in range(GROUP):
                k = first + i
                pivot = columns[i][k : k + 1, :]
                inverse = 1.0 / pivot
                root = lax.rsqrt(pivot)
                below = jnp.where(place > k, columns[i], 0.0)
                for t in range(i + 1, GROUP):
                    columns[t] = columns[t] - below * (columns[t][k : k + 1, :] * inverse)
                here = place == k
                one, two_ = left[k : k + 1, :], right[k : k + 1, :]
                left = jnp.where(here, one * root, left - below * (one * inverse))
                right = jnp.where(here, two_ * root, right - below * (two_ * inverse))
        m_ref[top : top + PANEL, :n] = left
        m_ref[top : top + PANEL, n:] = right
        if top + PANEL < n:
            both_sides = jnp.concatenate([left, right], axis=1)
            update = lax.dot_general(
                left, both_sides, (((0,), (0,)), ((), ())),
                precision=HIGH, preferred_element_type=jnp.float32,
            )
            m_ref[top + PANEL :, :] = m_ref[top + PANEL :, :] - update[top + PANEL :, :]


def orthonormal(own, got, filtered, s):
    k = s.k
    parts = 4
    rows = s.cells // parts

    def body(own_ref, got_ref, f_ref, b_hbm, o_ref, m_ref, b_ref, sems):
        even = places(s)[7] == 0
        one, other = own_ref[: k // 2, :], got_ref[: k // 2, :]
        upper = jnp.concatenate(
            [jnp.where(even, one, other), jnp.where(even, other, one)], axis=0
        )
        low, high = own_ref[k // 2 : k // 2 + 1, :], got_ref[k // 2 : k // 2 + 1, :]
        turned = upper.T
        below = lax.broadcasted_iota(jnp.int32, (k, k), 0)
        along = lax.broadcasted_iota(jnp.int32, (k, k), 1)
        m_ref[:, :k] = jnp.where(below >= along, upper, turned)
        m_ref[:, k:] = jnp.where(below == along, 1.0, 0.0)
        eliminate(m_ref, k)
        inverse = m_ref[:, k:]
        pair = two(inverse.T)
        pair = jnp.concatenate([pair, pair], axis=0)
        copies = []
        for i in range(parts):
            here = pl.ds(i * rows, rows)
            out = jnp.dot(f_ref[here, :], pair, preferred_element_type=jnp.float32)
            b_ref[here, :] = out[:, :k] + out[:, k:]
            copies.append(pltpu.make_async_copy(b_ref.at[here], b_hbm.at[here], sems.at[i]))
            copies[-1].start()
        raw = jnp.where(below < along, upper, turned)
        raw = jnp.where(below == along, jnp.where(even, low, high), raw)
        half = jnp.dot(inverse, raw, precision=HIGH, preferred_element_type=jnp.float32)
        o_ref[...] = lax.dot_general(
            half, inverse, (((1,), (1,)), ((), ())),
            precision=HIGH, preferred_element_type=jnp.float32,
        )
        for copy in copies:
            copy.wait()

    return pl.pallas_call(
        body,
        out_shape=[f32(s.cells, k), f32(k, k)],
        in_specs=[VMEM, VMEM, VMEM],
        out_specs=(pl.BlockSpec(memory_space=pl.ANY), VMEM),
        scratch_shapes=[
            pltpu.VMEM((k, 2 * k), jnp.float32),
            pltpu.VMEM((s.cells, k), jnp.float32),
            pltpu.SemaphoreType.DMA((parts,)),
        ],
        compiler_params=pltpu.CompilerParams(vmem_limit_bytes=32 * 1024 * 1024),
        cost_estimate=pl.CostEstimate(
            flops=8 * s.cells * k * k, bytes_accessed=8 * s.cells * k, transcendentals=0
        ),
    )(own, got, filtered)


def on_device(block, conductivity):
    s = Shape(block.shape)
    sizes = [lax.axis_size(a) for a in ("gx", "gy", "gz")]
    nz = 1 if sizes[2] == 2 else 2
    cells = float(s.cells * sizes[0] * sizes[1] * sizes[2])
    axes = [("gx", 0), ("gx", 1), ("gy", 0), ("gy", 1), ("gz", 0), ("gz", 1)][: 4 + nz]

    flat = block.reshape(s.cells, s.k)
    turned = jnp.transpose(conductivity, (1, 2, 0))
    w, wide, *rest = prepare(flat, turned, s, nz)
    faces, edge = rest[: 4 + nz], rest[4 + nz :]
    before = None
    for step in range(DEG):
        ghosts = exchange(faces, axes)
        part = interior(w, before, wide, s)
        scale = (1.0 if before is None else 2.0) / half_value
        before = w
        w, *faces = finish(part, wide, edge, ghosts, s, nz, scale, step == DEG - 1)
    ghosts = one_way(faces, s, nz)
    filtered, gram, own = gather_terms(w, wide, s)
    halves = total(*pack_terms(gram, own, w, ghosts, s, nz, cells))
    basis, projected = orthonormal(*halves, filtered, s)
    return (basis.reshape(block.shape), projected)


def solution(mesh):
    return jax.shard_map(
        on_device,
        mesh=mesh,
        in_specs=(P("gx", "gy", "gz", None), P("gx", "gy", "gz")),
        out_specs=(P("gx", "gy", "gz", None), P()),
        check_vma=False,
    )
```

```python
import functools
import jax
import jax.numpy as jnp
from jax import lax
from jax.experimental import pallas as pl
from jax.experimental.pallas import tpu as pltpu
from jax.sharding import PartitionSpec as P

DEG = 4

HIGH = lax.Precision.HIGHEST
center_value = 3.25
half_value = 2.75
VMEM = pl.BlockSpec(memory_space=pltpu.VMEM)
BF = jnp.bfloat16


def call(body, outs, ins, flops, aliases=None):
    moved = sum(4 * a.size for a in list(outs) + list(ins))
    return pl.pallas_call(
        body,
        out_shape=outs,
        in_specs=[VMEM] * len(ins),
        out_specs=tuple(VMEM for _ in outs),
        input_output_aliases=aliases or {},
        compiler_params=pltpu.CompilerParams(vmem_limit_bytes=32 * 1024 * 1024),
        cost_estimate=pl.CostEstimate(flops=flops, bytes_accessed=moved, transcendentals=0),
    )(*ins)


def f32(rows, width):
    return jax.ShapeDtypeStruct((rows, width), jnp.float32)


class Shape:
    def __init__(self, shape):
        self.x, self.y, self.z, self.k = shape
        self.row = self.y * self.z
        self.cells = self.x * self.row
        self.room = self.cells + self.z


def places(s):
    odd = [lax.rem(lax.axis_index(a), 2) for a in ("gx", "gy", "gz")]
    tops = (s.x - 1, s.y - 1, s.z - 1)
    at = [jnp.where(odd[d] == first, tops[d], 0) for d in range(3) for first in range(2)]
    return at + [odd[2], odd[1]]


def faces_of(s, at, w_ref, out, with_z=True):
    if with_z:
        for i in range(out["nz"]):
            out["z"][i][...] = w_ref[pl.ds(at[4 + i], s.x * s.y, stride=s.z), :]
    for i in range(2):
        out["x"][i][...] = w_ref[pl.ds(at[i] * s.row, s.row), :]
        for x in range(s.x):
            out["y"][i][pl.ds(x * s.z, s.z), :] = w_ref[
                pl.ds(x * s.row + at[2 + i] * s.z, s.z), :
            ]


def face_shapes(s, nz):
    return (
        [f32(s.row, s.k)] * 2 + [f32(s.x * s.z, s.k)] * 2 + [f32(s.x * s.y, s.k)] * nz
    )


def split_faces(refs, nz):
    return {"x": refs[0:2], "y": refs[2:4], "z": refs[4 : 4 + nz], "nz": nz}


def prepare(block, turned, s, nz):
    parts = 4
    each = s.x // parts

    def body(k_ref, *all_refs):
        b_refs, (w_ref, wide_ref, *refs) = all_refs[:parts], all_refs[parts:]
        at_ref = places(s)
        for y in range(s.y):
            tile = k_ref[y]
            for x in range(s.x):
                here = pl.ds(x * s.row + y * s.z, s.z)
                k = jnp.broadcast_to(tile[:, x : x + 1], (s.z, s.k))
                wide_ref[here, :] = k
                b = b_refs[x // each][(x % each) * s.row + y * s.z : (x % each) * s.row + (y + 1) * s.z, :]
                w_ref[here, :] = jnp.sqrt(k) * b
        for i in range(nz):
            refs[4 + nz + i][...] = wide_ref[pl.ds(at_ref[4 + i], s.x * s.y, stride=s.z), :]
        faces_of(s, at_ref, w_ref, split_faces(refs, nz))

    outs = [f32(s.room, s.k)] * 2 + face_shapes(s, nz) + [f32(s.x * s.y, s.k)] * nz
    slices = [block[i * each * s.row : (i + 1) * each * s.row] for i in range(parts)]
    return call(body, outs, [turned] + slices, 4 * s.cells * s.k)


def around(s, w_ref, o_ref, x, low, high, emit):
    base = pl.multiple_of(x * s.row, s.row)
    place = lax.broadcasted_iota(jnp.int32, (s.z, s.k), 0)
    tiles = [w_ref[pl.ds(base + y * s.z, s.z), :] for y in range(s.y)]
    done = []
    for y in range(s.y):
        c = tiles[y]
        up = jnp.where(place == s.z - 1, 0.0, pltpu.roll(c, s.z - 1, 0))
        down = jnp.where(place == 0, 0.0, pltpu.roll(c, 1, 0))
        near = up + down
        if y > 0:
            near = near + tiles[y - 1]
        if y < s.y - 1:
            near = near + tiles[y + 1]
        if low:
            near = near + w_ref[pl.ds(base - s.row + y * s.z, s.z), :]
        if high:
            near = near + w_ref[pl.ds(base + s.row + y * s.z, s.z), :]
        here = pl.ds(base + y * s.z, s.z)
        done.append((here, emit(here, c, near)))
    for here, new in done:
        o_ref[here, :] = new


def sweep(s, w_ref, o_ref, emit):
    around(s, w_ref, o_ref, 0, False, True, emit)

    def step(x, _):
        around(s, w_ref, o_ref, x, True, True, emit)
        return 0

    lax.fori_loop(1, s.x - 1, step, 0, unroll=2)
    around(s, w_ref, o_ref, s.x - 1, True, False, emit)


def interior(w, before, wide, s):
    scale = (1.0 if before is None else 2.0) / half_value

    def body(w_ref, k_ref, *rest):
        o_ref = rest[-1]

        def emit(here, c, near):
            new = k_ref[here, :] * ((c - near * (1.0 / 6.0)) * scale) - (scale * center_value) * c
            if before is not None:
                new = new - rest[0][here, :]
            return new

        sweep(s, w_ref, o_ref, emit)

    ins = [w, wide] + ([] if before is None else [before])
    return call(body, [f32(s.room, s.k)], ins, 12 * s.cells * s.k)[0]


def finish(part, wide, edge, ghosts, s, nz, scale, last):
    def body(p_ref, k_ref, *refs):
        del p_ref
        at_ref = places(s)
        edges = refs[:nz]
        ghost = split_faces(refs[nz : 4 + 2 * nz], nz)
        w_ref = refs[4 + 2 * nz]
        if last:
            out = refs[5 + 2 * nz :]
        else:
            out = split_faces(refs[5 + 2 * nz :], nz)
        factor = scale / 6.0
        for i in range(2):
            here = pl.ds(at_ref[i] * s.row, s.row)
            w_ref[here, :] = w_ref[here, :] - (k_ref[here, :] * factor) * ghost["x"][i][...]
            done = []
            for x in range(s.x):
                here = pl.ds(x * s.row + at_ref[2 + i] * s.z, s.z)
                g = ghost["y"][i][pl.ds(x * s.z, s.z), :]
                done.append((here, w_ref[here, :] - (k_ref[here, :] * factor) * g))
            for here, new in done:
                w_ref[here, :] = new
        for i in range(nz):
            for first in range(0, s.x, 8):
                done = []
                for x in range(first, min(first + 8, s.x)):
                    here = pl.ds(x * s.row + at_ref[4 + i], s.y, stride=s.z)
                    flat = pl.ds(x * s.y, s.y)
                    new = w_ref[here, :] - (edges[i][flat, :] * factor) * ghost["z"][i][flat, :]
                    done.append((here, flat, new))
                for here, flat, new in done:
                    w_ref[here, :] = new
                    if not last:
                        out["z"][i][flat, :] = new
        if last:
            out[0][...] = w_ref[: s.row, :]
        else:
            faces_of(s, at_ref, w_ref, out, with_z=False)

    if last:
        outs = [f32(s.room, s.k), f32(s.row, s.k)]
    else:
        outs = [f32(s.room, s.k)] + face_shapes(s, nz)
    ins = [part, wide] + list(edge) + list(ghosts)
    return call(body, outs, ins, 4 * s.x * s.y * s.k, {0: 0})


def last_faces(w, s, nz):
    def body(w_ref, *out):
        at_ref = places(s)
        for x in range(s.x):
            out[0][x * s.z : (x + 1) * s.z, :] = w_ref[x * s.row : x * s.row + s.z, :]
        if halved(s, nz):
            start = (1 - at_ref[6]) * (s.cells // 2) + at_ref[4]
            out[1][...] = w_ref[pl.ds(start, s.x * s.y // 2, stride=s.z), :]
        else:
            out[1][...] = w_ref[pl.ds(0, s.x * s.y, stride=s.z), :]

    outs = [f32(s.x * s.z, s.k), f32(s.x * s.y // (2 if halved(s, nz) else 1), s.k)]
    return list(call(body, outs, [w], s.x * s.y * s.k))


def halved(s, nz):
    return nz == 1 and s.x % 2 == 0


def one_way(faces, s, nz):
    got = []
    for face, axis in zip(faces, ("gx", "gy", "gz")):
        pairs = [(i, i - 1) for i in range(1, lax.axis_size(axis))]
        if axis == "gz" and halved(s, nz):
            pairs = [(0, 1), (1, 0)]
        got.append(lax.ppermute(face, axis, pairs))
    return got


def exchange(faces, axes):
    got = []
    for face, (axis, first) in zip(faces, axes):
        count = lax.axis_size(axis)
        pairs = []
        for i in range(first, count - 1, 2):
            pairs += [(i, i + 1), (i + 1, i)]
        got.append(lax.ppermute(face, axis, pairs))
    return got


def transposed_dot(left, right):
    return lax.dot_general(
        left, right, (((0,), (0,)), ((), ())), preferred_element_type=jnp.float32
    )


def two(value):
    high = value.astype(BF)
    low = (value - high.astype(jnp.float32)).astype(BF)
    return jnp.concatenate([high, low], axis=1)


def both(full):
    k = full.shape[0] // 2
    return full[:k, :k] + (full[:k, k:] + full[k:, :k]) + full[k:, k:]


def gather_terms(w, wide, s):
    rows = s.cells // 4

    def body(w_ref, k_ref, f_ref, g_ref, m_ref, q_ref):
        def emit(here, c, near):
            return c - near * (1.0 / 6.0)

        sweep(s, w_ref, q_ref, emit)
        sums = jnp.zeros((2 * s.k, 4 * s.k), jnp.float32)
        for i in range(s.cells // rows):
            here = pl.ds(i * rows, rows)
            k = k_ref[here, :]
            inverse = lax.rsqrt(k)
            pair = two(w_ref[here, :] * inverse)
            f_ref[here, :] = pair
            image = two((k * inverse) * q_ref[here, :])
            sums += transposed_dot(pair, jnp.concatenate([pair, image], axis=1))
        g_ref[...] = both(sums[:, : 2 * s.k])
        m_ref[...] = both(sums[:, 2 * s.k :])

    outs = [jax.ShapeDtypeStruct((s.cells, 2 * s.k), BF), f32(s.k, s.k), f32(s.k, s.k)]
    moved = 4 * 4 * s.cells * s.k
    return pl.pallas_call(
        body,
        out_shape=outs,
        in_specs=[VMEM, VMEM],
        out_specs=(VMEM, VMEM, VMEM),
        scratch_shapes=[pltpu.VMEM((s.cells, s.k), jnp.float32)],
        compiler_params=pltpu.CompilerParams(vmem_limit_bytes=32 * 1024 * 1024),
        cost_estimate=pl.CostEstimate(
            flops=16 * s.cells * s.k * s.k, bytes_accessed=moved, transcendentals=0
        ),
    )(w, wide)


def pack_terms(gram, own, w, ghosts, s, nz, cells):
    k = s.k

    def body(g_ref, m_ref, w_ref, x_ref, y_ref, z_ref, mine_ref, other_ref):
        at_ref = places(s)
        lefts = [w_ref[s.cells - s.row : s.cells, :]]
        tops = [w_ref[(x + 1) * s.row - s.z : (x + 1) * s.row, :] for x in range(s.x)]
        lefts.append(jnp.concatenate(tops, axis=0))
        if halved(s, nz):
            start = at_ref[6] * (s.cells // 2) + at_ref[4]
            lefts.append(w_ref[pl.ds(start, s.x * s.y // 2, stride=s.z), :])
        else:
            lefts.append(w_ref[pl.ds(s.z - 1, s.x * s.y, stride=s.z), :])
        left = jnp.concatenate(lefts, axis=0)
        right = jnp.concatenate([x_ref[...], y_ref[...], z_ref[...]], axis=0)
        m = m_ref[...] - both(transposed_dot(two(left), two(right))) * (2.0 / 6.0)
        raw = (m + m.T) * (0.5 / cells)
        below = lax.broadcasted_iota(jnp.int32, (k, k), 0)
        along = lax.broadcasted_iota(jnp.int32, (k, k), 1)
        full = jnp.where(below >= along, g_ref[...] * (1.0 / cells), raw)
        diagonal = jnp.sum(jnp.where(below == along, raw, 0.0), axis=0, keepdims=True)
        even = at_ref[7] == 0
        for ref, first in ((mine_ref, even), (other_ref, jnp.logical_not(even))):
            ref[: k // 2, :] = jnp.where(first, full[: k // 2, :], full[k // 2 :, :])
            ref[k // 2 :, :] = jnp.broadcast_to(diagonal, (8, k))

    ins = [gram, own, w] + list(ghosts)
    return call(body, [f32(k // 2 + 8, k)] * 2, ins, 6 * s.cells * k)


def total(mine, other):
    axes = ("gx", "gy", "gz")
    sizes = [lax.axis_size(a) for a in axes]

    def swap(value, flip):
        pairs = []
        for i in range(sizes[0] * sizes[1] * sizes[2]):
            x, y, z = i // (sizes[1] * sizes[2]), i // sizes[2] % sizes[1], i % sizes[2]
            x, y, z = x ^ flip[0], y ^ flip[1], z ^ flip[2]
            pairs.append((i, (x * sizes[1] + y) * sizes[2] + z))
        return lax.ppermute(value, axes, pairs)

    hops = []
    for d, first in ((1, 2), (2, 1), (0, 1)):
        bit = first
        while bit < sizes[d]:
            hops.append(tuple(bit if e == d else 0 for e in range(3)))
            bit *= 2
    pair = (0, 1, 0)
    value = mine + swap(other, pair)
    while hops:
        a, *hops = hops
        if hops:
            b, *hops = hops
            c = tuple(i ^ j for i, j in zip(a, b))
            value = (value + swap(value, a)) + (swap(value, b) + swap(value, c))
        else:
            value = value + swap(value, a)
    return value, swap(value, pair)


PANEL = 64
GROUP = 16


def eliminate(m_ref, n):
    place = lax.broadcasted_iota(jnp.int32, (PANEL, n), 0)
    for top in range(0, n, PANEL):
        left, right = m_ref[top : top + PANEL, :n], m_ref[top : top + PANEL, n:]
        for first in range(0, PANEL, GROUP):
            columns = [
                jnp.broadcast_to(left[:, top + k : top + k + 1], (PANEL, n))
                for k in range(first, first + GROUP)
            ]
            for i in range(GROUP):
                k = first + i
                pivot = columns[i][k : k + 1, :]
                inverse = 1.0 / pivot
                root = lax.rsqrt(pivot)
                below = jnp.where(place > k, columns[i], 0.0)
                for t in range(i + 1, GROUP):
                    columns[t] = columns[t] - below * (columns[t][k : k + 1, :] * inverse)
                here = place == k
                one, two_ = left[k : k + 1, :], right[k : k + 1, :]
                left = jnp.where(here, one * root, left - below * (one * inverse))
                right = jnp.where(here, two_ * root, right - below * (two_ * inverse))
        m_ref[top : top + PANEL, :n] = left
        m_ref[top : top + PANEL, n:] = right
        if top + PANEL < n:
            both_sides = jnp.concatenate([left, right], axis=1)
            update = lax.dot_general(
                left, both_sides, (((0,), (0,)), ((), ())),
                precision=HIGH, preferred_element_type=jnp.float32,
            )
            m_ref[top + PANEL :, :] = m_ref[top + PANEL :, :] - update[top + PANEL :, :]


def orthonormal(own, got, filtered, s):
    k = s.k
    parts = 8
    rows = s.cells // parts

    def body(own_ref, got_ref, f_ref, b_hbm, o_ref, m_ref, b_ref, sems):
        even = places(s)[7] == 0
        one, other = own_ref[: k // 2, :], got_ref[: k // 2, :]
        upper = jnp.concatenate(
            [jnp.where(even, one, other), jnp.where(even, other, one)], axis=0
        )
        low, high = own_ref[k // 2 : k // 2 + 1, :], got_ref[k // 2 : k // 2 + 1, :]
        turned = upper.T
        below = lax.broadcasted_iota(jnp.int32, (k, k), 0)
        along = lax.broadcasted_iota(jnp.int32, (k, k), 1)
        m_ref[:, :k] = jnp.where(below >= along, upper, turned)
        m_ref[:, k:] = jnp.where(below == along, 1.0, 0.0)
        eliminate(m_ref, k)
        inverse = m_ref[:, k:]
        pair = two(inverse.T)
        pair = jnp.concatenate([pair, pair], axis=0)
        copies = []
        for i in range(parts):
            here = pl.ds(i * rows, rows)
            out = jnp.dot(f_ref[here, :], pair, preferred_element_type=jnp.float32)
            b_ref[here, :] = out[:, :k] + out[:, k:]
            copies.append(pltpu.make_async_copy(b_ref.at[here], b_hbm.at[here], sems.at[i]))
            copies[-1].start()
        raw = jnp.where(below < along, upper, turned)
        raw = jnp.where(below == along, jnp.where(even, low, high), raw)
        half = jnp.dot(inverse, raw, precision=HIGH, preferred_element_type=jnp.float32)
        o_ref[...] = lax.dot_general(
            half, inverse, (((1,), (1,)), ((), ())),
            precision=HIGH, preferred_element_type=jnp.float32,
        )
        for copy in copies:
            copy.wait()

    return pl.pallas_call(
        body,
        out_shape=[f32(s.cells, k), f32(k, k)],
        in_specs=[VMEM, VMEM, VMEM],
        out_specs=(pl.BlockSpec(memory_space=pl.ANY), VMEM),
        scratch_shapes=[
            pltpu.VMEM((k, 2 * k), jnp.float32),
            pltpu.VMEM((s.cells, k), jnp.float32),
            pltpu.SemaphoreType.DMA((parts,)),
        ],
        compiler_params=pltpu.CompilerParams(vmem_limit_bytes=32 * 1024 * 1024),
        cost_estimate=pl.CostEstimate(
            flops=8 * s.cells * k * k, bytes_accessed=8 * s.cells * k, transcendentals=0
        ),
    )(own, got, filtered)


def on_device(block, conductivity):
    s = Shape(block.shape)
    sizes = [lax.axis_size(a) for a in ("gx", "gy", "gz")]
    nz = 1 if sizes[2] == 2 else 2
    cells = float(s.cells * sizes[0] * sizes[1] * sizes[2])
    axes = [("gx", 0), ("gx", 1), ("gy", 0), ("gy", 1), ("gz", 0), ("gz", 1)][: 4 + nz]

    flat = block.reshape(s.cells, s.k)
    turned = jnp.transpose(conductivity, (1, 2, 0))
    w, wide, *rest = prepare(flat, turned, s, nz)
    faces, edge = rest[: 4 + nz], rest[4 + nz :]
    before = None
    for step in range(DEG):
        ghosts = exchange(faces, axes)
        part = interior(w, before, wide, s)
        scale = (1.0 if before is None else 2.0) / half_value
        before = w
        w, *faces = finish(part, wide, edge, ghosts, s, nz, scale, step == DEG - 1)
    ghosts = one_way(faces + last_faces(w, s, nz), s, nz)
    filtered, gram, own = gather_terms(w, wide, s)
    halves = total(*pack_terms(gram, own, w, ghosts, s, nz, cells))
    basis, projected = orthonormal(*halves, filtered, s)
    return (basis.reshape(block.shape), projected)


def solution(mesh):
    return jax.shard_map(
        on_device,
        mesh=mesh,
        in_specs=(P("gx", "gy", "gz", None), P("gx", "gy", "gz")),
        out_specs=(P("gx", "gy", "gz", None), P()),
        check_vma=False,
    )
```

```python
import functools
import jax
import jax.numpy as jnp
from jax import lax
from jax.experimental import pallas as pl
from jax.experimental.pallas import tpu as pltpu
from jax.sharding import PartitionSpec as P

DEG = 4

HIGH = lax.Precision.HIGHEST
center_value = 3.25
half_value = 2.75
VMEM = pl.BlockSpec(memory_space=pltpu.VMEM)
BF = jnp.bfloat16


def call(body, outs, ins, flops, aliases=None):
    moved = sum(4 * a.size for a in list(outs) + list(ins))
    return pl.pallas_call(
        body,
        out_shape=outs,
        in_specs=[VMEM] * len(ins),
        out_specs=tuple(VMEM for _ in outs),
        input_output_aliases=aliases or {},
        compiler_params=pltpu.CompilerParams(vmem_limit_bytes=32 * 1024 * 1024),
        cost_estimate=pl.CostEstimate(flops=flops, bytes_accessed=moved, transcendentals=0),
    )(*ins)


def f32(rows, width):
    return jax.ShapeDtypeStruct((rows, width), jnp.float32)


class Shape:
    def __init__(self, shape):
        self.x, self.y, self.z, self.k = shape
        self.row = self.y * self.z
        self.cells = self.x * self.row
        self.room = self.cells + self.z


def places(s):
    odd = [lax.rem(lax.axis_index(a), 2) for a in ("gx", "gy", "gz")]
    tops = (s.x - 1, s.y - 1, s.z - 1)
    at = [jnp.where(odd[d] == first, tops[d], 0) for d in range(3) for first in range(2)]
    return at + [odd[2], odd[1]]


def faces_of(s, at, w_ref, out, with_z=True):
    if with_z:
        for i in range(out["nz"]):
            out["z"][i][...] = w_ref[pl.ds(at[4 + i], s.x * s.y, stride=s.z), :]
    for i in range(2):
        out["x"][i][...] = w_ref[pl.ds(at[i] * s.row, s.row), :]
        for x in range(s.x):
            out["y"][i][pl.ds(x * s.z, s.z), :] = w_ref[
                pl.ds(x * s.row + at[2 + i] * s.z, s.z), :
            ]


def face_shapes(s, nz):
    return (
        [f32(s.row, s.k)] * 2 + [f32(s.x * s.z, s.k)] * 2 + [f32(s.x * s.y, s.k)] * nz
    )


def split_faces(refs, nz):
    return {"x": refs[0:2], "y": refs[2:4], "z": refs[4 : 4 + nz], "nz": nz}


def prepare(block, turned, s, nz):
    parts = 4
    each = s.x // parts

    def body(k_ref, *all_refs):
        b_refs, (w_ref, wide_ref, *refs) = all_refs[:parts], all_refs[parts:]
        at_ref = places(s)
        for y in range(s.y):
            tile = k_ref[y]
            for x in range(s.x):
                here = pl.ds(x * s.row + y * s.z, s.z)
                k = jnp.broadcast_to(tile[:, x : x + 1], (s.z, s.k))
                wide_ref[here, :] = k
                b = b_refs[x // each][(x % each) * s.row + y * s.z : (x % each) * s.row + (y + 1) * s.z, :]
                w_ref[here, :] = jnp.sqrt(k) * b
        for i in range(nz):
            refs[4 + nz + i][...] = wide_ref[pl.ds(at_ref[4 + i], s.x * s.y, stride=s.z), :]
        faces_of(s, at_ref, w_ref, split_faces(refs, nz))

    outs = [f32(s.room, s.k)] * 2 + face_shapes(s, nz) + [f32(s.x * s.y, s.k)] * nz
    slices = [block[i * each * s.row : (i + 1) * each * s.row] for i in range(parts)]
    return call(body, outs, [turned] + slices, 4 * s.cells * s.k)


def around(s, w_ref, o_ref, x, low, high, emit):
    base = pl.multiple_of(x * s.row, s.row)
    place = lax.broadcasted_iota(jnp.int32, (s.z, s.k), 0)
    tiles = [w_ref[pl.ds(base + y * s.z, s.z), :] for y in range(s.y)]
    done = []
    for y in range(s.y):
        c = tiles[y]
        up = jnp.where(place == s.z - 1, 0.0, pltpu.roll(c, s.z - 1, 0))
        down = jnp.where(place == 0, 0.0, pltpu.roll(c, 1, 0))
        near = up + down
        if y > 0:
            near = near + tiles[y - 1]
        if y < s.y - 1:
            near = near + tiles[y + 1]
        if low:
            near = near + w_ref[pl.ds(base - s.row + y * s.z, s.z), :]
        if high:
            near = near + w_ref[pl.ds(base + s.row + y * s.z, s.z), :]
        here = pl.ds(base + y * s.z, s.z)
        done.append((here, emit(here, c, near)))
    for here, new in done:
        o_ref[here, :] = new


def sweep(s, w_ref, o_ref, emit):
    around(s, w_ref, o_ref, 0, False, True, emit)

    def step(x, _):
        around(s, w_ref, o_ref, x, True, True, emit)
        return 0

    lax.fori_loop(1, s.x - 1, step, 0, unroll=2)
    around(s, w_ref, o_ref, s.x - 1, True, False, emit)


def interior(w, before, wide, s):
    scale = (1.0 if before is None else 2.0) / half_value

    def body(w_ref, k_ref, *rest):
        o_ref = rest[-1]

        def emit(here, c, near):
            new = k_ref[here, :] * ((c - near * (1.0 / 6.0)) * scale) - (scale * center_value) * c
            if before is not None:
                new = new - rest[0][here, :]
            return new

        sweep(s, w_ref, o_ref, emit)

    ins = [w, wide] + ([] if before is None else [before])
    return call(body, [f32(s.room, s.k)], ins, 12 * s.cells * s.k)[0]


def finish(part, wide, edge, ghosts, s, nz, scale, last):
    def body(p_ref, k_ref, *refs):
        del p_ref
        at_ref = places(s)
        edges = refs[:nz]
        ghost = split_faces(refs[nz : 4 + 2 * nz], nz)
        w_ref = refs[4 + 2 * nz]
        out = split_faces(refs[5 + 2 * nz :], nz)
        half = last and halved(s, nz)
        factor = scale / 6.0
        for i in range(2):
            here = pl.ds(at_ref[i] * s.row, s.row)
            w_ref[here, :] = w_ref[here, :] - (k_ref[here, :] * factor) * ghost["x"][i][...]
            done = []
            for x in range(s.x):
                here = pl.ds(x * s.row + at_ref[2 + i] * s.z, s.z)
                g = ghost["y"][i][pl.ds(x * s.z, s.z), :]
                done.append((here, w_ref[here, :] - (k_ref[here, :] * factor) * g))
            for here, new in done:
                w_ref[here, :] = new
        for i in range(nz):
            for first in range(0, s.x, 8):
                done = []
                for x in range(first, min(first + 8, s.x)):
                    here = pl.ds(x * s.row + at_ref[4 + i], s.y, stride=s.z)
                    flat = pl.ds(x * s.y, s.y)
                    new = w_ref[here, :] - (edges[i][flat, :] * factor) * ghost["z"][i][flat, :]
                    done.append((here, flat, new))
                for here, flat, new in done:
                    w_ref[here, :] = new
                    if not half:
                        out["z"][i][flat, :] = new
        faces_of(s, at_ref, w_ref, out, with_z=False)
        if half:
            start = (1 - at_ref[6]) * (s.cells // 2) + at_ref[4]
            out["z"][0][...] = w_ref[pl.ds(start, s.x * s.y // 2, stride=s.z), :]

    outs = [f32(s.room, s.k)] + face_shapes(s, nz)
    if last and halved(s, nz):
        outs[5] = f32(s.x * s.y // 2, s.k)
    ins = [part, wide] + list(edge) + list(ghosts)
    return call(body, outs, ins, 4 * s.x * s.y * s.k, {0: 0})


def halved(s, nz):
    return nz == 1 and s.x % 2 == 0


def exchange(faces, axes):
    got = []
    for face, (axis, first) in zip(faces, axes):
        count = lax.axis_size(axis)
        pairs = []
        for i in range(first, count - 1, 2):
            pairs += [(i, i + 1), (i + 1, i)]
        got.append(lax.ppermute(face, axis, pairs))
    return got


def transposed_dot(left, right):
    return lax.dot_general(
        left, right, (((0,), (0,)), ((), ())), preferred_element_type=jnp.float32
    )


def two(value):
    high = value.astype(BF)
    low = (value - high.astype(jnp.float32)).astype(BF)
    return jnp.concatenate([high, low], axis=1)


def both(full):
    k = full.shape[0] // 2
    return full[:k, :k] + (full[:k, k:] + full[k:, :k]) + full[k:, k:]


def gather_terms(w, wide, s):
    rows = s.cells // 4

    def body(w_ref, k_ref, f_ref, g_ref, m_ref, q_ref):
        def emit(here, c, near):
            return c - near * (1.0 / 6.0)

        sweep(s, w_ref, q_ref, emit)
        sums = jnp.zeros((2 * s.k, 4 * s.k), jnp.float32)
        for i in range(s.cells // rows):
            here = pl.ds(i * rows, rows)
            k = k_ref[here, :]
            inverse = lax.rsqrt(k)
            pair = two(w_ref[here, :] * inverse)
            f_ref[here, :] = pair
            image = two((k * inverse) * q_ref[here, :])
            sums += transposed_dot(pair, jnp.concatenate([pair, image], axis=1))
        g_ref[...] = both(sums[:, : 2 * s.k])
        m_ref[...] = both(sums[:, 2 * s.k :])

    outs = [jax.ShapeDtypeStruct((s.cells, 2 * s.k), BF), f32(s.k, s.k), f32(s.k, s.k)]
    moved = 4 * 4 * s.cells * s.k
    return pl.pallas_call(
        body,
        out_shape=outs,
        in_specs=[VMEM, VMEM],
        out_specs=(VMEM, VMEM, VMEM),
        scratch_shapes=[pltpu.VMEM((s.cells, s.k), jnp.float32)],
        compiler_params=pltpu.CompilerParams(vmem_limit_bytes=32 * 1024 * 1024),
        cost_estimate=pl.CostEstimate(
            flops=16 * s.cells * s.k * s.k, bytes_accessed=moved, transcendentals=0
        ),
    )(w, wide)


def pack_terms(gram, own, w, ghosts, s, nz, cells):
    k = s.k

    def body(g_ref, m_ref, w_ref, *refs):
        at_ref = places(s)
        ghost = split_faces(refs[: 4 + nz], nz)
        mine_ref, other_ref = refs[4 + nz :]
        lefts = [w_ref[pl.ds(at_ref[i] * s.row, s.row), :] for i in range(2)]
        for i in range(2):
            lefts += [
                w_ref[pl.ds(x * s.row + at_ref[2 + i] * s.z, s.z), :] for x in range(s.x)
            ]
        rights = [g[...] for g in list(ghost["x"]) + list(ghost["y"])]
        if halved(s, nz):
            start = at_ref[6] * (s.cells // 2) + at_ref[4]
            lefts.append(w_ref[pl.ds(start, s.x * s.y // 2, stride=s.z), :])
            rights.append(2.0 * ghost["z"][0][...])
        else:
            for i in range(nz):
                lefts.append(w_ref[pl.ds(at_ref[4 + i], s.x * s.y, stride=s.z), :])
                rights.append(ghost["z"][i][...])
        left = jnp.concatenate(lefts, axis=0)
        right = jnp.concatenate(rights, axis=0)
        m = m_ref[...] - both(transposed_dot(two(left), two(right))) * (1.0 / 6.0)
        raw = (m + m.T) * (0.5 / cells)
        below = lax.broadcasted_iota(jnp.int32, (k, k), 0)
        along = lax.broadcasted_iota(jnp.int32, (k, k), 1)
        full = jnp.where(below >= along, g_ref[...] * (1.0 / cells), raw)
        diagonal = jnp.sum(jnp.where(below == along, raw, 0.0), axis=0, keepdims=True)
        even = at_ref[7] == 0
        for ref, first in ((mine_ref, even), (other_ref, jnp.logical_not(even))):
            ref[: k // 2, :] = jnp.where(first, full[: k // 2, :], full[k // 2 :, :])
            ref[k // 2 :, :] = jnp.broadcast_to(diagonal, (8, k))

    ins = [gram, own, w] + list(ghosts)
    return call(body, [f32(k // 2 + 8, k)] * 2, ins, 6 * s.cells * k)


def total(mine, other):
    axes = ("gx", "gy", "gz")
    sizes = [lax.axis_size(a) for a in axes]

    def swap(value, flip):
        pairs = []
        for i in range(sizes[0] * sizes[1] * sizes[2]):
            x, y, z = i // (sizes[1] * sizes[2]), i // sizes[2] % sizes[1], i % sizes[2]
            x, y, z = x ^ flip[0], y ^ flip[1], z ^ flip[2]
            pairs.append((i, (x * sizes[1] + y) * sizes[2] + z))
        return lax.ppermute(value, axes, pairs)

    hops = []
    for d, first in ((1, 2), (2, 1), (0, 1)):
        bit = first
        while bit < sizes[d]:
            hops.append(tuple(bit if e == d else 0 for e in range(3)))
            bit *= 2
    pair = (0, 1, 0)
    value = mine + swap(other, pair)
    while hops:
        a, *hops = hops
        if hops:
            b, *hops = hops
            c = tuple(i ^ j for i, j in zip(a, b))
            value = (value + swap(value, a)) + (swap(value, b) + swap(value, c))
        else:
            value = value + swap(value, a)
    return value, swap(value, pair)


PANEL = 64
GROUP = 16


def eliminate(m_ref, n):
    place = lax.broadcasted_iota(jnp.int32, (PANEL, n), 0)
    for top in range(0, n, PANEL):
        left, right = m_ref[top : top + PANEL, :n], m_ref[top : top + PANEL, n:]
        for first in range(0, PANEL, GROUP):
            columns = [
                jnp.broadcast_to(left[:, top + k : top + k + 1], (PANEL, n))
                for k in range(first, first + GROUP)
            ]
            for i in range(GROUP):
                k = first + i
                pivot = columns[i][k : k + 1, :]
                inverse = 1.0 / pivot
                root = lax.rsqrt(pivot)
                below = jnp.where(place > k, columns[i], 0.0)
                for t in range(i + 1, GROUP):
                    columns[t] = columns[t] - below * (columns[t][k : k + 1, :] * inverse)
                here = place == k
                one, two_ = left[k : k + 1, :], right[k : k + 1, :]
                left = jnp.where(here, one * root, left - below * (one * inverse))
                right = jnp.where(here, two_ * root, right - below * (two_ * inverse))
        m_ref[top : top + PANEL, :n] = left
        m_ref[top : top + PANEL, n:] = right
        if top + PANEL < n:
            both_sides = jnp.concatenate([left, right], axis=1)
            update = lax.dot_general(
                left, both_sides, (((0,), (0,)), ((), ())),
                precision=HIGH, preferred_element_type=jnp.float32,
            )
            m_ref[top + PANEL :, :] = m_ref[top + PANEL :, :] - update[top + PANEL :, :]


def orthonormal(own, got, filtered, s):
    k = s.k
    parts = 8
    rows = s.cells // parts

    def body(own_ref, got_ref, f_ref, b_hbm, o_ref, m_ref, b_ref, sems):
        even = places(s)[7] == 0
        one, other = own_ref[: k // 2, :], got_ref[: k // 2, :]
        upper = jnp.concatenate(
            [jnp.where(even, one, other), jnp.where(even, other, one)], axis=0
        )
        low, high = own_ref[k // 2 : k // 2 + 1, :], got_ref[k // 2 : k // 2 + 1, :]
        turned = upper.T
        below = lax.broadcasted_iota(jnp.int32, (k, k), 0)
        along = lax.broadcasted_iota(jnp.int32, (k, k), 1)
        m_ref[:, :k] = jnp.where(below >= along, upper, turned)
        m_ref[:, k:] = jnp.where(below == along, 1.0, 0.0)
        eliminate(m_ref, k)
        inverse = m_ref[:, k:]
        pair = two(inverse.T)
        pair = jnp.concatenate([pair, pair], axis=0)
        copies = []
        for i in range(parts):
            here = pl.ds(i * rows, rows)
            out = jnp.dot(f_ref[here, :], pair, preferred_element_type=jnp.float32)
            b_ref[here, :] = out[:, :k] + out[:, k:]
            copies.append(pltpu.make_async_copy(b_ref.at[here], b_hbm.at[here], sems.at[i]))
            copies[-1].start()
        raw = jnp.where(below < along, upper, turned)
        raw = jnp.where(below == along, jnp.where(even, low, high), raw)
        half = jnp.dot(inverse, raw, precision=HIGH, preferred_element_type=jnp.float32)
        o_ref[...] = lax.dot_general(
            half, inverse, (((1,), (1,)), ((), ())),
            precision=HIGH, preferred_element_type=jnp.float32,
        )
        for copy in copies:
            copy.wait()

    return pl.pallas_call(
        body,
        out_shape=[f32(s.cells, k), f32(k, k)],
        in_specs=[VMEM, VMEM, VMEM],
        out_specs=(pl.BlockSpec(memory_space=pl.ANY), VMEM),
        scratch_shapes=[
            pltpu.VMEM((k, 2 * k), jnp.float32),
            pltpu.VMEM((s.cells, k), jnp.float32),
            pltpu.SemaphoreType.DMA((parts,)),
        ],
        compiler_params=pltpu.CompilerParams(vmem_limit_bytes=32 * 1024 * 1024),
        cost_estimate=pl.CostEstimate(
            flops=8 * s.cells * k * k, bytes_accessed=8 * s.cells * k, transcendentals=0
        ),
    )(own, got, filtered)


def on_device(block, conductivity):
    s = Shape(block.shape)
    sizes = [lax.axis_size(a) for a in ("gx", "gy", "gz")]
    nz = 1 if sizes[2] == 2 else 2
    cells = float(s.cells * sizes[0] * sizes[1] * sizes[2])
    axes = [("gx", 0), ("gx", 1), ("gy", 0), ("gy", 1), ("gz", 0), ("gz", 1)][: 4 + nz]

    flat = block.reshape(s.cells, s.k)
    turned = jnp.transpose(conductivity, (1, 2, 0))
    w, wide, *rest = prepare(flat, turned, s, nz)
    faces, edge = rest[: 4 + nz], rest[4 + nz :]
    before = None
    for step in range(DEG):
        ghosts = exchange(faces, axes)
        part = interior(w, before, wide, s)
        scale = (1.0 if before is None else 2.0) / half_value
        before = w
        w, *faces = finish(part, wide, edge, ghosts, s, nz, scale, step == DEG - 1)
    ghosts = exchange(faces, axes)
    filtered, gram, own = gather_terms(w, wide, s)
    halves = total(*pack_terms(gram, own, w, ghosts, s, nz, cells))
    basis, projected = orthonormal(*halves, filtered, s)
    return (basis.reshape(block.shape), projected)


def solution(mesh):
    return jax.shard_map(
        on_device,
        mesh=mesh,
        in_specs=(P("gx", "gy", "gz", None), P("gx", "gy", "gz")),
        out_specs=(P("gx", "gy", "gz", None), P()),
        check_vma=False,
    )
```

```python
import functools
import jax
import jax.numpy as jnp
from jax import lax
from jax.experimental import pallas as pl
from jax.experimental.pallas import tpu as pltpu
from jax.sharding import PartitionSpec as P

DEG = 4

HIGH = lax.Precision.HIGHEST
center_value = 3.25
half_value = 2.75
VMEM = pl.BlockSpec(memory_space=pltpu.VMEM)
BF = jnp.bfloat16


def call(body, outs, ins, flops, aliases=None):
    moved = sum(4 * a.size for a in list(outs) + list(ins))
    return pl.pallas_call(
        body,
        out_shape=outs,
        in_specs=[VMEM] * len(ins),
        out_specs=tuple(VMEM for _ in outs),
        input_output_aliases=aliases or {},
        compiler_params=pltpu.CompilerParams(vmem_limit_bytes=32 * 1024 * 1024),
        cost_estimate=pl.CostEstimate(flops=flops, bytes_accessed=moved, transcendentals=0),
    )(*ins)


def f32(rows, width):
    return jax.ShapeDtypeStruct((rows, width), jnp.float32)


class Shape:
    def __init__(self, shape):
        self.x, self.y, self.z, self.k = shape
        self.row = self.y * self.z
        self.cells = self.x * self.row
        self.room = self.cells + self.z


def places(s):
    odd = [lax.rem(lax.axis_index(a), 2) for a in ("gx", "gy", "gz")]
    tops = (s.x - 1, s.y - 1, s.z - 1)
    at = [jnp.where(odd[d] == first, tops[d], 0) for d in range(3) for first in range(2)]
    return at + [odd[2], odd[1]]


def faces_of(s, at, w_ref, out, with_z=True):
    if with_z:
        for i in range(out["nz"]):
            out["z"][i][...] = w_ref[pl.ds(at[4 + i], s.x * s.y, stride=s.z), :]
    for i in range(2):
        out["x"][i][...] = w_ref[pl.ds(at[i] * s.row, s.row), :]
        for x in range(s.x):
            out["y"][i][pl.ds(x * s.z, s.z), :] = w_ref[
                pl.ds(x * s.row + at[2 + i] * s.z, s.z), :
            ]


def face_shapes(s, nz):
    return (
        [f32(s.row, s.k)] * 2 + [f32(s.x * s.z, s.k)] * 2 + [f32(s.x * s.y, s.k)] * nz
    )


def split_faces(refs, nz):
    return {"x": refs[0:2], "y": refs[2:4], "z": refs[4 : 4 + nz], "nz": nz}


def prepare(block, turned, s, nz):
    parts = 4
    each = s.x // parts

    def body(k_ref, *all_refs):
        b_refs, (w_ref, wide_ref, *refs) = all_refs[:parts], all_refs[parts:]
        at_ref = places(s)
        for y in range(s.y):
            tile = k_ref[y]
            for x in range(s.x):
                here = pl.ds(x * s.row + y * s.z, s.z)
                k = jnp.broadcast_to(tile[:, x : x + 1], (s.z, s.k))
                wide_ref[here, :] = k
                b = b_refs[x // each][(x % each) * s.row + y * s.z : (x % each) * s.row + (y + 1) * s.z, :]
                w_ref[here, :] = jnp.sqrt(k) * b
        for i in range(nz):
            refs[4 + nz + i][...] = wide_ref[pl.ds(at_ref[4 + i], s.x * s.y, stride=s.z), :]
        faces_of(s, at_ref, w_ref, split_faces(refs, nz))

    outs = [f32(s.room, s.k)] * 2 + face_shapes(s, nz) + [f32(s.x * s.y, s.k)] * nz
    slices = [block[i * each * s.row : (i + 1) * each * s.row] for i in range(parts)]
    return call(body, outs, [turned] + slices, 4 * s.cells * s.k)


def around(s, w_ref, o_ref, x, low, high, emit):
    base = pl.multiple_of(x * s.row, s.row)
    place = lax.broadcasted_iota(jnp.int32, (s.z, s.k), 0)
    tiles = [w_ref[pl.ds(base + y * s.z, s.z), :] for y in range(s.y)]
    done = []
    for y in range(s.y):
        c = tiles[y]
        up = jnp.where(place == s.z - 1, 0.0, pltpu.roll(c, s.z - 1, 0))
        down = jnp.where(place == 0, 0.0, pltpu.roll(c, 1, 0))
        near = up + down
        if y > 0:
            near = near + tiles[y - 1]
        if y < s.y - 1:
            near = near + tiles[y + 1]
        if low:
            near = near + w_ref[pl.ds(base - s.row + y * s.z, s.z), :]
        if high:
            near = near + w_ref[pl.ds(base + s.row + y * s.z, s.z), :]
        here = pl.ds(base + y * s.z, s.z)
        done.append((here, emit(here, c, near)))
    for here, new in done:
        o_ref[here, :] = new


def sweep(s, w_ref, o_ref, emit):
    around(s, w_ref, o_ref, 0, False, True, emit)

    def step(x, _):
        around(s, w_ref, o_ref, x, True, True, emit)
        return 0

    lax.fori_loop(1, s.x - 1, step, 0, unroll=2)
    around(s, w_ref, o_ref, s.x - 1, True, False, emit)


def interior(w, before, wide, s):
    scale = (1.0 if before is None else 2.0) / half_value

    def body(w_ref, k_ref, *rest):
        o_ref = rest[-1]

        def emit(here, c, near):
            new = k_ref[here, :] * ((c - near * (1.0 / 6.0)) * scale) - (scale * center_value) * c
            if before is not None:
                new = new - rest[0][here, :]
            return new

        sweep(s, w_ref, o_ref, emit)

    ins = [w, wide] + ([] if before is None else [before])
    return call(body, [f32(s.room, s.k)], ins, 12 * s.cells * s.k)[0]


def finish(part, wide, edge, ghosts, s, nz, scale, last):
    def body(p_ref, k_ref, *refs):
        del p_ref
        at_ref = places(s)
        edges = refs[:nz]
        ghost = split_faces(refs[nz : 4 + 2 * nz], nz)
        w_ref = refs[4 + 2 * nz]
        out = split_faces(refs[5 + 2 * nz :], nz)
        half = last and halved(s, nz)
        factor = scale / 6.0
        for i in range(2):
            here = pl.ds(at_ref[i] * s.row, s.row)
            w_ref[here, :] = w_ref[here, :] - (k_ref[here, :] * factor) * ghost["x"][i][...]
            done = []
            for x in range(s.x):
                here = pl.ds(x * s.row + at_ref[2 + i] * s.z, s.z)
                g = ghost["y"][i][pl.ds(x * s.z, s.z), :]
                done.append((here, w_ref[here, :] - (k_ref[here, :] * factor) * g))
            for here, new in done:
                w_ref[here, :] = new
        for i in range(nz):
            for first in range(0, s.x, 8):
                done = []
                for x in range(first, min(first + 8, s.x)):
                    here = pl.ds(x * s.row + at_ref[4 + i], s.y, stride=s.z)
                    flat = pl.ds(x * s.y, s.y)
                    new = w_ref[here, :] - (edges[i][flat, :] * factor) * ghost["z"][i][flat, :]
                    done.append((here, flat, new))
                for here, flat, new in done:
                    w_ref[here, :] = new
                    if not half:
                        out["z"][i][flat, :] = new
        faces_of(s, at_ref, w_ref, out, with_z=False)
        if half:
            start = (1 - at_ref[6]) * (s.cells // 2) + at_ref[4]
            out["z"][0][...] = w_ref[pl.ds(start, s.x * s.y // 2, stride=s.z), :]

    outs = [f32(s.room, s.k)] + face_shapes(s, nz)
    if last and halved(s, nz):
        outs[5] = f32(s.x * s.y // 2, s.k)
    ins = [part, wide] + list(edge) + list(ghosts)
    return call(body, outs, ins, 4 * s.x * s.y * s.k, {0: 0})


def halved(s, nz):
    return nz == 1 and s.x % 2 == 0


def exchange(faces, axes):
    got = []
    for face, (axis, first) in zip(faces, axes):
        count = lax.axis_size(axis)
        pairs = []
        for i in range(first, count - 1, 2):
            pairs += [(i, i + 1), (i + 1, i)]
        got.append(lax.ppermute(face, axis, pairs))
    return got


def transposed_dot(left, right):
    return lax.dot_general(
        left, right, (((0,), (0,)), ((), ())), preferred_element_type=jnp.float32
    )


def two(value):
    high = value.astype(BF)
    low = (value - high.astype(jnp.float32)).astype(BF)
    return jnp.concatenate([high, low], axis=1)


def both(full):
    k = full.shape[0] // 2
    return full[:k, :k] + (full[:k, k:] + full[k:, :k]) + full[k:, k:]


def gather_terms(w, wide, s):
    rows = s.cells // 4

    def body(w_ref, k_ref, f_ref, g_ref, m_ref, q_ref):
        def emit(here, c, near):
            return c - near * (1.0 / 6.0)

        sweep(s, w_ref, q_ref, emit)
        sums = jnp.zeros((2 * s.k, 4 * s.k), jnp.float32)
        for i in range(s.cells // rows):
            here = pl.ds(i * rows, rows)
            k = k_ref[here, :]
            inverse = lax.rsqrt(k)
            pair = two(w_ref[here, :] * inverse)
            f_ref[here, :] = pair
            image = two((k * inverse) * q_ref[here, :])
            sums += transposed_dot(pair, jnp.concatenate([pair, image], axis=1))
        g_ref[...] = both(sums[:, : 2 * s.k])
        m_ref[...] = both(sums[:, 2 * s.k :])

    outs = [jax.ShapeDtypeStruct((s.cells, 2 * s.k), BF), f32(s.k, s.k), f32(s.k, s.k)]
    moved = 4 * 4 * s.cells * s.k
    return pl.pallas_call(
        body,
        out_shape=outs,
        in_specs=[VMEM, VMEM],
        out_specs=(VMEM, VMEM, VMEM),
        scratch_shapes=[pltpu.VMEM((s.cells, s.k), jnp.float32)],
        compiler_params=pltpu.CompilerParams(vmem_limit_bytes=32 * 1024 * 1024),
        cost_estimate=pl.CostEstimate(
            flops=16 * s.cells * s.k * s.k, bytes_accessed=moved, transcendentals=0
        ),
    )(w, wide)


def pack_terms(gram, own, w, ghosts, s, nz, cells):
    k = s.k

    def body(g_ref, m_ref, w_ref, *refs):
        at_ref = places(s)
        ghost = split_faces(refs[: 4 + nz], nz)
        p_ref = refs[4 + nz]
        lefts = [w_ref[pl.ds(at_ref[i] * s.row, s.row), :] for i in range(2)]
        for i in range(2):
            lefts += [
                w_ref[pl.ds(x * s.row + at_ref[2 + i] * s.z, s.z), :] for x in range(s.x)
            ]
        rights = [g[...] for g in list(ghost["x"]) + list(ghost["y"])]
        if halved(s, nz):
            start = at_ref[6] * (s.cells // 2) + at_ref[4]
            lefts.append(w_ref[pl.ds(start, s.x * s.y // 2, stride=s.z), :])
            rights.append(2.0 * ghost["z"][0][...])
        else:
            for i in range(nz):
                lefts.append(w_ref[pl.ds(at_ref[4 + i], s.x * s.y, stride=s.z), :])
                rights.append(ghost["z"][i][...])
        left = jnp.concatenate(lefts, axis=0)
        right = jnp.concatenate(rights, axis=0)
        m = m_ref[...] - both(transposed_dot(two(left), two(right))) * (1.0 / 6.0)
        raw = (m + m.T) * (0.5 / cells)
        below = lax.broadcasted_iota(jnp.int32, (k, k), 0)
        along = lax.broadcasted_iota(jnp.int32, (k, k), 1)
        full = jnp.where(below >= along, g_ref[...] * (1.0 / cells), raw)
        diagonal = jnp.sum(jnp.where(below == along, raw, 0.0), axis=0, keepdims=True)
        p_ref[:k, :] = full
        p_ref[k:, :] = jnp.broadcast_to(diagonal, (8, k))

    ins = [gram, own, w] + list(ghosts)
    return call(body, [f32(k + 8, k)], ins, 6 * s.cells * k)[0]


def total(mine):
    axes = ("gx", "gy", "gz")
    sizes = [lax.axis_size(a) for a in axes]

    def swap(value, flip):
        pairs = []
        for i in range(sizes[0] * sizes[1] * sizes[2]):
            x, y, z = i // (sizes[1] * sizes[2]), i // sizes[2] % sizes[1], i % sizes[2]
            x, y, z = x ^ flip[0], y ^ flip[1], z ^ flip[2]
            pairs.append((i, (x * sizes[1] + y) * sizes[2] + z))
        return lax.ppermute(value, axes, pairs)

    hops = []
    for d, first in ((1, 2), (2, 1), (0, 1)):
        bit = first
        while bit < sizes[d]:
            hops.append(tuple(bit if e == d else 0 for e in range(3)))
            bit *= 2
    pair = (0, 1, 0)
    value = mine + swap(mine, pair)
    while hops:
        a, *hops = hops
        if hops:
            b, *hops = hops
            c = tuple(i ^ j for i, j in zip(a, b))
            value = (value + swap(value, a)) + (swap(value, b) + swap(value, c))
        else:
            value = value + swap(value, a)
    return value


PANEL = 64
GROUP = 16


def eliminate(m_ref, n):
    place = lax.broadcasted_iota(jnp.int32, (PANEL, n), 0)
    for top in range(0, n, PANEL):
        left, right = m_ref[top : top + PANEL, :n], m_ref[top : top + PANEL, n:]
        for first in range(0, PANEL, GROUP):
            columns = [
                jnp.broadcast_to(left[:, top + k : top + k + 1], (PANEL, n))
                for k in range(first, first + GROUP)
            ]
            for i in range(GROUP):
                k = first + i
                pivot = columns[i][k : k + 1, :]
                inverse = 1.0 / pivot
                root = lax.rsqrt(pivot)
                below = jnp.where(place > k, columns[i], 0.0)
                for t in range(i + 1, GROUP):
                    columns[t] = columns[t] - below * (columns[t][k : k + 1, :] * inverse)
                here = place == k
                one, two_ = left[k : k + 1, :], right[k : k + 1, :]
                left = jnp.where(here, one * root, left - below * (one * inverse))
                right = jnp.where(here, two_ * root, right - below * (two_ * inverse))
        m_ref[top : top + PANEL, :n] = left
        m_ref[top : top + PANEL, n:] = right
        if top + PANEL < n:
            both_sides = jnp.concatenate([left, right], axis=1)
            update = lax.dot_general(
                left, both_sides, (((0,), (0,)), ((), ())),
                precision=HIGH, preferred_element_type=jnp.float32,
            )
            m_ref[top + PANEL :, :] = m_ref[top + PANEL :, :] - update[top + PANEL :, :]


def orthonormal(packed, filtered, s):
    k = s.k
    parts = 8
    rows = s.cells // parts

    def body(p_ref, f_ref, b_hbm, o_ref, m_ref, b_ref, sems):
        upper = p_ref[:k, :]
        turned = upper.T
        below = lax.broadcasted_iota(jnp.int32, (k, k), 0)
        along = lax.broadcasted_iota(jnp.int32, (k, k), 1)
        m_ref[:, :k] = jnp.where(below >= along, upper, turned)
        m_ref[:, k:] = jnp.where(below == along, 1.0, 0.0)
        eliminate(m_ref, k)
        inverse = m_ref[:, k:]
        pair = two(inverse.T)
        pair = jnp.concatenate([pair, pair], axis=0)
        copies = []
        for i in range(parts):
            here = pl.ds(i * rows, rows)
            out = jnp.dot(f_ref[here, :], pair, preferred_element_type=jnp.float32)
            b_ref[here, :] = out[:, :k] + out[:, k:]
            copies.append(pltpu.make_async_copy(b_ref.at[here], b_hbm.at[here], sems.at[i]))
            copies[-1].start()
        raw = jnp.where(below < along, upper, turned)
        raw = jnp.where(below == along, p_ref[k : k + 1, :], raw)
        half = jnp.dot(inverse, raw, precision=HIGH, preferred_element_type=jnp.float32)
        o_ref[...] = lax.dot_general(
            half, inverse, (((1,), (1,)), ((), ())),
            precision=HIGH, preferred_element_type=jnp.float32,
        )
        for copy in copies:
            copy.wait()

    return pl.pallas_call(
        body,
        out_shape=[f32(s.cells, k), f32(k, k)],
        in_specs=[VMEM, VMEM],
        out_specs=(pl.BlockSpec(memory_space=pl.ANY), VMEM),
        scratch_shapes=[
            pltpu.VMEM((k, 2 * k), jnp.float32),
            pltpu.VMEM((s.cells, k), jnp.float32),
            pltpu.SemaphoreType.DMA((parts,)),
        ],
        compiler_params=pltpu.CompilerParams(vmem_limit_bytes=32 * 1024 * 1024),
        cost_estimate=pl.CostEstimate(
            flops=8 * s.cells * k * k, bytes_accessed=8 * s.cells * k, transcendentals=0
        ),
    )(packed, filtered)


def on_device(block, conductivity):
    s = Shape(block.shape)
    sizes = [lax.axis_size(a) for a in ("gx", "gy", "gz")]
    nz = 1 if sizes[2] == 2 else 2
    cells = float(s.cells * sizes[0] * sizes[1] * sizes[2])
    axes = [("gx", 0), ("gx", 1), ("gy", 0), ("gy", 1), ("gz", 0), ("gz", 1)][: 4 + nz]

    flat = block.reshape(s.cells, s.k)
    turned = jnp.transpose(conductivity, (1, 2, 0))
    w, wide, *rest = prepare(flat, turned, s, nz)
    faces, edge = rest[: 4 + nz], rest[4 + nz :]
    before = None
    for step in range(DEG):
        ghosts = exchange(faces, axes)
        part = interior(w, before, wide, s)
        scale = (1.0 if before is None else 2.0) / half_value
        before = w
        w, *faces = finish(part, wide, edge, ghosts, s, nz, scale, step == DEG - 1)
    ghosts = exchange(faces, axes)
    filtered, gram, own = gather_terms(w, wide, s)
    packed = total(pack_terms(gram, own, w, ghosts, s, nz, cells))
    basis, projected = orthonormal(packed, filtered, s)
    return (basis.reshape(block.shape), projected)


def solution(mesh):
    return jax.shard_map(
        on_device,
        mesh=mesh,
        in_specs=(P("gx", "gy", "gz", None), P("gx", "gy", "gz")),
        out_specs=(P("gx", "gy", "gz", None), P()),
        check_vma=False,
    )
```

```python
import functools
import jax
import jax.numpy as jnp
from jax import lax
from jax.experimental import pallas as pl
from jax.experimental.pallas import tpu as pltpu
from jax.sharding import PartitionSpec as P

DEG = 4

HIGH = lax.Precision.HIGHEST
center_value = 3.25
half_value = 2.75
VMEM = pl.BlockSpec(memory_space=pltpu.VMEM)
BF = jnp.bfloat16


def call(body, outs, ins, flops, aliases=None):
    moved = sum(4 * a.size for a in list(outs) + list(ins))
    return pl.pallas_call(
        body,
        out_shape=outs,
        in_specs=[VMEM] * len(ins),
        out_specs=tuple(VMEM for _ in outs),
        input_output_aliases=aliases or {},
        compiler_params=pltpu.CompilerParams(vmem_limit_bytes=32 * 1024 * 1024),
        cost_estimate=pl.CostEstimate(flops=flops, bytes_accessed=moved, transcendentals=0),
    )(*ins)


def f32(rows, width):
    return jax.ShapeDtypeStruct((rows, width), jnp.float32)


class Shape:
    def __init__(self, shape):
        self.x, self.y, self.z, self.k = shape
        self.row = self.y * self.z
        self.cells = self.x * self.row
        self.room = self.cells + self.z


def places(s):
    odd = [lax.rem(lax.axis_index(a), 2) for a in ("gx", "gy", "gz")]
    tops = (s.x - 1, s.y - 1, s.z - 1)
    at = [jnp.where(odd[d] == first, tops[d], 0) for d in range(3) for first in range(2)]
    return at + [odd[2], odd[1]]


def faces_of(s, at, w_ref, out, with_z=True):
    if with_z:
        for i in range(out["nz"]):
            out["z"][i][...] = w_ref[pl.ds(at[4 + i], s.x * s.y, stride=s.z), :]
    for i in range(2):
        out["x"][i][...] = w_ref[pl.ds(at[i] * s.row, s.row), :]
        for x in range(s.x):
            out["y"][i][pl.ds(x * s.z, s.z), :] = w_ref[
                pl.ds(x * s.row + at[2 + i] * s.z, s.z), :
            ]


def face_shapes(s, nz):
    return (
        [f32(s.row, s.k)] * 2 + [f32(s.x * s.z, s.k)] * 2 + [f32(s.x * s.y, s.k)] * nz
    )


def split_faces(refs, nz):
    return {"x": refs[0:2], "y": refs[2:4], "z": refs[4 : 4 + nz], "nz": nz}


def prepare(block, turned, s, nz):
    parts = 4
    each = s.x // parts

    def body(k_ref, *all_refs):
        b_refs, (w_ref, wide_ref, *refs) = all_refs[:parts], all_refs[parts:]
        at_ref = places(s)
        for y in range(s.y):
            tile = k_ref[y]
            for x in range(s.x):
                here = pl.ds(x * s.row + y * s.z, s.z)
                k = jnp.broadcast_to(tile[:, x : x + 1], (s.z, s.k))
                wide_ref[here, :] = k
                b = b_refs[x // each][(x % each) * s.row + y * s.z : (x % each) * s.row + (y + 1) * s.z, :]
                w_ref[here, :] = jnp.sqrt(k) * b
        for i in range(nz):
            refs[4 + nz + i][...] = wide_ref[pl.ds(at_ref[4 + i], s.x * s.y, stride=s.z), :]
        faces_of(s, at_ref, w_ref, split_faces(refs, nz))

    outs = [f32(s.room, s.k)] * 2 + face_shapes(s, nz) + [f32(s.x * s.y, s.k)] * nz
    slices = [block[i * each * s.row : (i + 1) * each * s.row] for i in range(parts)]
    return call(body, outs, [turned] + slices, 4 * s.cells * s.k)


def around(s, w_ref, o_ref, x, low, high, emit):
    base = pl.multiple_of(x * s.row, s.row)
    place = lax.broadcasted_iota(jnp.int32, (s.z, s.k), 0)
    tiles = [w_ref[pl.ds(base + y * s.z, s.z), :] for y in range(s.y)]
    done = []
    for y in range(s.y):
        c = tiles[y]
        up = jnp.where(place == s.z - 1, 0.0, pltpu.roll(c, s.z - 1, 0))
        down = jnp.where(place == 0, 0.0, pltpu.roll(c, 1, 0))
        near = up + down
        if y > 0:
            near = near + tiles[y - 1]
        if y < s.y - 1:
            near = near + tiles[y + 1]
        if low:
            near = near + w_ref[pl.ds(base - s.row + y * s.z, s.z), :]
        if high:
            near = near + w_ref[pl.ds(base + s.row + y * s.z, s.z), :]
        here = pl.ds(base + y * s.z, s.z)
        done.append((here, emit(here, c, near)))
    for here, new in done:
        o_ref[here, :] = new


def sweep(s, w_ref, o_ref, emit):
    around(s, w_ref, o_ref, 0, False, True, emit)

    def step(x, _):
        around(s, w_ref, o_ref, x, True, True, emit)
        return 0

    lax.fori_loop(1, s.x - 1, step, 0, unroll=5)
    around(s, w_ref, o_ref, s.x - 1, True, False, emit)


def interior(w, before, wide, s):
    scale = (1.0 if before is None else 2.0) / half_value

    def body(w_ref, k_ref, *rest):
        o_ref = rest[-1]

        def emit(here, c, near):
            new = k_ref[here, :] * ((c - near * (1.0 / 6.0)) * scale) - (scale * center_value) * c
            if before is not None:
                new = new - rest[0][here, :]
            return new

        sweep(s, w_ref, o_ref, emit)

    ins = [w, wide] + ([] if before is None else [before])
    return call(body, [f32(s.room, s.k)], ins, 12 * s.cells * s.k)[0]


def finish(part, wide, edge, ghosts, s, nz, scale, last):
    def body(p_ref, k_ref, *refs):
        del p_ref
        at_ref = places(s)
        edges = refs[:nz]
        ghost = split_faces(refs[nz : 4 + 2 * nz], nz)
        w_ref = refs[4 + 2 * nz]
        out = split_faces(refs[5 + 2 * nz :], nz)
        half = last and halved(s, nz)
        factor = scale / 6.0
        for i in range(2):
            here = pl.ds(at_ref[i] * s.row, s.row)
            w_ref[here, :] = w_ref[here, :] - (k_ref[here, :] * factor) * ghost["x"][i][...]
            done = []
            for x in range(s.x):
                here = pl.ds(x * s.row + at_ref[2 + i] * s.z, s.z)
                g = ghost["y"][i][pl.ds(x * s.z, s.z), :]
                done.append((here, w_ref[here, :] - (k_ref[here, :] * factor) * g))
            for here, new in done:
                w_ref[here, :] = new
        for i in range(nz):
            for first in range(0, s.x, 8):
                done = []
                for x in range(first, min(first + 8, s.x)):
                    here = pl.ds(x * s.row + at_ref[4 + i], s.y, stride=s.z)
                    flat = pl.ds(x * s.y, s.y)
                    new = w_ref[here, :] - (edges[i][flat, :] * factor) * ghost["z"][i][flat, :]
                    done.append((here, flat, new))
                for here, flat, new in done:
                    w_ref[here, :] = new
                    if not half:
                        out["z"][i][flat, :] = new
        faces_of(s, at_ref, w_ref, out, with_z=False)
        if half:
            start = (1 - at_ref[6]) * (s.cells // 2) + at_ref[4]
            out["z"][0][...] = w_ref[pl.ds(start, s.x * s.y // 2, stride=s.z), :]

    outs = [f32(s.room, s.k)] + face_shapes(s, nz)
    if last and halved(s, nz):
        outs[5] = f32(s.x * s.y // 2, s.k)
    ins = [part, wide] + list(edge) + list(ghosts)
    return call(body, outs, ins, 4 * s.x * s.y * s.k, {0: 0})


def halved(s, nz):
    return nz == 1 and s.x % 2 == 0


def exchange(faces, axes):
    got = []
    for face, (axis, first) in zip(faces, axes):
        count = lax.axis_size(axis)
        pairs = []
        for i in range(first, count - 1, 2):
            pairs += [(i, i + 1), (i + 1, i)]
        got.append(lax.ppermute(face, axis, pairs))
    return got


def transposed_dot(left, right):
    return lax.dot_general(
        left, right, (((0,), (0,)), ((), ())), preferred_element_type=jnp.float32
    )


def two(value):
    high = value.astype(BF)
    low = (value - high.astype(jnp.float32)).astype(BF)
    return jnp.concatenate([high, low], axis=1)


def both(full):
    k = full.shape[0] // 2
    return full[:k, :k] + (full[:k, k:] + full[k:, :k]) + full[k:, k:]


def gather_terms(w, wide, s):
    rows = s.cells // 4

    def body(w_ref, k_ref, f_ref, g_ref, m_ref, q_ref):
        def emit(here, c, near):
            return c - near * (1.0 / 6.0)

        sweep(s, w_ref, q_ref, emit)
        sums = jnp.zeros((2 * s.k, 4 * s.k), jnp.float32)
        for i in range(s.cells // rows):
            here = pl.ds(i * rows, rows)
            k = k_ref[here, :]
            inverse = lax.rsqrt(k)
            pair = two(w_ref[here, :] * inverse)
            f_ref[here, :] = pair
            image = two((k * inverse) * q_ref[here, :])
            sums += transposed_dot(pair, jnp.concatenate([pair, image], axis=1))
        g_ref[...] = both(sums[:, : 2 * s.k])
        m_ref[...] = both(sums[:, 2 * s.k :])

    outs = [jax.ShapeDtypeStruct((s.cells, 2 * s.k), BF), f32(s.k, s.k), f32(s.k, s.k)]
    moved = 4 * 4 * s.cells * s.k
    return pl.pallas_call(
        body,
        out_shape=outs,
        in_specs=[VMEM, VMEM],
        out_specs=(VMEM, VMEM, VMEM),
        scratch_shapes=[pltpu.VMEM((s.cells, s.k), jnp.float32)],
        compiler_params=pltpu.CompilerParams(vmem_limit_bytes=32 * 1024 * 1024),
        cost_estimate=pl.CostEstimate(
            flops=16 * s.cells * s.k * s.k, bytes_accessed=moved, transcendentals=0
        ),
    )(w, wide)


def pack_terms(gram, own, w, ghosts, s, nz, cells):
    k = s.k

    def body(g_ref, m_ref, w_ref, *refs):
        at_ref = places(s)
        ghost = split_faces(refs[: 4 + nz], nz)
        p_ref = refs[4 + nz]
        lefts = [w_ref[pl.ds(at_ref[i] * s.row, s.row), :] for i in range(2)]
        for i in range(2):
            lefts += [
                w_ref[pl.ds(x * s.row + at_ref[2 + i] * s.z, s.z), :] for x in range(s.x)
            ]
        rights = [g[...] for g in list(ghost["x"]) + list(ghost["y"])]
        if halved(s, nz):
            start = at_ref[6] * (s.cells // 2) + at_ref[4]
            lefts.append(w_ref[pl.ds(start, s.x * s.y // 2, stride=s.z), :])
            rights.append(2.0 * ghost["z"][0][...])
        else:
            for i in range(nz):
                lefts.append(w_ref[pl.ds(at_ref[4 + i], s.x * s.y, stride=s.z), :])
                rights.append(ghost["z"][i][...])
        left = jnp.concatenate(lefts, axis=0)
        right = jnp.concatenate(rights, axis=0)
        m = m_ref[...] - both(transposed_dot(two(left), two(right))) * (1.0 / 6.0)
        raw = (m + m.T) * (0.5 / cells)
        below = lax.broadcasted_iota(jnp.int32, (k, k), 0)
        along = lax.broadcasted_iota(jnp.int32, (k, k), 1)
        full = jnp.where(below >= along, g_ref[...] * (1.0 / cells), raw)
        diagonal = jnp.sum(jnp.where(below == along, raw, 0.0), axis=0, keepdims=True)
        p_ref[:k, :] = full
        p_ref[k:, :] = jnp.broadcast_to(diagonal, (8, k))

    ins = [gram, own, w] + list(ghosts)
    return call(body, [f32(k + 8, k)], ins, 6 * s.cells * k)[0]


def total(mine):
    axes = ("gx", "gy", "gz")
    sizes = [lax.axis_size(a) for a in axes]

    def swap(value, flip):
        pairs = []
        for i in range(sizes[0] * sizes[1] * sizes[2]):
            x, y, z = i // (sizes[1] * sizes[2]), i // sizes[2] % sizes[1], i % sizes[2]
            x, y, z = x ^ flip[0], y ^ flip[1], z ^ flip[2]
            pairs.append((i, (x * sizes[1] + y) * sizes[2] + z))
        return lax.ppermute(value, axes, pairs)

    hops = []
    for d, first in ((1, 2), (2, 1), (0, 1)):
        bit = first
        while bit < sizes[d]:
            hops.append(tuple(bit if e == d else 0 for e in range(3)))
            bit *= 2
    pair = (0, 1, 0)
    value = mine + swap(mine, pair)
    while hops:
        a, *hops = hops
        if hops:
            b, *hops = hops
            c = tuple(i ^ j for i, j in zip(a, b))
            value = (value + swap(value, a)) + (swap(value, b) + swap(value, c))
        else:
            value = value + swap(value, a)
    return value


PANEL = 64
GROUP = 16


def eliminate(m_ref, n):
    place = lax.broadcasted_iota(jnp.int32, (PANEL, n), 0)
    for top in range(0, n, PANEL):
        left, right = m_ref[top : top + PANEL, :n], m_ref[top : top + PANEL, n:]
        for first in range(0, PANEL, GROUP):
            columns = [
                jnp.broadcast_to(left[:, top + k : top + k + 1], (PANEL, n))
                for k in range(first, first + GROUP)
            ]
            for i in range(GROUP):
                k = first + i
                pivot = columns[i][k : k + 1, :]
                inverse = 1.0 / pivot
                root = lax.rsqrt(pivot)
                below = jnp.where(place > k, columns[i], 0.0)
                for t in range(i + 1, GROUP):
                    columns[t] = columns[t] - below * (columns[t][k : k + 1, :] * inverse)
                here = place == k
                one, two_ = left[k : k + 1, :], right[k : k + 1, :]
                left = jnp.where(here, one * root, left - below * (one * inverse))
                right = jnp.where(here, two_ * root, right - below * (two_ * inverse))
        m_ref[top : top + PANEL, :n] = left
        m_ref[top : top + PANEL, n:] = right
        if top + PANEL < n:
            both_sides = jnp.concatenate([left, right], axis=1)
            update = lax.dot_general(
                left, both_sides, (((0,), (0,)), ((), ())),
                precision=HIGH, preferred_element_type=jnp.float32,
            )
            m_ref[top + PANEL :, :] = m_ref[top + PANEL :, :] - update[top + PANEL :, :]


def orthonormal(packed, filtered, s):
    k = s.k
    parts = 8
    rows = s.cells // parts

    def body(p_ref, f_ref, b_hbm, o_ref, m_ref, b_ref, sems):
        upper = p_ref[:k, :]
        turned = upper.T
        below = lax.broadcasted_iota(jnp.int32, (k, k), 0)
        along = lax.broadcasted_iota(jnp.int32, (k, k), 1)
        m_ref[:, :k] = jnp.where(below >= along, upper, turned)
        m_ref[:, k:] = jnp.where(below == along, 1.0, 0.0)
        eliminate(m_ref, k)
        inverse = m_ref[:, k:]
        pair = two(inverse.T)
        pair = jnp.concatenate([pair, pair], axis=0)
        copies = []
        for i in range(parts):
            here = pl.ds(i * rows, rows)
            out = jnp.dot(f_ref[here, :], pair, preferred_element_type=jnp.float32)
            b_ref[here, :] = out[:, :k] + out[:, k:]
            copies.append(pltpu.make_async_copy(b_ref.at[here], b_hbm.at[here], sems.at[i]))
            copies[-1].start()
        raw = jnp.where(below < along, upper, turned)
        raw = jnp.where(below == along, p_ref[k : k + 1, :], raw)
        half = jnp.dot(inverse, raw, precision=HIGH, preferred_element_type=jnp.float32)
        o_ref[...] = lax.dot_general(
            half, inverse, (((1,), (1,)), ((), ())),
            precision=HIGH, preferred_element_type=jnp.float32,
        )
        for copy in copies:
            copy.wait()

    return pl.pallas_call(
        body,
        out_shape=[f32(s.cells, k), f32(k, k)],
        in_specs=[VMEM, VMEM],
        out_specs=(pl.BlockSpec(memory_space=pl.ANY), VMEM),
        scratch_shapes=[
            pltpu.VMEM((k, 2 * k), jnp.float32),
            pltpu.VMEM((s.cells, k), jnp.float32),
            pltpu.SemaphoreType.DMA((parts,)),
        ],
        compiler_params=pltpu.CompilerParams(vmem_limit_bytes=32 * 1024 * 1024),
        cost_estimate=pl.CostEstimate(
            flops=8 * s.cells * k * k, bytes_accessed=8 * s.cells * k, transcendentals=0
        ),
    )(packed, filtered)


def on_device(block, conductivity):
    s = Shape(block.shape)
    sizes = [lax.axis_size(a) for a in ("gx", "gy", "gz")]
    nz = 1 if sizes[2] == 2 else 2
    cells = float(s.cells * sizes[0] * sizes[1] * sizes[2])
    axes = [("gx", 0), ("gx", 1), ("gy", 0), ("gy", 1), ("gz", 0), ("gz", 1)][: 4 + nz]

    flat = block.reshape(s.cells, s.k)
    turned = jnp.transpose(conductivity, (1, 2, 0))
    w, wide, *rest = prepare(flat, turned, s, nz)
    faces, edge = rest[: 4 + nz], rest[4 + nz :]
    before = None
    for step in range(DEG):
        ghosts = exchange(faces, axes)
        part = interior(w, before, wide, s)
        scale = (1.0 if before is None else 2.0) / half_value
        before = w
        w, *faces = finish(part, wide, edge, ghosts, s, nz, scale, step == DEG - 1)
    ghosts = exchange(faces, axes)
    filtered, gram, own = gather_terms(w, wide, s)
    packed = total(pack_terms(gram, own, w, ghosts, s, nz, cells))
    basis, projected = orthonormal(packed, filtered, s)
    return (basis.reshape(block.shape), projected)


def solution(mesh):
    return jax.shard_map(
        on_device,
        mesh=mesh,
        in_specs=(P("gx", "gy", "gz", None), P("gx", "gy", "gz")),
        out_specs=(P("gx", "gy", "gz", None), P()),
        check_vma=False,
    )
```

```python
import functools
import jax
import jax.numpy as jnp
from jax import lax
from jax.experimental import pallas as pl
from jax.experimental.pallas import tpu as pltpu
from jax.sharding import PartitionSpec as P

DEG = 4

HIGH = lax.Precision.HIGHEST
center_value = 3.25
half_value = 2.75
VMEM = pl.BlockSpec(memory_space=pltpu.VMEM)
BF = jnp.bfloat16


def call(body, outs, ins, flops, aliases=None):
    moved = sum(4 * a.size for a in list(outs) + list(ins))
    return pl.pallas_call(
        body,
        out_shape=outs,
        in_specs=[VMEM] * len(ins),
        out_specs=tuple(VMEM for _ in outs),
        input_output_aliases=aliases or {},
        compiler_params=pltpu.CompilerParams(vmem_limit_bytes=32 * 1024 * 1024),
        cost_estimate=pl.CostEstimate(flops=flops, bytes_accessed=moved, transcendentals=0),
    )(*ins)


def f32(rows, width):
    return jax.ShapeDtypeStruct((rows, width), jnp.float32)


class Shape:
    def __init__(self, shape):
        self.x, self.y, self.z, self.k = shape
        self.row = self.y * self.z
        self.cells = self.x * self.row
        self.room = self.cells + self.z


def places(s):
    odd = [lax.rem(lax.axis_index(a), 2) for a in ("gx", "gy", "gz")]
    tops = (s.x - 1, s.y - 1, s.z - 1)
    at = [jnp.where(odd[d] == first, tops[d], 0) for d in range(3) for first in range(2)]
    return at + [odd[2], odd[1]]


def faces_of(s, at, w_ref, out, with_z=True):
    if with_z:
        for i in range(out["nz"]):
            out["z"][i][...] = w_ref[pl.ds(at[4 + i], s.x * s.y, stride=s.z), :]
    for i in range(2):
        out["x"][i][...] = w_ref[pl.ds(at[i] * s.row, s.row), :]
        for x in range(s.x):
            out["y"][i][pl.ds(x * s.z, s.z), :] = w_ref[
                pl.ds(x * s.row + at[2 + i] * s.z, s.z), :
            ]


def face_shapes(s, nz):
    return (
        [f32(s.row, s.k)] * 2 + [f32(s.x * s.z, s.k)] * 2 + [f32(s.x * s.y, s.k)] * nz
    )


def split_faces(refs, nz):
    return {"x": refs[0:2], "y": refs[2:4], "z": refs[4 : 4 + nz], "nz": nz}


def prepare(block, turned, s, nz):
    parts = 2
    each = s.x // parts

    def body(k_ref, *all_refs):
        b_refs, (w_ref, wide_ref, *refs) = all_refs[:parts], all_refs[parts:]
        at_ref = places(s)
        for y in range(s.y):
            tile = k_ref[y]
            for x in range(s.x):
                here = pl.ds(x * s.row + y * s.z, s.z)
                k = jnp.broadcast_to(tile[:, x : x + 1], (s.z, s.k))
                wide_ref[here, :] = k
                b = b_refs[x // each][(x % each) * s.row + y * s.z : (x % each) * s.row + (y + 1) * s.z, :]
                w_ref[here, :] = jnp.sqrt(k) * b
        for i in range(nz):
            refs[4 + nz + i][...] = wide_ref[pl.ds(at_ref[4 + i], s.x * s.y, stride=s.z), :]
        faces_of(s, at_ref, w_ref, split_faces(refs, nz))

    outs = [f32(s.room, s.k)] * 2 + face_shapes(s, nz) + [f32(s.x * s.y, s.k)] * nz
    slices = [block[i * each * s.row : (i + 1) * each * s.row] for i in range(parts)]
    return call(body, outs, [turned] + slices, 4 * s.cells * s.k)


def around(s, w_ref, o_ref, x, low, high, emit):
    base = pl.multiple_of(x * s.row, s.row)
    place = lax.broadcasted_iota(jnp.int32, (s.z, s.k), 0)
    tiles = [w_ref[pl.ds(base + y * s.z, s.z), :] for y in range(s.y)]
    done = []
    for y in range(s.y):
        c = tiles[y]
        up = jnp.where(place == s.z - 1, 0.0, pltpu.roll(c, s.z - 1, 0))
        down = jnp.where(place == 0, 0.0, pltpu.roll(c, 1, 0))
        near = up + down
        if y > 0:
            near = near + tiles[y - 1]
        if y < s.y - 1:
            near = near + tiles[y + 1]
        if low:
            near = near + w_ref[pl.ds(base - s.row + y * s.z, s.z), :]
        if high:
            near = near + w_ref[pl.ds(base + s.row + y * s.z, s.z), :]
        here = pl.ds(base + y * s.z, s.z)
        done.append((here, emit(here, c, near)))
    for here, new in done:
        o_ref[here, :] = new


def sweep(s, w_ref, o_ref, emit):
    around(s, w_ref, o_ref, 0, False, True, emit)

    def step(x, _):
        around(s, w_ref, o_ref, x, True, True, emit)
        return 0

    lax.fori_loop(1, s.x - 1, step, 0, unroll=2)
    around(s, w_ref, o_ref, s.x - 1, True, False, emit)


def interior(w, before, wide, s):
    scale = (1.0 if before is None else 2.0) / half_value

    def body(w_ref, k_ref, *rest):
        o_ref = rest[-1]

        def emit(here, c, near):
            new = k_ref[here, :] * ((c - near * (1.0 / 6.0)) * scale) - (scale * center_value) * c
            if before is not None:
                new = new - rest[0][here, :]
            return new

        sweep(s, w_ref, o_ref, emit)

    ins = [w, wide] + ([] if before is None else [before])
    return call(body, [f32(s.room, s.k)], ins, 12 * s.cells * s.k)[0]


def finish(part, wide, edge, ghosts, s, nz, scale, last):
    def body(p_ref, k_ref, *refs):
        del p_ref
        at_ref = places(s)
        edges = refs[:nz]
        ghost = split_faces(refs[nz : 4 + 2 * nz], nz)
        w_ref = refs[4 + 2 * nz]
        out = split_faces(refs[5 + 2 * nz :], nz)
        half = last and halved(s, nz)
        factor = scale / 6.0
        for i in range(2):
            here = pl.ds(at_ref[i] * s.row, s.row)
            w_ref[here, :] = w_ref[here, :] - (k_ref[here, :] * factor) * ghost["x"][i][...]
            done = []
            for x in range(s.x):
                here = pl.ds(x * s.row + at_ref[2 + i] * s.z, s.z)
                g = ghost["y"][i][pl.ds(x * s.z, s.z), :]
                done.append((here, w_ref[here, :] - (k_ref[here, :] * factor) * g))
            for here, new in done:
                w_ref[here, :] = new
        for i in range(nz):
            for first in range(0, s.x, 8):
                done = []
                for x in range(first, min(first + 8, s.x)):
                    here = pl.ds(x * s.row + at_ref[4 + i], s.y, stride=s.z)
                    flat = pl.ds(x * s.y, s.y)
                    new = w_ref[here, :] - (edges[i][flat, :] * factor) * ghost["z"][i][flat, :]
                    done.append((here, flat, new))
                for here, flat, new in done:
                    w_ref[here, :] = new
                    if not half:
                        out["z"][i][flat, :] = new
        faces_of(s, at_ref, w_ref, out, with_z=False)
        if half:
            start = (1 - at_ref[6]) * (s.cells // 2) + at_ref[4]
            out["z"][0][...] = w_ref[pl.ds(start, s.x * s.y // 2, stride=s.z), :]

    outs = [f32(s.room, s.k)] + face_shapes(s, nz)
    if last and halved(s, nz):
        outs[5] = f32(s.x * s.y // 2, s.k)
    ins = [part, wide] + list(edge) + list(ghosts)
    return call(body, outs, ins, 4 * s.x * s.y * s.k, {0: 0})


def halved(s, nz):
    return nz == 1 and s.x % 2 == 0


def exchange(faces, axes):
    got = []
    for face, (axis, first) in zip(faces, axes):
        count = lax.axis_size(axis)
        pairs = []
        for i in range(first, count - 1, 2):
            pairs += [(i, i + 1), (i + 1, i)]
        got.append(lax.ppermute(face, axis, pairs))
    return got


def transposed_dot(left, right):
    return lax.dot_general(
        left, right, (((0,), (0,)), ((), ())), preferred_element_type=jnp.float32
    )


def two(value):
    high = value.astype(BF)
    low = (value - high.astype(jnp.float32)).astype(BF)
    return jnp.concatenate([high, low], axis=1)


def both(full):
    k = full.shape[0] // 2
    return full[:k, :k] + (full[:k, k:] + full[k:, :k]) + full[k:, k:]


def gather_terms(w, wide, s):
    rows = s.cells // 4

    def body(w_ref, k_ref, f_ref, g_ref, m_ref, q_ref):
        def emit(here, c, near):
            return c - near * (1.0 / 6.0)

        sweep(s, w_ref, q_ref, emit)
        sums = jnp.zeros((2 * s.k, 4 * s.k), jnp.float32)
        for i in range(s.cells // rows):
            here = pl.ds(i * rows, rows)
            k = k_ref[here, :]
            inverse = lax.rsqrt(k)
            pair = two(w_ref[here, :] * inverse)
            f_ref[here, :] = pair
            image = two((k * inverse) * q_ref[here, :])
            sums += transposed_dot(pair, jnp.concatenate([pair, image], axis=1))
        g_ref[...] = both(sums[:, : 2 * s.k])
        m_ref[...] = both(sums[:, 2 * s.k :])

    outs = [jax.ShapeDtypeStruct((s.cells, 2 * s.k), BF), f32(s.k, s.k), f32(s.k, s.k)]
    moved = 4 * 4 * s.cells * s.k
    return pl.pallas_call(
        body,
        out_shape=outs,
        in_specs=[VMEM, VMEM],
        out_specs=(VMEM, VMEM, VMEM),
        scratch_shapes=[pltpu.VMEM((s.cells, s.k), jnp.float32)],
        compiler_params=pltpu.CompilerParams(vmem_limit_bytes=32 * 1024 * 1024),
        cost_estimate=pl.CostEstimate(
            flops=16 * s.cells * s.k * s.k, bytes_accessed=moved, transcendentals=0
        ),
    )(w, wide)


def pack_terms(gram, own, w, ghosts, s, nz, cells):
    k = s.k

    def body(g_ref, m_ref, w_ref, *refs):
        at_ref = places(s)
        ghost = split_faces(refs[: 4 + nz], nz)
        p_ref = refs[4 + nz]
        lefts = [w_ref[pl.ds(at_ref[i] * s.row, s.row), :] for i in range(2)]
        for i in range(2):
            lefts += [
                w_ref[pl.ds(x * s.row + at_ref[2 + i] * s.z, s.z), :] for x in range(s.x)
            ]
        rights = [g[...] for g in list(ghost["x"]) + list(ghost["y"])]
        if halved(s, nz):
            start = at_ref[6] * (s.cells // 2) + at_ref[4]
            lefts.append(w_ref[pl.ds(start, s.x * s.y // 2, stride=s.z), :])
            rights.append(2.0 * ghost["z"][0][...])
        else:
            for i in range(nz):
                lefts.append(w_ref[pl.ds(at_ref[4 + i], s.x * s.y, stride=s.z), :])
                rights.append(ghost["z"][i][...])
        left = jnp.concatenate(lefts, axis=0)
        right = jnp.concatenate(rights, axis=0)
        m = m_ref[...] - both(transposed_dot(two(left), two(right))) * (1.0 / 6.0)
        raw = (m + m.T) * (0.5 / cells)
        below = lax.broadcasted_iota(jnp.int32, (k, k), 0)
        along = lax.broadcasted_iota(jnp.int32, (k, k), 1)
        full = jnp.where(below >= along, g_ref[...] * (1.0 / cells), raw)
        diagonal = jnp.sum(jnp.where(below == along, raw, 0.0), axis=0, keepdims=True)
        p_ref[:k, :] = full
        p_ref[k:, :] = jnp.broadcast_to(diagonal, (8, k))

    ins = [gram, own, w] + list(ghosts)
    return call(body, [f32(k + 8, k)], ins, 6 * s.cells * k)[0]


def total(mine):
    axes = ("gx", "gy", "gz")
    sizes = [lax.axis_size(a) for a in axes]

    def swap(value, flip):
        pairs = []
        for i in range(sizes[0] * sizes[1] * sizes[2]):
            x, y, z = i // (sizes[1] * sizes[2]), i // sizes[2] % sizes[1], i % sizes[2]
            x, y, z = x ^ flip[0], y ^ flip[1], z ^ flip[2]
            pairs.append((i, (x * sizes[1] + y) * sizes[2] + z))
        return lax.ppermute(value, axes, pairs)

    hops = []
    for d, first in ((1, 2), (2, 1), (0, 1)):
        bit = first
        while bit < sizes[d]:
            hops.append(tuple(bit if e == d else 0 for e in range(3)))
            bit *= 2
    pair = (0, 1, 0)
    value = mine + swap(mine, pair)
    while hops:
        a, *hops = hops
        if hops:
            b, *hops = hops
            c = tuple(i ^ j for i, j in zip(a, b))
            value = (value + swap(value, a)) + (swap(value, b) + swap(value, c))
        else:
            value = value + swap(value, a)
    return value


PANEL = 64
GROUP = 16


def eliminate(m_ref, n):
    place = lax.broadcasted_iota(jnp.int32, (PANEL, n), 0)
    for top in range(0, n, PANEL):
        left, right = m_ref[top : top + PANEL, :n], m_ref[top : top + PANEL, n:]
        for first in range(0, PANEL, GROUP):
            columns = [
                jnp.broadcast_to(left[:, top + k : top + k + 1], (PANEL, n))
                for k in range(first, first + GROUP)
            ]
            for i in range(GROUP):
                k = first + i
                pivot = columns[i][k : k + 1, :]
                inverse = 1.0 / pivot
                root = lax.rsqrt(pivot)
                below = jnp.where(place > k, columns[i], 0.0)
                for t in range(i + 1, GROUP):
                    columns[t] = columns[t] - below * (columns[t][k : k + 1, :] * inverse)
                here = place == k
                one, two_ = left[k : k + 1, :], right[k : k + 1, :]
                left = jnp.where(here, one * root, left - below * (one * inverse))
                right = jnp.where(here, two_ * root, right - below * (two_ * inverse))
        m_ref[top : top + PANEL, :n] = left
        m_ref[top : top + PANEL, n:] = right
        if top + PANEL < n:
            both_sides = jnp.concatenate([left, right], axis=1)
            update = lax.dot_general(
                left, both_sides, (((0,), (0,)), ((), ())),
                precision=HIGH, preferred_element_type=jnp.float32,
            )
            m_ref[top + PANEL :, :] = m_ref[top + PANEL :, :] - update[top + PANEL :, :]


def orthonormal(packed, filtered, s):
    k = s.k
    parts = 8
    rows = s.cells // parts

    def body(p_ref, f_ref, b_hbm, o_ref, m_ref, b_ref, sems):
        upper = p_ref[:k, :]
        turned = upper.T
        below = lax.broadcasted_iota(jnp.int32, (k, k), 0)
        along = lax.broadcasted_iota(jnp.int32, (k, k), 1)
        m_ref[:, :k] = jnp.where(below >= along, upper, turned)
        m_ref[:, k:] = jnp.where(below == along, 1.0, 0.0)
        eliminate(m_ref, k)
        inverse = m_ref[:, k:]
        pair = two(inverse.T)
        pair = jnp.concatenate([pair, pair], axis=0)
        copies = []
        for i in range(parts):
            here = pl.ds(i * rows, rows)
            out = jnp.dot(f_ref[here, :], pair, preferred_element_type=jnp.float32)
            b_ref[here, :] = out[:, :k] + out[:, k:]
            copies.append(pltpu.make_async_copy(b_ref.at[here], b_hbm.at[here], sems.at[i]))
            copies[-1].start()
        raw = jnp.where(below < along, upper, turned)
        raw = jnp.where(below == along, p_ref[k : k + 1, :], raw)
        half = jnp.dot(inverse, raw, precision=HIGH, preferred_element_type=jnp.float32)
        o_ref[...] = lax.dot_general(
            half, inverse, (((1,), (1,)), ((), ())),
            precision=HIGH, preferred_element_type=jnp.float32,
        )
        for copy in copies:
            copy.wait()

    return pl.pallas_call(
        body,
        out_shape=[f32(s.cells, k), f32(k, k)],
        in_specs=[VMEM, VMEM],
        out_specs=(pl.BlockSpec(memory_space=pl.ANY), VMEM),
        scratch_shapes=[
            pltpu.VMEM((k, 2 * k), jnp.float32),
            pltpu.VMEM((s.cells, k), jnp.float32),
            pltpu.SemaphoreType.DMA((parts,)),
        ],
        compiler_params=pltpu.CompilerParams(vmem_limit_bytes=32 * 1024 * 1024),
        cost_estimate=pl.CostEstimate(
            flops=8 * s.cells * k * k, bytes_accessed=8 * s.cells * k, transcendentals=0
        ),
    )(packed, filtered)


def on_device(block, conductivity):
    s = Shape(block.shape)
    sizes = [lax.axis_size(a) for a in ("gx", "gy", "gz")]
    nz = 1 if sizes[2] == 2 else 2
    cells = float(s.cells * sizes[0] * sizes[1] * sizes[2])
    axes = [("gx", 0), ("gx", 1), ("gy", 0), ("gy", 1), ("gz", 0), ("gz", 1)][: 4 + nz]

    flat = block.reshape(s.cells, s.k)
    turned = jnp.transpose(conductivity, (1, 2, 0))
    w, wide, *rest = prepare(flat, turned, s, nz)
    faces, edge = rest[: 4 + nz], rest[4 + nz :]
    before = None
    for step in range(DEG):
        ghosts = exchange(faces, axes)
        part = interior(w, before, wide, s)
        scale = (1.0 if before is None else 2.0) / half_value
        before = w
        w, *faces = finish(part, wide, edge, ghosts, s, nz, scale, step == DEG - 1)
    ghosts = exchange(faces, axes)
    filtered, gram, own = gather_terms(w, wide, s)
    packed = total(pack_terms(gram, own, w, ghosts, s, nz, cells))
    basis, projected = orthonormal(packed, filtered, s)
    return (basis.reshape(block.shape), projected)


def solution(mesh):
    return jax.shard_map(
        on_device,
        mesh=mesh,
        in_specs=(P("gx", "gy", "gz", None), P("gx", "gy", "gz")),
        out_specs=(P("gx", "gy", "gz", None), P()),
        check_vma=False,
    )
```
